32 devices in a mesh: px: 8 (over z, x), py: 4 (over y, core).
Axes of the slice: x: 2, y: 2, z: 4, core: 2. Of those that a mesh axis runs over, the one named last changes fastest.
Arguments:
- displacement: float32 [3, 32, 64, 128], P(None, 'px', 'py'), may hold values from -6 to 6
- velocity: float32 [3, 32, 64, 128], P(None, 'px', 'py'), may hold values from -6 to 6
- inverse_mass: float32 [32, 64, 128], P('px', 'py'), may hold values from 0.5 to 2
- lame_first: float32 [5, 5, 5, 8, 512], P(None, None, None, 'px', 'py'), may hold values from 0.5 to 2
- lame_second: float32 [5, 5, 5, 8, 512], P(None, None, None, 'px', 'py'), may hold values from 0.5 to 2
- level_map: int32 [8, 512], P('px', 'py'), may hold values from 0 to 2, as said below
Outputs:
- new_displacement: float32 [3, 32, 64, 128], P(None, 'px', 'py')
- new_velocity: float32 [3, 32, 64, 128], P(None, 'px', 'py')
The draws below stay inside these ranges and needn't reach their ends.
Inputs may be any that keep to these rules, and one draw needn't show every extreme that they name: `level_map`: level 2 is the finest. The device whose blocks hold the most finest-level elements holds exactly 96 of them; no device holds more.
All inputs are finite; a program needn't handle non-finite values.
Results may differ from the reference program's by a relative error of at most 0.0003.
Values sent between devices are 32-bit elements; how exact they have to be, the bound alone decides.
No kernel may reach another device: no remote copies, remote signals or barrier semaphores. Data moves between devices by JAX's collectives and lax.ppermute only.
A program may use at most 64 MiB of HBM per device.

```python
import math
import jax
import jax.numpy as jnp
import numpy as np
from jax import lax

EX = 1
EY = 4
EZ = 32
LEVELS = 3
SUBSTEPS = 4
EXT = 8
EYT = 16
NXT = 32
NYT = 64
NZ = 128


def draw_level_map(key, part):
    fine_depth = 3 * EZ // 4
    depth_step = max(EZ // 8, 1)
    band_depth = EZ // 4
    rows_devices = EXT // EX
    cols_devices = EYT // EY
    centre_x_key, centre_y_key, rough_key = jax.random.split(key, 3)
    centre_x = jax.random.randint(centre_x_key, (), 0, rows_devices)
    centre_y = jax.random.randint(centre_y_key, (), 0, cols_devices)
    device_x = jnp.arange(EXT, dtype=jnp.int32) // EX
    device_y = jnp.arange(EYT, dtype=jnp.int32) // EY
    distance = jnp.abs(device_x - centre_x)[:, None] + jnp.abs(device_y - centre_y)[None, :]
    distance = jnp.minimum(distance, 4)
    roughness = jax.random.randint(rough_key, (EXT, EYT), 0, depth_step)
    depth = jnp.where(distance == 0, fine_depth, fine_depth - depth_step * distance - roughness)
    layer = jnp.arange(EZ, dtype=jnp.int32)[None, None, :]
    levels = jnp.where(layer < depth[:, :, None], LEVELS - 1, jnp.where(layer < depth[:, :, None] + band_depth, LEVELS - 2, 0))
    return levels.astype(jnp.int32).reshape(EXT, EYT * EZ)


def block_levels(key, dims, cuts, least, largest):
    def one(position, blocks):
        steps = jax.random.uniform(jax.random.fold_in(jax.random.fold_in(key, 6), position), (blocks,), jnp.float32, least / len(cuts), largest / len(cuts))
        return jnp.repeat(jnp.exp(steps), dims[position] // blocks).reshape((-1,) + (1,) * (len(dims) - position - 1))

    factor_of = one(*cuts[0])
    for cut in cuts[1:]:
        factor_of = factor_of * one(*cut)
    return factor_of


def gaussian(key, shape, scale, reach, cuts=(), kind=jnp.bfloat16):
    values = jax.random.normal(key, shape, jnp.float32) * scale
    if len(cuts) > 0:
        values = block_levels(key, shape, cuts, -0.22, 0.18) * values
    return jnp.clip(values, min=-reach, max=reach).astype(kind)


def setup_inputs(seed: int = 0) -> dict:
    key_list = jax.random.split(jax.random.key(seed), 7)
    displacement = gaussian(key_list[0], (3, NXT, NYT, NZ), 1.0, 6.0, ((1, 8), (2, 4)), jnp.float32)
    velocity = gaussian(key_list[1], (3, NXT, NYT, NZ), 1.0, 6.0, ((1, 8), (2, 4)), jnp.float32)
    inverse_mass = jnp.clip(jnp.exp(math.log(2.0) - 1.3862944 * jax.random.uniform(key_list[2], (NXT, NYT, NZ), jnp.float32) ** block_levels(key_list[2], (NXT, NYT, NZ), ((0, 8), (1, 4)), -0.2, 0.2)), 0.5, 2.0)
    lame_first = jnp.clip(jnp.exp(math.log(2.0) - 1.3862944 * jax.random.uniform(key_list[3], (5, 5, 5, EXT, EYT * EZ), jnp.float32) ** block_levels(key_list[3], (5, 5, 5, EXT, EYT * EZ), ((3, 8), (4, 4)), -0.2, 0.2)), 0.5, 2.0)
    lame_second = jnp.clip(jnp.exp(math.log(2.0) - 1.3862944 * jax.random.uniform(key_list[4], (5, 5, 5, EXT, EYT * EZ), jnp.float32) ** block_levels(key_list[4], (5, 5, 5, EXT, EYT * EZ), ((3, 8), (4, 4)), -0.2, 0.2)), 0.5, 2.0)
    level_map = draw_level_map(jax.random.fold_in(key_list[6], 71), 0)
    return {"displacement": displacement, "velocity": velocity, "inverse_mass": inverse_mass, "lame_first": lame_first, "lame_second": lame_second, "level_map": level_map}


time_step = 0.1

def gll_tables():
    points = np.array([-1.0, -np.sqrt(3.0 / 7.0), 0.0, np.sqrt(3.0 / 7.0), 1.0])
    weights = np.array([0.1, 49.0 / 90.0, 32.0 / 45.0, 49.0 / 90.0, 0.1])
    legendre = (35.0 * points ** 4 - 30.0 * points ** 2 + 3.0) / 8.0
    derivative = np.zeros((5, 5))
    for row_index in range(5):
        for col_index in range(5):
            if row_index != col_index:
                derivative[row_index, col_index] = legendre[row_index] / (legendre[col_index] * (points[row_index] - points[col_index]))
    derivative[0, 0] = -5.0
    derivative[4, 4] = 5.0
    return (derivative, weights)

def element_forces(displaced, lame_first, lame_second, derivative, weights):
    matrix_d = jnp.asarray(derivative, jnp.float32)
    gll_weights = jnp.asarray(weights, jnp.float32)
    precise = lax.Precision.HIGHEST
    grad_x = jnp.einsum('ai,cijk...->cajk...', matrix_d, displaced, precision=precise)
    grad_y = jnp.einsum('bj,cijk...->cibk...', matrix_d, displaced, precision=precise)
    grad_z = jnp.einsum('gk,cijk...->cijg...', matrix_d, displaced, precision=precise)
    cube_weights = gll_weights[:, None, None] * gll_weights[None, :, None] * gll_weights[None, None, :]
    cube_weights = cube_weights.reshape((5, 5, 5) + (1,) * (displaced.ndim - 4))
    lame_term = lame_first * cube_weights * (grad_x[0] + grad_y[1] + grad_z[2])
    shear_half = lame_second * cube_weights
    stress_xx = lame_term + 2.0 * shear_half * grad_x[0]
    stress_yy = lame_term + 2.0 * shear_half * grad_y[1]
    stress_zz = lame_term + 2.0 * shear_half * grad_z[2]
    stress_xy = shear_half * (grad_y[0] + grad_x[1])
    stress_xz = shear_half * (grad_z[0] + grad_x[2])
    stress_yz = shear_half * (grad_z[1] + grad_y[2])
    flux_x = jnp.stack([stress_xx, stress_xy, stress_xz])
    flux_y = jnp.stack([stress_xy, stress_yy, stress_yz])
    flux_z = jnp.stack([stress_xz, stress_yz, stress_zz])
    force_x = jnp.einsum('ai,cajk...->cijk...', matrix_d, flux_x, precision=precise)
    force_y = jnp.einsum('bj,cibk...->cijk...', matrix_d, flux_y, precision=precise)
    force_z = jnp.einsum('gk,cijg...->cijk...', matrix_d, flux_z, precision=precise)
    return force_x + force_y + force_z

def expand_axis(nodal_array, dim_index):
    outer_shape = nodal_array.shape[:dim_index]
    inner_shape = nodal_array.shape[dim_index + 1:]
    element_count = (nodal_array.shape[dim_index] - 1) // 4
    leading = lax.slice_in_dim(nodal_array, 0, 4 * element_count, axis=dim_index)
    leading = leading.reshape(outer_shape + (element_count, 4) + inner_shape)
    leading = jnp.moveaxis(leading, dim_index + 1, dim_index)
    trailing = lax.slice_in_dim(nodal_array, 4, 4 * element_count + 1, stride=4, axis=dim_index)
    trailing = jnp.expand_dims(trailing, dim_index)
    return jnp.concatenate([leading, trailing], axis=dim_index)

def collapse_axis(elemental, dim_index):
    outer_shape = elemental.shape[:dim_index]
    inner_shape = elemental.shape[dim_index + 2:]
    element_count = elemental.shape[dim_index + 1]
    leading = lax.slice_in_dim(elemental, 0, 4, axis=dim_index)
    leading = jnp.moveaxis(leading, dim_index, dim_index + 1).reshape(outer_shape + (4 * element_count,) + inner_shape)
    trailing = lax.slice_in_dim(elemental, 4, 5, axis=dim_index)
    zero_block = jnp.zeros_like(lax.slice_in_dim(elemental, 0, 3, axis=dim_index))
    trailing = jnp.concatenate([zero_block, trailing], axis=dim_index)
    trailing = jnp.moveaxis(trailing, dim_index, dim_index + 1).reshape(outer_shape + (4 * element_count,) + inner_shape)
    lead_pad = [(0, 0)] * len(outer_shape) + [(0, 1)] + [(0, 0)] * len(inner_shape)
    trail_pad = [(0, 0)] * len(outer_shape) + [(1, 0)] + [(0, 0)] * len(inner_shape)
    return jnp.pad(leading, lead_pad) + jnp.pad(trailing, trail_pad)

def assembled_force(displacement, lame_first, lame_second, level_map, level_index, derivative, weights):
    padded = jnp.pad(displacement, ((0, 0), (0, 1), (0, 1), (0, 1)))
    column_total = lame_first.shape[3]
    depth_total = displacement.shape[3] // 4
    across_total = lame_first.shape[4] // depth_total

    def slab_force(column):
        start = (column * 4).astype(jnp.int32)
        slab = lax.dynamic_slice_in_dim(padded, start, 5, axis=1)
        spread = expand_axis(expand_axis(slab, 2), 4)
        spread = jnp.transpose(spread, (0, 1, 2, 4, 3, 5)).reshape((3, 5, 5, 5, across_total * depth_total))
        first_slab = lax.dynamic_index_in_dim(lame_first, column, axis=3, keepdims=False)
        second_slab = lax.dynamic_index_in_dim(lame_second, column, axis=3, keepdims=False)
        level_slab = lax.dynamic_index_in_dim(level_map, column, axis=0, keepdims=False)
        chosen = (level_slab == level_index).astype(jnp.float32)
        forces = element_forces(spread, first_slab, second_slab, derivative, weights) * chosen
        forces = forces.reshape((3, 5, 5, 5, across_total, depth_total))
        forces = jnp.transpose(forces, (0, 1, 2, 4, 3, 5))
        nodal_force = collapse_axis(collapse_axis(forces, 4), 2)
        return (nodal_force[:, :4], nodal_force[:, 4])
    leading_parts, trailing_parts = lax.map(slab_force, jnp.arange(column_total, dtype=jnp.int32))
    trailing_shift = jnp.concatenate([jnp.zeros_like(trailing_parts[:1]), trailing_parts[:-1]], axis=0)
    leading_parts = leading_parts.at[:, :, 0].add(trailing_shift)
    nodal_force = jnp.moveaxis(leading_parts, 0, 1).reshape((3, 4 * column_total) + leading_parts.shape[3:])
    return nodal_force[:, :, :displacement.shape[2], :displacement.shape[3]]

def reference(displacement, velocity, inverse_mass, lame_first, lame_second, level_map):
    derivative, weights = gll_tables()
    stored = [None] * LEVELS
    for substep in range(SUBSTEPS):
        for level_index in range(LEVELS):
            if substep % 2 ** (LEVELS - 1 - level_index) == 0:
                stored[level_index] = assembled_force(displacement, lame_first, lame_second, level_map, level_index, derivative, weights)
        total_force = stored[0]
        for level_index in range(1, LEVELS):
            total_force = total_force + stored[level_index]
        velocity = velocity - time_step * inverse_mass[None] * total_force
        displacement = displacement + time_step * velocity
    return (displacement, velocity)
```

```python
import functools

import jax
import jax.numpy as jnp
import numpy as np
from jax import lax
from jax.experimental import pallas as pl
from jax.experimental.pallas import tpu as pltpu
from jax.sharding import PartitionSpec as P

time_step = 0.1
LEVELS = 3
F32 = jnp.float32
BF16 = jnp.bfloat16


def gll_tables():
    points = np.array([-1.0, -np.sqrt(3.0 / 7.0), 0.0, np.sqrt(3.0 / 7.0), 1.0])
    weights = np.array([0.1, 49.0 / 90.0, 32.0 / 45.0, 49.0 / 90.0, 0.1])
    legendre = (35.0 * points**4 - 30.0 * points**2 + 3.0) / 8.0
    derivative = np.zeros((5, 5))
    for row_index in range(5):
        for col_index in range(5):
            if row_index != col_index:
                derivative[row_index, col_index] = legendre[row_index] / (
                    legendre[col_index] * (points[row_index] - points[col_index])
                )
    derivative[0, 0] = -5.0
    derivative[4, 4] = 5.0
    return (derivative, weights)


D, W = gll_tables()


def split(table):
    high = np.asarray(table, np.float32).astype(BF16)
    low = (np.asarray(table, np.float64) - high.astype(np.float64)).astype(BF16)
    return high, low


def depth_tables(depth):
    lanes = 4 * depth
    table = np.zeros((lanes, 2 * lanes))
    for c in range(depth):
        for i in range(5):
            if 4 * c + i < lanes:
                for k in range(4):
                    table[4 * c + i, 4 * c + k] = D[k, i]
                table[4 * c + i, lanes + (4 * (c + 1)) % lanes] = D[4, i]
    high, low = split(table)
    gradient = np.concatenate([high, high, low], axis=0)
    divergence = np.concatenate([high.T, high.T, low.T], axis=0)
    return gradient, divergence


def weight_table(depth):
    lanes = 4 * depth
    pair = (W[:, None] * W[None, :]).reshape(25, 1)
    main = pair * np.tile(W[:4], depth)[None, :]
    last = pair * np.where(np.arange(lanes) % 4 == 0, W[4], 0.0)[None, :]
    return np.concatenate([main, last], axis=0).astype(np.float32)


def apply5(matrix, x):
    s0, s1 = x[0] + x[4], x[1] + x[3]
    d0, d1 = x[0] - x[4], x[1] - x[3]

    def even(a):
        p, q = (matrix[a, 0] - matrix[a, 4]) / 2, (matrix[a, 1] - matrix[a, 3]) / 2
        return d0 * float(p) + d1 * float(q)

    def odd(a):
        p, q = (matrix[a, 0] + matrix[a, 4]) / 2, (matrix[a, 1] + matrix[a, 3]) / 2
        return s0 * float(p) + s1 * float(q) + x[2] * float(matrix[a, 2])

    e0, e1, e2 = even(0), even(1), even(2)
    o0, o1 = odd(0), odd(1)
    return [e0 + o0, e1 + o1, e2, e1 - o1, e0 - o0]


def halves(x):
    high = x.astype(BF16)
    return high, (x - high.astype(F32)).astype(BF16)


def rolled(x, by):
    return pltpu.roll(x, by % x.shape[0], 0)


def swap_pairs(nx, ny, along_x, odd):
    pairs = []
    for i in range(nx):
        for j in range(ny):
            here, size = (i, nx) if along_x else (j, ny)
            there = here + 1 if (here % 2 == 1) == odd else here - 1
            if 0 <= there < size:
                target = (there, j) if along_x else (i, there)
            else:
                target = (i, j ^ 1) if along_x else (i ^ 1, j)
            if target[0] < nx and target[1] < ny:
                pairs.append((i * ny + j, target[0] * ny + target[1]))
    return pairs


def swap(mesh_sizes, along_x, odd, x):
    return lax.ppermute(x, ("px", "py"), swap_pairs(*mesh_sizes, along_x, odd))


def place(axis, size):
    here = lax.axis_index(axis)
    return lax.rem(here, 2) == 0, here == 0, here == size - 1


def prep_kernel(sizes, rows, own_ref, e_ref, o_ref, weight_ref, u_ref, v_ref, m_ref, lame_ref, level_ref, sel):
    ny, ey, lanes = sizes
    even, first, last = place("py", ny)
    base_v, base_m, base_first, base_second, base_level, total = rows
    tall = 4 * ey

    def left(at):
        return jnp.where(first, 0.0, jnp.where(even, o_ref[at], e_ref[at]))

    def right(at):
        return jnp.where(last, 0.0, jnp.where(even, e_ref[at], o_ref[at]))

    def spread(base, out):
        for j in range(4):
            at = pl.ds(base + j, ey, stride=4)
            out[j, 0:ey, :] = left((at, slice(None)))
            out[j, ey : 2 * ey, :] = own_ref[at, :]
            out[j, 2 * ey : 3 * ey, :] = right((at, slice(None)))
            out[j, 3 * ey :, :] = jnp.zeros((ey, lanes), F32)

    for c in range(3):
        for i in range(4):
            spread((c * 4 + i) * tall, u_ref.at[c, i])
            spread(base_v + (c * 4 + i) * tall, v_ref.at[c, i])
    for i in range(4):
        spread(base_m + i * tall, m_ref.at[i])

    tail = slice(base_first, total)
    sel[0] = left((tail, slice(None)))
    sel[1] = own_ref[tail, :]
    sel[2] = right((tail, slice(None)))

    shape = (2 * ey, lanes)
    sub = lax.broadcasted_iota(jnp.int32, shape, 0)
    lane = lax.broadcasted_iota(jnp.int32, shape, 1)
    ez = lanes // 4
    column = lax.rem(sub, ey) * ez
    main_at = column + lane // 4
    last_at = column + lax.rem(lane // 4 + ez - 1, ez)
    point = lax.rem(lane, 4)
    upper = sub < ey

    def both(row):
        zero = jnp.zeros(shape, F32)
        a = jnp.broadcast_to(sel[0, pl.ds(row, 1), :], shape)
        b = jnp.broadcast_to(sel[1, pl.ds(row, 1), :], shape)
        c = jnp.broadcast_to(sel[2, pl.ds(row, 1), :], shape)
        return jnp.where(upper, a, b), jnp.where(upper, c, zero)

    def gather(x, at):
        return jnp.take_along_axis(x, at, axis=1, mode="promise_in_bounds")

    def body(ij, carry):
        weight = jnp.broadcast_to(weight_ref[pl.ds(ij, 1), :], shape)
        weight_last = jnp.broadcast_to(weight_ref[pl.ds(25 + ij, 1), :], shape)
        for p in range(2):
            start = (base_second - base_first) * p + ij * 5
            points = [both(start + k) for k in range(5)]
            for h in range(2):
                got = [gather(points[k][h], main_at) for k in range(4)]
                main = jnp.where(
                    point < 2, jnp.where(point == 0, got[0], got[1]), jnp.where(point == 2, got[2], got[3])
                )
                lame_ref[p, 0, ij, 2 * ey * h : 2 * ey * (h + 1), :] = main * weight
                lame_ref[p, 1, ij, 2 * ey * h : 2 * ey * (h + 1), :] = gather(points[4][h], last_at) * weight_last
        return carry

    lax.fori_loop(0, 25, body, 0)
    levels = both(base_level - base_first)
    for h in range(2):
        level_ref[0, 2 * ey * h : 2 * ey * (h + 1), :] = gather(levels[h], main_at)
        level_ref[1, 2 * ey * h : 2 * ey * (h + 1), :] = gather(levels[h], last_at)


def forces(tall, windows, keep, us, lame, level, old, new, grad_ref, div_ref, gx, gz, flux_x, flux_z, qy, qz, out):
    lanes = us.shape[-1]
    flat = us[...].reshape(75 * tall, lanes)
    high, low = halves(flat)
    lhs = jnp.concatenate([high, low, high], axis=1)
    gz[...] = jnp.dot(lhs, grad_ref[...], preferred_element_type=F32).reshape(3, 25, tall, 2 * lanes)
    for c in range(3):
        for j in range(5):
            y = apply5(D, [us[c, i, j] for i in range(5)])
            for i in range(5):
                gx[c, 5 * i + j] = y[i]

    inner = (lax.broadcasted_iota(jnp.int32, (8, lanes), 1) > 0).astype(F32)

    def body(i, carry):
        for h in range(tall // 8):
            at = slice(8 * h, 8 * h + 8)
            table = slice(windows[0] + 8 * h, windows[0] + 8 * h + 8)
            stored = slice(windows[1] + 8 * h, windows[1] + 8 * h + 8)
            gy = [apply5(D, [us[c, i, j, at, :] for j in range(5)]) for c in range(3)]
            if keep is not None:
                fresh = [keep(level[e, table, :]) for e in range(2)]
            across = [[], [], []]
            for j in range(5):
                p = 5 * i + j
                grads_x = [gx[c, p, at, :] for c in range(3)]
                grads_y = [gy[c][j] for c in range(3)]
                sums = []
                for e in range(2):
                    grads_z = [gz[c, p, at, e * lanes : (e + 1) * lanes] for c in range(3)]
                    if e == 1:
                        grads_x = [g * inner for g in grads_x]
                        grads_y = [g * inner for g in grads_y]
                    first, second = lame[0, e, p, table, :], lame[1, e, p, table, :]
                    trace = first * (grads_x[0] + grads_y[1] + grads_z[2])
                    twice = second + second
                    stress = [
                        trace + twice * grads_x[0],
                        trace + twice * grads_y[1],
                        second * (grads_y[0] + grads_x[1]),
                        second * (grads_z[0] + grads_x[2]),
                        second * (grads_z[1] + grads_y[2]),
                        trace + twice * grads_z[2],
                    ]
                    if keep is not None:
                        stress = [
                            jnp.where(fresh[e], stress[n], old[n, e, p, stored, :]) for n in range(6)
                        ]
                    if new is not None:
                        for n in range(6):
                            new[n, e, p, at, :] = stress[n]
                    if flux_z is not None:
                        for n in range(3):
                            flux_z[n, e, p, at, :] = stress[3 + n]
                    if e == 1:
                        stress = [x * inner for x in stress[:5]]
                    sums.append(stress)
                xx, yy, xy, xz, yz = [sums[0][n] + sums[1][n] for n in range(5)]
                for c, value in enumerate((xx, xy, xz)):
                    flux_x[c, p, at, :] = value
                for c, value in enumerate((xy, yy, yz)):
                    across[c].append(value)
            for c in range(3):
                y = apply5(D.T, across[c])
                for j in range(5):
                    qy[c, 5 * i + j, at, :] = y[j]
        return carry

    lax.fori_loop(0, 5, body, 0)
    if flux_z is None:
        flux_z = new.at[3:6]
    high0, low0 = halves(flux_z[:, 0].reshape(75 * tall, lanes))
    high1, low1 = halves(flux_z[:, 1].reshape(75 * tall, lanes))
    lhs = jnp.concatenate([high0, high1, low0, low1, high0, high1], axis=1)
    qz[...] = jnp.dot(lhs, div_ref[...], preferred_element_type=F32).reshape(3, 25, tall, lanes)
    for c in range(3):
        ends = None
        for j in (4, 0, 1, 2, 3):
            x = apply5(D.T, [flux_x[c, 5 * i + j] for i in range(5)])
            x = [x[i] + (qy[c, 5 * i + j] + qz[c, 5 * i + j]) for i in range(5)]
            if j == 4:
                ends = [rolled(v, 1) for v in x]
                continue
            for i in range(5):
                out[c, i, j] = x[i] + ends[i] if j == 0 else x[i]


def fill_points(us, c, i, values):
    for j in range(4):
        us[c, i, j] = values[j]
    us[c, i, 4] = rolled(values[0], -1)


def start_kernel(sizes, u_ref, v_ref, m_ref, lame, level, a_ref, b_ref, grad_ref, div_ref,
                 rim_ref, old_ref, total_ref, send_a, send_b, us, gx, gz, flux_x, qy, qz):
    nx, ey, lanes = sizes
    even, _, last = place("px", nx)
    tall = 4 * ey
    wide = 3 * ey
    for c in range(3):
        for i in range(4):
            fill_points(us, c, i, [u_ref[c, i, j] for j in range(4)])
        for j in range(4):
            at = pl.ds(j, wide, stride=4)
            rim = jnp.where(last, 0.0, jnp.where(even, a_ref[c, at, :], b_ref[c, at, :]))
            rim_ref[c, j, 0:wide, :] = rim
            rim_ref[c, j, wide:, :] = jnp.zeros((tall - wide, lanes), F32)
        fill_points(us, c, 4, [rim_ref[c, j] for j in range(4)])
    forces(tall, (0, 0), None, us, lame, level, None, old_ref, grad_ref, div_ref, gx, gz, flux_x, None, qy, qz, total_ref)
    count = wide - 2
    for j in range(4):
        at = slice(j * count, (j + 1) * count)
        mass = m_ref[0, j, 1 : 1 + count, :]
        for c in range(3):
            back = v_ref[c, 0, j, 1 : 1 + count, :] - time_step * mass * total_ref[c, 0, j, 1 : 1 + count, :]
            ahead = total_ref[c, 4, j, 1 : 1 + count, :]
            send_a[c, at, :] = jnp.where(even, ahead, back)
            send_b[c, at, :] = jnp.where(even, back, ahead)
        send_a[3, at, :] = mass
        send_b[3, at, :] = mass


def second_kernel(sizes, u_ref, rim_ref, v_ref, m_ref, total_ref, a_ref, b_ref, old, lame, level, grad_ref, div_ref,
                  u_out, v_out, m_out, total_out, send_a, send_b,
                  got, us, gx, gz, flux_x, flux_z, qy, qz, total):
    nx, ey, lanes = sizes
    even, first, last = place("px", nx)
    tall, count = 4 * ey, 3 * ey - 2
    low, high = ey - 2, 3 * ey - 2
    got[...] = jnp.zeros(got.shape, F32)
    for j in range(4):
        at = slice(j * count, (j + 1) * count)
        for c in range(4):
            got[0, c, j, 1 : 1 + count, :] = jnp.where(last, 0.0, jnp.where(even, a_ref[c, at, :], b_ref[c, at, :]))
        for c in range(3):
            got[1, c, j, 1 : 1 + count, :] = jnp.where(first, 0.0, jnp.where(even, b_ref[c, at, :], a_ref[c, at, :]))
    for c in range(3):
        for i in range(5):
            values = []
            for j in range(4):
                force = total_ref[c, i, j]
                mass = m_ref[i, j] if i < 4 else got[0, 3, j]
                if i == 0:
                    force = force + got[1, c, j]
                before = v_ref[c, i, j] if i < 4 else got[0, c, j]
                position = u_ref[c, i, j] if i < 4 else rim_ref[c, j]
                speed = before - time_step * mass * force
                position = position + time_step * speed
                u_out[c, i, j] = position[low:high]
                v_out[c, i, j] = speed[low:high]
                if c == 0:
                    m_out[i, j] = mass[low:high]
                values.append(position)
            fill_points(us, c, i, values)
    forces(tall, (0, 0), lambda level_of: level_of > 1.5, us, lame, level, old, None, grad_ref, div_ref,
           gx, gz, flux_x, flux_z, qy, qz, total)
    for c in range(3):
        for i in range(5):
            for j in range(4):
                total_out[c, i, j] = total[c, i, j, low:high, :]
        for j in range(4):
            back, ahead = total_out[c, 0, j], total_out[c, 4, j]
            send_a[c, j] = jnp.where(even, ahead, back)
            send_b[c, j] = jnp.where(even, back, ahead)


def later_kernel(sizes, final, u_ref, v_ref, m_ref, total_ref, a_ref, b_ref, old, lame, level, grad_ref, div_ref, *refs):
    nx, ey, lanes = sizes
    if final:
        u_out, v_out, total_out, send_a, send_b, us, gx, gz, flux_x, flux_z, qy, qz = refs
        new, keep, windows = None, lambda level_of: level_of > 1.5, (ey - 2, 0)
    else:
        u_out, v_out, new, total_out, send_a, send_b, us, gx, gz, flux_x, qy, qz = refs
        flux_z, keep, windows = None, lambda level_of: level_of > 0.5, (ey - 2, ey - 2)
    even, first, last = place("px", nx)
    for c in range(3):
        for i in range(5):
            values = []
            for j in range(4):
                force = total_ref[c, i, j]
                if i == 0:
                    force = force + jnp.where(first, 0.0, jnp.where(even, b_ref[c, j], a_ref[c, j]))
                if i == 4:
                    force = force + jnp.where(last, 0.0, jnp.where(even, a_ref[c, j], b_ref[c, j]))
                speed = v_ref[c, i, j] - time_step * m_ref[i, j] * force
                position = u_ref[c, i, j] + time_step * speed
                u_out[c, i, j] = position
                v_out[c, i, j] = speed
                values.append(position)
            fill_points(us, c, i, values)
    forces(2 * ey, windows, keep, us, lame, level, old, new, grad_ref, div_ref,
           gx, gz, flux_x, flux_z, qy, qz, total_out)
    for c in range(3):
        for j in range(4):
            if final:
                at = slice(j * ey, (j + 1) * ey)
                send_a[c, at, :] = total_out[c, 4, j, 2 : 2 + ey, :]
                send_b[c, at, :] = send_a[c, at, :]
            else:
                back, ahead = total_out[c, 0, j], total_out[c, 4, j]
                send_a[c, j] = jnp.where(even, ahead, back)
                send_b[c, j] = jnp.where(even, back, ahead)


def end_kernel(sizes, u_ref, v_ref, m_ref, total_ref, a_ref, b_ref, u_out, v_out):
    nx, ey, lanes = sizes
    even, first, _ = place("px", nx)
    mine = slice(2, 2 + ey)
    for c in range(3):
        for i in range(4):
            for j in range(4):
                force = total_ref[c, i, j, mine, :]
                if i == 0:
                    at = slice(j * ey, (j + 1) * ey)
                    force = force + jnp.where(first, 0.0, jnp.where(even, b_ref[c, at, :], a_ref[c, at, :]))
                speed = v_ref[c, i, j, mine, :] - time_step * m_ref[i, j, mine, :] * force
                v_out[c, i, pl.ds(j, ey, stride=4), :] = speed
                u_out[c, i, pl.ds(j, ey, stride=4), :] = u_ref[c, i, j, mine, :] + time_step * speed


def call(kernel, name, outs, scratch, *args):
    shapes = [jax.ShapeDtypeStruct(s, F32) for s in outs]
    return pl.pallas_call(
        kernel,
        out_shape=shapes,
        scratch_shapes=[pltpu.VMEM(s, F32) for s in scratch],
        compiler_params=pltpu.CompilerParams(vmem_limit_bytes=32 * 1024 * 1024),
        name=name,
    )(*args)


def shards(sizes, displacement, velocity, inverse_mass, lame_first, lame_second, level_map):
    nx, ny = sizes
    _, ex4, ey4, lanes = displacement.shape
    ey = ey4 // 4
    tall, wide, short = 4 * ey, 3 * ey, 2 * ey
    move = functools.partial(swap, sizes)

    def rows_of(x, pad):
        x = x.reshape(-1, lanes).astype(F32)
        return jnp.pad(x, ((0, pad), (0, 0))) if pad else x

    pieces = [rows_of(displacement, 0), rows_of(velocity, 0), rows_of(inverse_mass, 0),
              rows_of(lame_first, 3), rows_of(lame_second, 3), rows_of(level_map, 7)]
    bounds = np.cumsum([0] + [p.shape[0] for p in pieces])
    own = jnp.concatenate(pieces, axis=0)
    from_e = move(False, False, own)
    from_o = move(False, True, own)
    here = lax.axis_index("py")
    even_y = here % 2 == 0

    def layer(x):
        return x[: bounds[1]].reshape(3, 4, ey4, lanes)[:, 0]

    layer_left = jnp.where(here == 0, 0.0, jnp.where(even_y, layer(from_o), layer(from_e)))
    layer_right = jnp.where(here == ny - 1, 0.0, jnp.where(even_y, layer(from_e), layer(from_o)))
    rim = jnp.concatenate([layer_left, displacement[:, 0], layer_right], axis=1)
    rim_a = move(True, False, rim)
    rim_b = move(True, True, rim)

    weights = jnp.asarray(weight_table(lanes // 4))
    gradient, divergence = (jnp.asarray(t) for t in depth_tables(lanes // 4))
    field = (3, 4, 4, tall, lanes)
    u, v, m, lame, level = call(
        functools.partial(prep_kernel, (ny, ey, lanes), tuple(int(b) for b in bounds[1:])), "prep",
        [field, field, field[1:], (2, 2, 25, tall, lanes), (2, tall, lanes)],
        [(3, int(bounds[6] - bounds[3]), lanes)],
        own, from_e, from_o, weights,
    )

    def scratch(rows, with_flux):
        points = (3, 25, rows, lanes)
        flux = [(3, 2, 25, rows, lanes)] if with_flux else []
        return [(3, 5, 5, rows, lanes), points, (3, 25, rows, 2 * lanes), points] + flux + [points, points]

    sizes_x = (nx, ey, lanes)
    count = wide - 2
    rim_u, old, total, send_a, send_b = call(
        functools.partial(start_kernel, sizes_x), "substep0",
        [(3, 4, tall, lanes), (6, 2, 25, tall, lanes), (3, 5, 4, tall, lanes), (4, 4 * count, lanes), (4, 4 * count, lanes)],
        scratch(tall, False),
        u, v, m, lame, level, rim_a, rim_b, gradient, divergence,
    )
    got_a, got_b = move(True, False, send_a), move(True, True, send_b)

    state = (3, 5, 4, short, lanes)
    message = (3, 4, short, lanes)
    u, v, m, total, send_a, send_b = call(
        functools.partial(second_kernel, sizes_x), "substep1",
        [state, state, state[1:], state, message, message],
        [(2, 4, 4, tall, lanes)] + scratch(tall, True) + [(3, 5, 4, tall, lanes)],
        u, rim_u, v, m, total, got_a, got_b, old, lame, level, gradient, divergence,
    )
    got_a, got_b = move(True, False, send_a), move(True, True, send_b)

    u, v, old, total, send_a, send_b = call(
        functools.partial(later_kernel, sizes_x, False), "substep2",
        [state, state, (6, 2, 25, short, lanes), state, message, message],
        scratch(short, False),
        u, v, m, total, got_a, got_b, old, lame, level, gradient, divergence,
    )
    got_a, got_b = move(True, False, send_a), move(True, True, send_b)

    u, v, total, send_a, send_b = call(
        functools.partial(later_kernel, sizes_x, True), "substep3",
        [state, state, state, (3, 4 * ey, lanes), (3, 4 * ey, lanes)],
        scratch(short, True),
        u, v, m, total, got_a, got_b, old, lame, level, gradient, divergence,
    )
    got_a, got_b = move(True, False, send_a), move(True, True, send_b)

    return tuple(call(
        functools.partial(end_kernel, sizes_x), "end",
        [displacement.shape, velocity.shape], [],
        u, v, m, total, got_a, got_b,
    ))


def solution(mesh):
    sizes = (mesh.shape["px"], mesh.shape["py"])
    in_specs = (
        P(None, "px", "py", None),
        P(None, "px", "py", None),
        P("px", "py", None),
        P(None, None, None, "px", "py"),
        P(None, None, None, "px", "py"),
        P("px", "py"),
    )
    out_specs = (P(None, "px", "py", None), P(None, "px", "py", None))
    return jax.shard_map(
        functools.partial(shards, sizes), mesh=mesh, in_specs=in_specs, out_specs=out_specs, check_vma=False
    )
```

```python
import functools

import jax
import jax.numpy as jnp
import numpy as np
from jax import lax
from jax.experimental import pallas as pl
from jax.experimental.pallas import tpu as pltpu
from jax.sharding import PartitionSpec as P

time_step = 0.1
LEVELS = 3
F32 = jnp.float32
BF16 = jnp.bfloat16


def gll_tables():
    points = np.array([-1.0, -np.sqrt(3.0 / 7.0), 0.0, np.sqrt(3.0 / 7.0), 1.0])
    weights = np.array([0.1, 49.0 / 90.0, 32.0 / 45.0, 49.0 / 90.0, 0.1])
    legendre = (35.0 * points**4 - 30.0 * points**2 + 3.0) / 8.0
    derivative = np.zeros((5, 5))
    for row_index in range(5):
        for col_index in range(5):
            if row_index != col_index:
                derivative[row_index, col_index] = legendre[row_index] / (
                    legendre[col_index] * (points[row_index] - points[col_index])
                )
    derivative[0, 0] = -5.0
    derivative[4, 4] = 5.0
    return (derivative, weights)


D, W = gll_tables()


def split(table):
    high = np.asarray(table, np.float32).astype(BF16)
    low = (np.asarray(table, np.float64) - high.astype(np.float64)).astype(BF16)
    return high, low


def depth_tables(depth):
    lanes = 4 * depth
    table = np.zeros((lanes, 2 * lanes))
    for c in range(depth):
        for i in range(5):
            if 4 * c + i < lanes:
                for k in range(4):
                    table[4 * c + i, 4 * c + k] = D[k, i]
                table[4 * c + i, lanes + (4 * (c + 1)) % lanes] = D[4, i]
    high, low = split(table)
    gradient = np.concatenate([high, high, low], axis=0)
    divergence = np.concatenate([high.T, high.T, low.T], axis=0)
    return gradient, divergence


def weight_table(depth):
    lanes = 4 * depth
    pair = (W[:, None] * W[None, :]).reshape(25, 1)
    main = pair * np.tile(W[:4], depth)[None, :]
    last = pair * np.where(np.arange(lanes) % 4 == 0, W[4], 0.0)[None, :]
    return np.concatenate([main, last], axis=0).astype(np.float32)


def apply5(matrix, x):
    s0, s1 = x[0] + x[4], x[1] + x[3]
    d0, d1 = x[0] - x[4], x[1] - x[3]

    def even(a):
        p, q = (matrix[a, 0] - matrix[a, 4]) / 2, (matrix[a, 1] - matrix[a, 3]) / 2
        return d0 * float(p) + d1 * float(q)

    def odd(a):
        p, q = (matrix[a, 0] + matrix[a, 4]) / 2, (matrix[a, 1] + matrix[a, 3]) / 2
        return s0 * float(p) + s1 * float(q) + x[2] * float(matrix[a, 2])

    e0, e1, e2 = even(0), even(1), even(2)
    o0, o1 = odd(0), odd(1)
    return [e0 + o0, e1 + o1, e2, e1 - o1, e0 - o0]


def halves(x):
    high = x.astype(BF16)
    return high, (x - high.astype(F32)).astype(BF16)


def rolled(x, by):
    return pltpu.roll(x, by % x.shape[0], 0)


def swap_pairs(nx, ny, along_x, odd):
    pairs = []
    for i in range(nx):
        for j in range(ny):
            here, size = (i, nx) if along_x else (j, ny)
            there = here + 1 if (here % 2 == 1) == odd else here - 1
            if 0 <= there < size:
                target = (there, j) if along_x else (i, there)
            else:
                target = (i, j ^ 1) if along_x else (i ^ 1, j)
            if target[0] < nx and target[1] < ny:
                pairs.append((i * ny + j, target[0] * ny + target[1]))
    return pairs


def swap(mesh_sizes, along_x, odd, x):
    return lax.ppermute(x, ("px", "py"), swap_pairs(*mesh_sizes, along_x, odd))


def place(axis, size):
    here = lax.axis_index(axis)
    return lax.rem(here, 2) == 0, here == 0, here == size - 1


def load_kernel(bounds, *refs):
    u_hbm, v_hbm, m_hbm, first_hbm, second_hbm, level_hbm, *tables_hbm = refs[: 6 + 3]
    u_out, out, *tables = refs[9 : 9 + 2 + 3]
    first, second, level, sems = refs[14:]
    copies = [
        (first_hbm, first), (second_hbm, second), (level_hbm, level), (u_hbm, u_out),
        (v_hbm, out.at[0 : bounds[0]]), (m_hbm, out.at[bounds[0] : bounds[1]]), *zip(tables_hbm, tables),
    ]
    copies = [pltpu.make_async_copy(a, b, sems.at[n]) for n, (a, b) in enumerate(copies)]
    for copy in copies:
        copy.start()
    for p, table in enumerate((first, second)):
        copies[p].wait()
        for row in range(125):
            i, j, k = row // 25, row // 5 % 5, row % 5
            out[bounds[1 + p] + row : bounds[1 + p] + row + 1, :] = table[i, j, k]
    copies[2].wait()
    out[bounds[3] : bounds[3] + 1, :] = level[...].astype(F32)
    for copy in copies[3:]:
        copy.wait()


def prep_kernel(sizes, bounds, own_u, e_u, o_u, own_ref, e_ref, o_ref, weight_ref, u_ref, v_ref, m_ref, lame_ref, level_ref, sel):
    ny, ey, lanes = sizes
    even, first, last = place("py", ny)
    tall = 4 * ey
    base_first, base_second, base_level = bounds[1:4]

    def left(e, o, at):
        return jnp.where(first, 0.0, jnp.where(even, o[at], e[at]))

    def right(e, o, at):
        return jnp.where(last, 0.0, jnp.where(even, e[at], o[at]))

    def spread(own, e, o, base, out):
        for j in range(4):
            at = (pl.ds(base + j, ey, stride=4), slice(None))
            out[j, 0:ey, :] = left(e, o, at)
            out[j, ey : 2 * ey, :] = own[at]
            out[j, 2 * ey : 3 * ey, :] = right(e, o, at)
            out[j, 3 * ey :, :] = jnp.zeros((ey, lanes), F32)

    for i in range(4):
        for c in range(3):
            spread(own_u, e_u, o_u, (c * 4 + i) * tall, u_ref.at[c, i])
            spread(own_ref, e_ref, o_ref, (c * 4 + i) * tall, v_ref.at[c, i])
        spread(own_ref, e_ref, o_ref, bounds[0] + i * tall, m_ref.at[i])

    tail = (slice(base_first, own_ref.shape[0]), slice(None))
    sel[0] = left(e_ref, o_ref, tail)
    sel[1] = own_ref[tail]
    sel[2] = right(e_ref, o_ref, tail)

    shape = (2 * ey, lanes)
    sub = lax.broadcasted_iota(jnp.int32, shape, 0)
    lane = lax.broadcasted_iota(jnp.int32, shape, 1)
    ez = lanes // 4
    column = lax.rem(sub, ey) * ez
    main_at = column + lane // 4
    last_at = column + lax.rem(lane // 4 + ez - 1, ez)
    point = lax.rem(lane, 4)
    upper = sub < ey

    def both(row):
        zero = jnp.zeros(shape, F32)
        a = jnp.broadcast_to(sel[0, pl.ds(row, 1), :], shape)
        b = jnp.broadcast_to(sel[1, pl.ds(row, 1), :], shape)
        c = jnp.broadcast_to(sel[2, pl.ds(row, 1), :], shape)
        return jnp.where(upper, a, b), jnp.where(upper, c, zero)

    def gather(x, at):
        return jnp.take_along_axis(x, at, axis=1, mode="promise_in_bounds")

    def body(ij, carry):
        weight = jnp.broadcast_to(weight_ref[pl.ds(ij, 1), :], shape)
        weight_last = jnp.broadcast_to(weight_ref[pl.ds(25 + ij, 1), :], shape)
        for p in range(2):
            start = (base_second - base_first) * p + ij * 5
            points = [both(start + k) for k in range(5)]
            for h in range(2):
                got = [gather(points[k][h], main_at) for k in range(4)]
                main = jnp.where(
                    point < 2, jnp.where(point == 0, got[0], got[1]), jnp.where(point == 2, got[2], got[3])
                )
                lame_ref[p, 0, ij, 2 * ey * h : 2 * ey * (h + 1), :] = main * weight
                lame_ref[p, 1, ij, 2 * ey * h : 2 * ey * (h + 1), :] = gather(points[4][h], last_at) * weight_last
        return carry

    lax.fori_loop(0, 25, body, 0)
    levels = both(base_level - base_first)
    for h in range(2):
        level_ref[0, 2 * ey * h : 2 * ey * (h + 1), :] = gather(levels[h], main_at)
        level_ref[1, 2 * ey * h : 2 * ey * (h + 1), :] = gather(levels[h], last_at)


def forces(tall, windows, keep, us, lame, level, old, new, grad_ref, div_ref, gx, gz, flux_x, flux_z, qy, qz, out):
    lanes = us.shape[-1]
    flat = us[...].reshape(75 * tall, lanes)
    high, low = halves(flat)
    lhs = jnp.concatenate([high, low, high], axis=1)
    gz[...] = jnp.dot(lhs, grad_ref[...], preferred_element_type=F32).reshape(3, 25, tall, 2 * lanes)
    for c in range(3):
        for j in range(5):
            y = apply5(D, [us[c, i, j] for i in range(5)])
            for i in range(5):
                gx[c, 5 * i + j] = y[i]

    inner = (lax.broadcasted_iota(jnp.int32, (8, lanes), 1) > 0).astype(F32)

    def body(i, carry):
        for h in range(tall // 8):
            at = slice(8 * h, 8 * h + 8)
            table = slice(windows[0] + 8 * h, windows[0] + 8 * h + 8)
            stored = slice(windows[1] + 8 * h, windows[1] + 8 * h + 8)
            gy = [apply5(D, [us[c, i, j, at, :] for j in range(5)]) for c in range(3)]
            if keep is not None:
                fresh = [keep(level[e, table, :]) for e in range(2)]
            across = [[], [], []]
            for j in range(5):
                p = 5 * i + j
                grads_x = [gx[c, p, at, :] for c in range(3)]
                grads_y = [gy[c][j] for c in range(3)]
                sums = []
                for e in range(2):
                    grads_z = [gz[c, p, at, e * lanes : (e + 1) * lanes] for c in range(3)]
                    if e == 1:
                        grads_x = [g * inner for g in grads_x]
                        grads_y = [g * inner for g in grads_y]
                    first, second = lame[0, e, p, table, :], lame[1, e, p, table, :]
                    trace = first * (grads_x[0] + grads_y[1] + grads_z[2])
                    twice = second + second
                    stress = [
                        trace + twice * grads_x[0],
                        trace + twice * grads_y[1],
                        second * (grads_y[0] + grads_x[1]),
                        second * (grads_z[0] + grads_x[2]),
                        second * (grads_z[1] + grads_y[2]),
                        trace + twice * grads_z[2],
                    ]
                    if keep is not None:
                        stress = [
                            jnp.where(fresh[e], stress[n], old[n, e, p, stored, :]) for n in range(6)
                        ]
                    if new is not None:
                        for n in range(6):
                            new[n, e, p, at, :] = stress[n]
                    if flux_z is not None:
                        for n in range(3):
                            flux_z[n, e, p, at, :] = stress[3 + n]
                    if e == 1:
                        stress = [x * inner for x in stress[:5]]
                    sums.append(stress)
                xx, yy, xy, xz, yz = [sums[0][n] + sums[1][n] for n in range(5)]
                for c, value in enumerate((xx, xy, xz)):
                    flux_x[c, p, at, :] = value
                for c, value in enumerate((xy, yy, yz)):
                    across[c].append(value)
            for c in range(3):
                y = apply5(D.T, across[c])
                for j in range(5):
                    qy[c, 5 * i + j, at, :] = y[j]
        return carry

    lax.fori_loop(0, 5, body, 0)
    if flux_z is None:
        flux_z = new.at[3:6]
    high0, low0 = halves(flux_z[:, 0].reshape(75 * tall, lanes))
    high1, low1 = halves(flux_z[:, 1].reshape(75 * tall, lanes))
    lhs = jnp.concatenate([high0, high1, low0, low1, high0, high1], axis=1)
    qz[...] = jnp.dot(lhs, div_ref[...], preferred_element_type=F32).reshape(3, 25, tall, lanes)
    for c in range(3):
        ends = None
        for j in (4, 0, 1, 2, 3):
            x = apply5(D.T, [flux_x[c, 5 * i + j] for i in range(5)])
            x = [x[i] + (qy[c, 5 * i + j] + qz[c, 5 * i + j]) for i in range(5)]
            if j == 4:
                ends = [rolled(v, 1) for v in x]
                continue
            for i in range(5):
                out[c, i, j] = x[i] + ends[i] if j == 0 else x[i]


def fill_points(us, c, i, values):
    for j in range(4):
        us[c, i, j] = values[j]
    us[c, i, 4] = rolled(values[0], -1)


def start_kernel(sizes, u_ref, v_ref, m_ref, lame, level, a_ref, b_ref, grad_ref, div_ref,
                 rim_ref, old_ref, total_ref, send_a, send_b, us, gx, gz, flux_x, qy, qz):
    nx, ey, lanes = sizes
    even, _, last = place("px", nx)
    tall = 4 * ey
    wide = 3 * ey
    for c in range(3):
        for i in range(4):
            fill_points(us, c, i, [u_ref[c, i, j] for j in range(4)])
        for j in range(4):
            at = pl.ds(j, wide, stride=4)
            rim = jnp.where(last, 0.0, jnp.where(even, a_ref[c, at, :], b_ref[c, at, :]))
            rim_ref[c, j, 0:wide, :] = rim
            rim_ref[c, j, wide:, :] = jnp.zeros((tall - wide, lanes), F32)
        fill_points(us, c, 4, [rim_ref[c, j] for j in range(4)])
    forces(tall, (0, 0), None, us, lame, level, None, old_ref, grad_ref, div_ref, gx, gz, flux_x, None, qy, qz, total_ref)
    count = wide - 2
    for j in range(4):
        at = slice(j * count, (j + 1) * count)
        mass = m_ref[0, j, 1 : 1 + count, :]
        for c in range(3):
            back = v_ref[c, 0, j, 1 : 1 + count, :] - time_step * mass * total_ref[c, 0, j, 1 : 1 + count, :]
            ahead = total_ref[c, 4, j, 1 : 1 + count, :]
            send_a[c, at, :] = jnp.where(even, ahead, back)
            send_b[c, at, :] = jnp.where(even, back, ahead)
        send_a[3, at, :] = mass
        send_b[3, at, :] = mass


def second_kernel(sizes, u_ref, rim_ref, v_ref, m_ref, total_ref, a_ref, b_ref, old, lame, level, grad_ref, div_ref,
                  u_out, v_out, m_out, total_out, send_a, send_b,
                  got, us, gx, gz, flux_x, flux_z, qy, qz, total):
    nx, ey, lanes = sizes
    even, first, last = place("px", nx)
    tall, count = 4 * ey, 3 * ey - 2
    low, high = ey - 2, 3 * ey - 2
    got[...] = jnp.zeros(got.shape, F32)
    for j in range(4):
        at = slice(j * count, (j + 1) * count)
        for c in range(4):
            got[0, c, j, 1 : 1 + count, :] = jnp.where(last, 0.0, jnp.where(even, a_ref[c, at, :], b_ref[c, at, :]))
        for c in range(3):
            got[1, c, j, 1 : 1 + count, :] = jnp.where(first, 0.0, jnp.where(even, b_ref[c, at, :], a_ref[c, at, :]))
    for c in range(3):
        for i in range(5):
            values = []
            for j in range(4):
                force = total_ref[c, i, j]
                mass = m_ref[i, j] if i < 4 else got[0, 3, j]
                if i == 0:
                    force = force + got[1, c, j]
                before = v_ref[c, i, j] if i < 4 else got[0, c, j]
                position = u_ref[c, i, j] if i < 4 else rim_ref[c, j]
                speed = before - time_step * mass * force
                position = position + time_step * speed
                u_out[c, i, j] = position[low:high]
                v_out[c, i, j] = speed[low:high]
                if c == 0:
                    m_out[i, j] = mass[low:high]
                values.append(position)
            fill_points(us, c, i, values)
    forces(tall, (0, 0), lambda level_of: level_of > 1.5, us, lame, level, old, None, grad_ref, div_ref,
           gx, gz, flux_x, flux_z, qy, qz, total)
    for c in range(3):
        for i in range(5):
            for j in range(4):
                total_out[c, i, j] = total[c, i, j, low:high, :]
        for j in range(4):
            back, ahead = total_out[c, 0, j], total_out[c, 4, j]
            send_a[c, j] = jnp.where(even, ahead, back)
            send_b[c, j] = jnp.where(even, back, ahead)


def later_kernel(sizes, final, u_ref, v_ref, m_ref, total_ref, a_ref, b_ref, old, lame, level, grad_ref, div_ref, *refs):
    nx, ey, lanes = sizes
    if final:
        u_out, v_out, total_out, send_a, send_b, us, gx, gz, flux_x, flux_z, qy, qz = refs
        new, keep, windows = None, lambda level_of: level_of > 1.5, (ey - 2, 0)
    else:
        u_out, v_out, new, total_out, send_a, send_b, us, gx, gz, flux_x, qy, qz = refs
        flux_z, keep, windows = None, lambda level_of: level_of > 0.5, (ey - 2, ey - 2)
    even, first, last = place("px", nx)
    for c in range(3):
        for i in range(5):
            values = []
            for j in range(4):
                force = total_ref[c, i, j]
                if i == 0:
                    force = force + jnp.where(first, 0.0, jnp.where(even, b_ref[c, j], a_ref[c, j]))
                if i == 4:
                    force = force + jnp.where(last, 0.0, jnp.where(even, a_ref[c, j], b_ref[c, j]))
                speed = v_ref[c, i, j] - time_step * m_ref[i, j] * force
                position = u_ref[c, i, j] + time_step * speed
                u_out[c, i, j] = position
                v_out[c, i, j] = speed
                values.append(position)
            fill_points(us, c, i, values)
    forces(2 * ey, windows, keep, us, lame, level, old, new, grad_ref, div_ref,
           gx, gz, flux_x, flux_z, qy, qz, total_out)
    for c in range(3):
        for j in range(4):
            if final:
                at = slice(j * ey, (j + 1) * ey)
                send_a[c, at, :] = total_out[c, 4, j, 2 : 2 + ey, :]
                send_b[c, at, :] = send_a[c, at, :]
            else:
                back, ahead = total_out[c, 0, j], total_out[c, 4, j]
                send_a[c, j] = jnp.where(even, ahead, back)
                send_b[c, j] = jnp.where(even, back, ahead)


def end_kernel(sizes, u_ref, v_ref, m_ref, total_ref, a_ref, b_ref, u_out, v_out):
    nx, ey, lanes = sizes
    even, first, _ = place("px", nx)
    mine = slice(2, 2 + ey)
    for c in range(3):
        for i in range(4):
            for j in range(4):
                force = total_ref[c, i, j, mine, :]
                if i == 0:
                    at = slice(j * ey, (j + 1) * ey)
                    force = force + jnp.where(first, 0.0, jnp.where(even, b_ref[c, at, :], a_ref[c, at, :]))
                speed = v_ref[c, i, j, mine, :] - time_step * m_ref[i, j, mine, :] * force
                v_out[c, i, pl.ds(j, ey, stride=4), :] = speed
                u_out[c, i, pl.ds(j, ey, stride=4), :] = u_ref[c, i, j, mine, :] + time_step * speed


def call(kernel, name, outs, scratch, *args):
    shapes = [jax.ShapeDtypeStruct(s, F32) if name == "end" else pltpu.VMEM(s, F32) for s in outs]
    return pl.pallas_call(
        kernel,
        out_shape=shapes,
        scratch_shapes=[pltpu.VMEM(s, F32) for s in scratch],
        compiler_params=pltpu.CompilerParams(vmem_limit_bytes=32 * 1024 * 1024),
        name=name,
    )(*args)


def shards(sizes, displacement, velocity, inverse_mass, lame_first, lame_second, level_map):
    nx, ny = sizes
    _, ex4, ey4, lanes = displacement.shape
    ey = ey4 // 4
    tall, wide, short = 4 * ey, 3 * ey, 2 * ey
    move = functools.partial(swap, sizes)

    flat_u = displacement.reshape(-1, lanes)
    u_e, u_o = move(False, False, flat_u), move(False, True, flat_u)
    flat_v, flat_m = velocity.reshape(-1, lanes), inverse_mass.reshape(-1, lanes)
    bounds = [int(b) for b in np.cumsum([flat_v.shape[0], flat_m.shape[0], 128, 128, 8])]
    gradient, divergence = depth_tables(lanes // 4)
    tables = [jnp.asarray(t) for t in (gradient, divergence, weight_table(lanes // 4))]
    anywhere = pl.BlockSpec(memory_space=pl.ANY)
    own_u, own, gradient, divergence, weights = pl.pallas_call(
        functools.partial(load_kernel, bounds),
        out_shape=[pltpu.VMEM(flat_u.shape, F32), pltpu.VMEM((bounds[4], lanes), F32)]
        + [pltpu.VMEM(t.shape, t.dtype) for t in tables],
        in_specs=[anywhere] * 9,
        scratch_shapes=[
            pltpu.VMEM(lame_first.shape, F32),
            pltpu.VMEM(lame_second.shape, F32),
            pltpu.VMEM(level_map.shape, jnp.int32),
            pltpu.SemaphoreType.DMA((9,)),
        ],
        name="load",
    )(flat_u, flat_v, flat_m, lame_first, lame_second, level_map, *tables)
    from_e, from_o = move(False, False, own), move(False, True, own)
    here = lax.axis_index("py")
    even_y = here % 2 == 0

    def layer(x):
        return x.reshape(3, 4, ey4, lanes)[:, 0]

    layer_left = jnp.where(here == 0, 0.0, jnp.where(even_y, layer(u_o), layer(u_e)))
    layer_right = jnp.where(here == ny - 1, 0.0, jnp.where(even_y, layer(u_e), layer(u_o)))
    rim = jnp.concatenate([layer_left, layer(own_u), layer_right], axis=1)
    rim_a = move(True, False, rim)
    rim_b = move(True, True, rim)

    field = (3, 4, 4, tall, lanes)
    u, v, m, lame, level = call(
        functools.partial(prep_kernel, (ny, ey, lanes), bounds), "prep",
        [field, field, field[1:], (2, 2, 25, tall, lanes), (2, tall, lanes)],
        [(3, bounds[4] - bounds[1], lanes)],
        own_u, u_e, u_o, own, from_e, from_o, weights,
    )

    def scratch(rows, with_flux):
        points = (3, 25, rows, lanes)
        flux = [(3, 2, 25, rows, lanes)] if with_flux else []
        return [(3, 5, 5, rows, lanes), points, (3, 25, rows, 2 * lanes), points] + flux + [points, points]

    sizes_x = (nx, ey, lanes)
    count = wide - 2
    rim_u, old, total, send_a, send_b = call(
        functools.partial(start_kernel, sizes_x), "substep0",
        [(3, 4, tall, lanes), (6, 2, 25, tall, lanes), (3, 5, 4, tall, lanes), (4, 4 * count, lanes), (4, 4 * count, lanes)],
        scratch(tall, False),
        u, v, m, lame, level, rim_a, rim_b, gradient, divergence,
    )
    got_a, got_b = move(True, False, send_a), move(True, True, send_b)

    state = (3, 5, 4, short, lanes)
    message = (3, 4, short, lanes)
    u, v, m, total, send_a, send_b = call(
        functools.partial(second_kernel, sizes_x), "substep1",
        [state, state, state[1:], state, message, message],
        [(2, 4, 4, tall, lanes)] + scratch(tall, True) + [(3, 5, 4, tall, lanes)],
        u, rim_u, v, m, total, got_a, got_b, old, lame, level, gradient, divergence,
    )
    got_a, got_b = move(True, False, send_a), move(True, True, send_b)

    u, v, old, total, send_a, send_b = call(
        functools.partial(later_kernel, sizes_x, False), "substep2",
        [state, state, (6, 2, 25, short, lanes), state, message, message],
        scratch(short, False),
        u, v, m, total, got_a, got_b, old, lame, level, gradient, divergence,
    )
    got_a, got_b = move(True, False, send_a), move(True, True, send_b)

    u, v, total, send_a, send_b = call(
        functools.partial(later_kernel, sizes_x, True), "substep3",
        [state, state, state, (3, 4 * ey, lanes), (3, 4 * ey, lanes)],
        scratch(short, True),
        u, v, m, total, got_a, got_b, old, lame, level, gradient, divergence,
    )
    got_a, got_b = move(True, False, send_a), move(True, True, send_b)

    return tuple(call(
        functools.partial(end_kernel, sizes_x), "end",
        [displacement.shape, velocity.shape], [],
        u, v, m, total, got_a, got_b,
    ))


def solution(mesh):
    sizes = (mesh.shape["px"], mesh.shape["py"])
    in_specs = (
        P(None, "px", "py", None),
        P(None, "px", "py", None),
        P("px", "py", None),
        P(None, None, None, "px", "py"),
        P(None, None, None, "px", "py"),
        P("px", "py"),
    )
    out_specs = (P(None, "px", "py", None), P(None, "px", "py", None))
    return jax.shard_map(
        functools.partial(shards, sizes), mesh=mesh, in_specs=in_specs, out_specs=out_specs, check_vma=False
    )
```

```python
import functools

import jax
import jax.numpy as jnp
import numpy as np
from jax import lax
from jax.experimental import pallas as pl
from jax.experimental.pallas import tpu as pltpu
from jax.sharding import PartitionSpec as P

time_step = 0.1
LEVELS = 3
F32 = jnp.float32
BF16 = jnp.bfloat16


def gll_tables():
    points = np.array([-1.0, -np.sqrt(3.0 / 7.0), 0.0, np.sqrt(3.0 / 7.0), 1.0])
    weights = np.array([0.1, 49.0 / 90.0, 32.0 / 45.0, 49.0 / 90.0, 0.1])
    legendre = (35.0 * points**4 - 30.0 * points**2 + 3.0) / 8.0
    derivative = np.zeros((5, 5))
    for row_index in range(5):
        for col_index in range(5):
            if row_index != col_index:
                derivative[row_index, col_index] = legendre[row_index] / (
                    legendre[col_index] * (points[row_index] - points[col_index])
                )
    derivative[0, 0] = -5.0
    derivative[4, 4] = 5.0
    return (derivative, weights)


D, W = gll_tables()


def split(table):
    high = np.asarray(table, np.float32).astype(BF16)
    low = (np.asarray(table, np.float64) - high.astype(np.float64)).astype(BF16)
    return high, low


def depth_tables(depth):
    lanes = 4 * depth
    table = np.zeros((lanes, 2 * lanes))
    for c in range(depth):
        for i in range(5):
            if 4 * c + i < lanes:
                for k in range(4):
                    table[4 * c + i, 4 * c + k] = D[k, i]
                table[4 * c + i, lanes + (4 * (c + 1)) % lanes] = D[4, i]
    high, low = split(table)
    gradient = np.concatenate([high, high, low], axis=0)
    divergence = np.concatenate([high.T, high.T, low.T], axis=0)
    return gradient, divergence


def weight_table(depth):
    lanes = 4 * depth
    pair = (W[:, None] * W[None, :]).reshape(25, 1)
    main = pair * np.tile(W[:4], depth)[None, :]
    last = pair * np.where(np.arange(lanes) % 4 == 0, W[4], 0.0)[None, :]
    return np.concatenate([main, last], axis=0).astype(np.float32)


def apply5(matrix, x):
    s0, s1 = x[0] + x[4], x[1] + x[3]
    d0, d1 = x[0] - x[4], x[1] - x[3]

    def even(a):
        p, q = (matrix[a, 0] - matrix[a, 4]) / 2, (matrix[a, 1] - matrix[a, 3]) / 2
        return d0 * float(p) + d1 * float(q)

    def odd(a):
        p, q = (matrix[a, 0] + matrix[a, 4]) / 2, (matrix[a, 1] + matrix[a, 3]) / 2
        return s0 * float(p) + s1 * float(q) + x[2] * float(matrix[a, 2])

    e0, e1, e2 = even(0), even(1), even(2)
    o0, o1 = odd(0), odd(1)
    return [e0 + o0, e1 + o1, e2, e1 - o1, e0 - o0]


def apply5_middle(matrix, x):
    s1, d1 = x[0] + x[2], x[0] - x[2]
    e = [d1 * float((matrix[a, 1] - matrix[a, 3]) / 2) for a in range(3)]
    o = [s1 * float((matrix[a, 1] + matrix[a, 3]) / 2) + x[1] * float(matrix[a, 2]) for a in range(2)]
    return [e[0] + o[0], e[1] + o[1], e[2], e[1] - o[1], e[0] - o[0]]


def apply5_ends(matrix, first, last, middle):
    s0, d0 = first + last, first - last
    e = [d0 * float((matrix[a, 0] - matrix[a, 4]) / 2) for a in range(3)]
    o = [s0 * float((matrix[a, 0] + matrix[a, 4]) / 2) for a in range(2)]
    ends = [e[0] + o[0], e[1] + o[1], e[2], e[1] - o[1], e[0] - o[0]]
    return [middle[a] + ends[a] for a in range(5)]


def halves(x):
    high = x.astype(BF16)
    return high, (x - high.astype(F32)).astype(BF16)


def rolled(x, by):
    return pltpu.roll(x, by % x.shape[0], 0)


def swap_pairs(nx, ny, along_x, odd):
    pairs = []
    for i in range(nx):
        for j in range(ny):
            here, size = (i, nx) if along_x else (j, ny)
            there = here + 1 if (here % 2 == 1) == odd else here - 1
            if 0 <= there < size:
                target = (there, j) if along_x else (i, there)
            else:
                target = (i, j ^ 1) if along_x else (i ^ 1, j)
            if target[0] < nx and target[1] < ny:
                pairs.append((i * ny + j, target[0] * ny + target[1]))
    return pairs


def swap(mesh_sizes, along_x, odd, x):
    return lax.ppermute(x, ("px", "py"), swap_pairs(*mesh_sizes, along_x, odd))


def place(axis, size):
    here = lax.axis_index(axis)
    return lax.rem(here, 2) == 0, here == 0, here == size - 1


def load_kernel(count, *refs):
    sources, targets, layer, sems = refs[:count], refs[count : 2 * count], refs[2 * count], refs[2 * count + 1]
    copies = [pltpu.make_async_copy(a, b, sems.at[n]) for n, (a, b) in enumerate(zip(sources, targets))]
    for copy in copies:
        copy.start()
    copies[0].wait()
    across = layer.shape[1]
    for c in range(3):
        layer[c] = targets[0][4 * c * across : (4 * c + 1) * across, :]
    for copy in copies[1:]:
        copy.wait()


def pack_kernel(starts, first_ref, second_ref, level_ref, out):
    for p, table in enumerate((first_ref, second_ref)):
        for row in range(125):
            i, j, k = row // 25, row // 5 % 5, row % 5
            out[starts[p] + row : starts[p] + row + 1, :] = table[i, j, k]
    out[starts[2] : starts[2] + 1, :] = level_ref[...].astype(F32)


def join_kernel(v_ref, m_ref, out):
    count = v_ref.shape[0]
    out[:count, :] = v_ref[...]
    out[count:, :] = m_ref[...]


def sides(ny):
    even, first, last = place("py", ny)

    def left(e, o, at):
        return jnp.where(first, 0.0, jnp.where(even, o[at], e[at]))

    def right(e, o, at):
        return jnp.where(last, 0.0, jnp.where(even, e[at], o[at]))

    return left, right


def rim_kernel(ny, own, e, o, out):
    left, right = sides(ny)
    across = own.shape[1]
    for c in range(3):
        at = (slice(4 * c * across, (4 * c + 1) * across), slice(None))
        out[c, :across, :] = left(e, o, at)
        out[c, across : 2 * across, :] = own[c]
        out[c, 2 * across :, :] = right(e, o, at)


def spread(sizes, own, e, o, base, out):
    ny, ey, lanes = sizes
    left, right = sides(ny)
    for j in range(4):
        at = (pl.ds(base + j, ey, stride=4), slice(None))
        out[j, 0:ey, :] = left(e, o, at)
        out[j, ey : 2 * ey, :] = own[at]
        out[j, 2 * ey : 3 * ey, :] = right(e, o, at)
        out[j, 3 * ey :, :] = jnp.zeros((ey, lanes), F32)


def spread_u_kernel(sizes, own, e, o, ends, inner):
    tall = 4 * sizes[1]
    for c in range(3):
        spread(sizes, own, e, o, 4 * c * tall, ends.at[c])
        for i in range(3):
            spread(sizes, own, e, o, (4 * c + 1 + i) * tall, inner.at[c, i])


def spread_v_kernel(sizes, own_v, own_m, e, o, v_ends, v_inner, m_ends, m_inner):
    tall = 4 * sizes[1]
    base = 12 * tall
    for c in range(3):
        spread(sizes, own_v, e, o, 4 * c * tall, v_ends.at[c])
        for i in range(3):
            spread(sizes, own_v, e, o, (4 * c + 1 + i) * tall, v_inner.at[c, i])
    spread(sizes, own_m, e.at[base:], o.at[base:], 0, m_ends)
    for i in range(3):
        spread(sizes, own_m, e.at[base:], o.at[base:], (1 + i) * tall, m_inner.at[i])


def tables_kernel(sizes, starts, own_ref, e_ref, o_ref, weight_ref, lame_ref, level_ref, sel):
    ny, ey, lanes = sizes
    left, right = sides(ny)
    sel[0] = left(e_ref, o_ref, ...)
    sel[1] = own_ref[...]
    sel[2] = right(e_ref, o_ref, ...)

    shape = (2 * ey, lanes)
    sub = lax.broadcasted_iota(jnp.int32, shape, 0)
    lane = lax.broadcasted_iota(jnp.int32, shape, 1)
    ez = lanes // 4
    column = lax.rem(sub, ey) * ez
    main_at = column + lane // 4
    last_at = column + lax.rem(lane // 4 + ez - 1, ez)
    point = lax.rem(lane, 4)
    upper = sub < ey

    def both(row):
        zero = jnp.zeros(shape, F32)
        a = jnp.broadcast_to(sel[0, pl.ds(row, 1), :], shape)
        b = jnp.broadcast_to(sel[1, pl.ds(row, 1), :], shape)
        c = jnp.broadcast_to(sel[2, pl.ds(row, 1), :], shape)
        return jnp.where(upper, a, b), jnp.where(upper, c, zero)

    def gather(x, at):
        return jnp.take_along_axis(x, at, axis=1, mode="promise_in_bounds")

    for ij in range(25):
        weight = jnp.broadcast_to(weight_ref[ij : ij + 1, :], shape)
        weight_last = jnp.broadcast_to(weight_ref[25 + ij : 26 + ij, :], shape)
        for p in range(2):
            points = [both(starts[p] + ij * 5 + k) for k in range(5)]
            for h in range(2):
                got = [gather(points[k][h], main_at) for k in range(4)]
                main = jnp.where(
                    point < 2, jnp.where(point == 0, got[0], got[1]), jnp.where(point == 2, got[2], got[3])
                )
                lame_ref[p, 0, ij, 2 * ey * h : 2 * ey * (h + 1), :] = main * weight
                lame_ref[p, 1, ij, 2 * ey * h : 2 * ey * (h + 1), :] = gather(points[4][h], last_at) * weight_last
    levels = both(starts[2])
    for h in range(2):
        level_ref[0, 2 * ey * h : 2 * ey * (h + 1), :] = gather(levels[h], main_at)
        level_ref[1, 2 * ey * h : 2 * ey * (h + 1), :] = gather(levels[h], last_at)


def five(values):
    return list(values) + [rolled(values[0], -1)]


def grad_z(points, grad_ref, out):
    count, tall, lanes = points.shape
    high, low = halves(points[...].reshape(count * tall, lanes))
    lhs = jnp.concatenate([high, low, high], axis=1)
    out[...] = jnp.dot(lhs, grad_ref[...], preferred_element_type=F32).reshape(count, tall, 2 * lanes)


def div_z(flux_z, spans, div_ref, out):
    _, _, _, tall, lanes = flux_z.shape
    parts = []
    for e in range(2):
        rows = [flux_z[c, e, at].reshape(-1, lanes) for c in range(3) for at in spans]
        parts.append(halves(jnp.concatenate(rows, axis=0)))
    lhs = jnp.concatenate([parts[0][0], parts[1][0], parts[0][1], parts[1][1], parts[0][0], parts[1][0]], axis=1)
    out[...] = jnp.dot(lhs, div_ref[...], preferred_element_type=F32).reshape(out.shape)


def before(inner, tall, grad_ref, gz, gy, px, us):
    for c in range(3):
        points = [five(inner[c][i]) for i in range(3)]
        for i in range(3):
            for j in range(5):
                us[15 * c + 5 * i + j] = points[i][j]
        for i in range(3):
            y = apply5(D, points[i])
            for j in range(5):
                gy[c, 5 * i + j] = y[j]
        for j in range(5):
            y = apply5_middle(D, [points[i][j] for i in range(3)])
            for i in range(5):
                px[c, 5 * i + j] = y[i]
    grad_z(us, grad_ref, gz)


def stresses(tall, windows, keep, ends, gz, gy, px, lame, level, old, new, flux, flux_z, grad_ref, div_ref, us, gx, gz_ends, qz, total):
    lanes = px.shape[-1]
    points = [[five(ends[c][side]) for side in range(2)] for c in range(3)]
    for c in range(3):
        for side in range(2):
            for j in range(5):
                us[10 * c + 5 * side + j] = points[c][side][j]
    grad_z(us, grad_ref, gz_ends)
    for c in range(3):
        for j in range(5):
            y = apply5_ends(D, points[c][0][j], points[c][1][j], [px[c, 5 * i + j] for i in range(5)])
            for i in range(5):
                gx[c, 5 * i + j] = y[i]
    inner = (lax.broadcasted_iota(jnp.int32, (8, lanes), 1) > 0).astype(F32)
    for h in range(tall // 8):
        at = slice(8 * h, 8 * h + 8)
        table = slice(windows[0] + 8 * h, windows[0] + 8 * h + 8)
        stored = slice(windows[1] + 8 * h, windows[1] + 8 * h + 8)
        if keep is not None:
            fresh = [keep(level[e, table, :]) for e in range(2)]
        for i in (0, 4, 1, 2, 3):
            side = {0: 0, 4: 1}.get(i)
            if side is not None:
                ends_y = [apply5(D, [us[10 * c + 5 * side + j, at, :] for j in range(5)]) for c in range(3)]
            for j in range(5):
                p = 5 * i + j
                grads_x = [gx[c, p, at, :] for c in range(3)]
                if side is None:
                    grads_y = [gy[c, p - 5, at, :] for c in range(3)]
                else:
                    grads_y = [ends_y[c][j] for c in range(3)]
                sums = []
                for e in range(2):
                    span = slice(e * lanes, (e + 1) * lanes)
                    if side is None:
                        grads_z = [gz[15 * c + p - 5, at, span] for c in range(3)]
                    else:
                        grads_z = [gz_ends[10 * c + 5 * side + j, at, span] for c in range(3)]
                    if e == 1:
                        grads_x = [g * inner for g in grads_x]
                        grads_y = [g * inner for g in grads_y]
                    first, second = lame[0, e, p, table, :], lame[1, e, p, table, :]
                    trace = first * (grads_x[0] + grads_y[1] + grads_z[2])
                    twice = second + second
                    stress = [
                        trace + twice * grads_x[0],
                        trace + twice * grads_y[1],
                        second * (grads_y[0] + grads_x[1]),
                        second * (grads_z[0] + grads_x[2]),
                        second * (grads_z[1] + grads_y[2]),
                        trace + twice * grads_z[2],
                    ]
                    if keep is not None:
                        stress = [jnp.where(fresh[e], stress[n], old[n, e, p, stored, :]) for n in range(6)]
                    if new is not None:
                        for n in range(6):
                            new[n, e, p, at, :] = stress[n]
                    else:
                        for n in range(3):
                            flux_z[n, e, p, at, :] = stress[3 + n]
                    if e == 1:
                        stress = [x * inner for x in stress[:5]]
                    sums.append(stress)
                for n in range(5):
                    flux[n, p, at, :] = sums[0][n] + sums[1][n]
    if flux_z is None:
        flux_z = new.at[3:6]
    div_z(flux_z, [slice(0, 5), slice(20, 25)], div_ref, qz)
    assemble((0, 4), flux, qz, lambda c, side, j, value: total.__setitem__((c, side, j), value))


ACROSS_X, ACROSS_Y = (0, 2, 3), (2, 1, 4)


def assemble(layers, flux, qz, put):
    for c in range(3):
        pieces = []
        for j in range(5):
            x = apply5(D.T, [flux[ACROSS_X[c], 5 * i + j] for i in range(5)])
            pieces.append([x[i] for i in layers])
        for n, i in enumerate(layers):
            y = apply5(D.T, [flux[ACROSS_Y[c], 5 * i + j] for j in range(5)])
            z = [pieces[j][n] + (y[j] + qz[c, 5 * n + j]) for j in range(5)]
            put(c, n, 0, z[0] + rolled(z[4], 1))
            for j in range(1, 4):
                put(c, n, j, z[j])


def first_kernel(u_inner, grad_ref, gz, gy, px, us):
    tall = u_inner.shape[3]
    inner = [[[u_inner[c, i, j] for j in range(4)] for i in range(3)] for c in range(3)]
    before(inner, tall, grad_ref, gz, gy, px, us)


def between_kernel(rows, last, flux, flux_z, u_ref, v_ref, m_ref, grad_ref, div_ref, *refs):
    if last:
        u_out, v_out, qz = refs
    else:
        u_out, v_out, m_out, gz, gy, px, qz, us = refs
    if flux_z.shape[0] == 6:
        flux_z = flux_z.at[3:6]
    div_z(flux_z, [slice(5, 20)], div_ref, qz)
    inner = [[[None] * 4 for _ in range(3)] for _ in range(3)]

    def put(c, n, j, force):
        mass = m_ref[n, j, rows, :]
        speed = v_ref[c, n, j, rows, :] - time_step * mass * force[rows]
        position = u_ref[c, n, j, rows, :] + time_step * speed
        if last:
            count = rows.stop - rows.start
            u_out[c, n, pl.ds(j, count, stride=4), :] = position
            v_out[c, n, pl.ds(j, count, stride=4), :] = speed
            return
        u_out[c, n, j], v_out[c, n, j] = position, speed
        if c == 0:
            m_out[n, j] = mass
        inner[c][n][j] = position

    assemble((1, 2, 3), flux, qz, put)
    if not last:
        before(inner, rows.stop - rows.start, grad_ref, gz, gy, px, us)


def start_kernel(sizes, u_ref, v_ref, m_ref, a_ref, b_ref, gz, gy, px, lame, level, grad_ref, div_ref,
                 rim_ref, new, flux, total, send_a, send_b, us, gx, gz_ends, qz):
    nx, ey, lanes = sizes
    even, _, last = place("px", nx)
    tall, wide = 4 * ey, 3 * ey
    for c in range(3):
        for j in range(4):
            at = pl.ds(j, wide, stride=4)
            rim = jnp.where(last, 0.0, jnp.where(even, a_ref[c, at, :], b_ref[c, at, :]))
            rim_ref[c, j, 0:wide, :] = rim
            rim_ref[c, j, wide:, :] = jnp.zeros((tall - wide, lanes), F32)
    ends = [[[u_ref[c, j] for j in range(4)], [rim_ref[c, j] for j in range(4)]] for c in range(3)]
    stresses(tall, (0, 0), None, ends, gz, gy, px, lame, level, None, new, flux, None, grad_ref, div_ref, us, gx, gz_ends, qz, total)
    count = wide - 2
    rows = slice(1, 1 + count)
    for j in range(4):
        at = slice(j * count, (j + 1) * count)
        mass = m_ref[j, rows, :]
        for c in range(3):
            back = v_ref[c, j, rows, :] - time_step * mass * total[c, 0, j, rows, :]
            ahead = total[c, 1, j, rows, :]
            send_a[c, at, :] = jnp.where(even, ahead, back)
            send_b[c, at, :] = jnp.where(even, back, ahead)
        send_a[3, at, :] = mass
        send_b[3, at, :] = mass


def second_kernel(sizes, u_ref, rim_ref, v_ref, m_ref, total_ref, a_ref, b_ref, gz, gy, px, old, lame, level, grad_ref, div_ref,
                  u_out, v_out, m_out, flux, flux_z, total_out, send_a, send_b, got, us, gx, gz_ends, qz, total):
    nx, ey, lanes = sizes
    even, first, last = place("px", nx)
    tall, count = 4 * ey, 3 * ey - 2
    rows = slice(1, 1 + count)
    window = slice(ey - 2, 3 * ey - 2)
    got[...] = jnp.zeros(got.shape, F32)
    for j in range(4):
        at = slice(j * count, (j + 1) * count)
        for c in range(4):
            got[0, c, j, rows, :] = jnp.where(last, 0.0, jnp.where(even, a_ref[c, at, :], b_ref[c, at, :]))
        for c in range(3):
            got[1, c, j, rows, :] = jnp.where(first, 0.0, jnp.where(even, b_ref[c, at, :], a_ref[c, at, :]))
    ends = [[[], []] for _ in range(3)]
    for c in range(3):
        for side in range(2):
            for j in range(4):
                if side == 0:
                    mass, speed, position = m_ref[j], v_ref[c, j], u_ref[c, j]
                    force = total_ref[c, 0, j] + got[1, c, j]
                else:
                    mass, speed, position = got[0, 3, j], got[0, c, j], rim_ref[c, j]
                    force = total_ref[c, 1, j]
                speed = speed - time_step * mass * force
                position = position + time_step * speed
                u_out[c, side, j], v_out[c, side, j] = position[window], speed[window]
                if c == 0:
                    m_out[side, j] = mass[window]
                ends[c][side].append(position)
    stresses(tall, (0, 0), lambda level_of: level_of > 1.5, ends, gz, gy, px, lame, level, old, None, flux, flux_z,
             grad_ref, div_ref, us, gx, gz_ends, qz, total)
    for c in range(3):
        for j in range(4):
            back, ahead = total[c, 0, j, window, :], total[c, 1, j, window, :]
            total_out[c, 0, j], total_out[c, 1, j] = back, ahead
            send_a[c, j] = jnp.where(even, ahead, back)
            send_b[c, j] = jnp.where(even, back, ahead)


def later_kernel(sizes, final, u_ref, v_ref, m_ref, total_ref, a_ref, b_ref, gz, gy, px, old, lame, level, grad_ref, div_ref, *refs):
    nx, ey, lanes = sizes
    u_out, v_out, flux, held, total, send_a, send_b, us, gx, gz_ends, qz = refs
    if final:
        new, flux_z, keep, windows = None, held, lambda level_of: level_of > 1.5, (ey - 2, 0)
    else:
        new, flux_z, keep, windows = held, None, lambda level_of: level_of > 0.5, (ey - 2, ey - 2)
    even, first, last = place("px", nx)
    ends = [[[], []] for _ in range(3)]
    for c in range(3):
        for side in range(2):
            for j in range(4):
                if side == 0:
                    got = jnp.where(first, 0.0, jnp.where(even, b_ref[c, j], a_ref[c, j]))
                else:
                    got = jnp.where(last, 0.0, jnp.where(even, a_ref[c, j], b_ref[c, j]))
                speed = v_ref[c, side, j] - time_step * m_ref[side, j] * (total_ref[c, side, j] + got)
                position = u_ref[c, side, j] + time_step * speed
                u_out[c, side, j], v_out[c, side, j] = position, speed
                ends[c][side].append(position)
    stresses(2 * ey, windows, keep, ends, gz, gy, px, lame, level, old, new, flux, flux_z,
             grad_ref, div_ref, us, gx, gz_ends, qz, total)
    for c in range(3):
        for j in range(4):
            if final:
                at = slice(j * ey, (j + 1) * ey)
                ahead = total[c, 1, j, 2 : 2 + ey, :]
                send_a[c, at, :] = ahead
                send_b[c, at, :] = ahead
            else:
                back, ahead = total[c, 0, j], total[c, 1, j]
                send_a[c, j] = jnp.where(even, ahead, back)
                send_b[c, j] = jnp.where(even, back, ahead)


def end_kernel(sizes, u_ref, v_ref, m_ref, total_ref, a_ref, b_ref, u_inner, v_inner, u_out, v_out):
    nx, ey, lanes = sizes
    even, first, _ = place("px", nx)
    mine = slice(2, 2 + ey)
    for c in range(3):
        for j in range(4):
            at = slice(j * ey, (j + 1) * ey)
            got = jnp.where(first, 0.0, jnp.where(even, b_ref[c, at, :], a_ref[c, at, :]))
            force = total_ref[c, 0, j, mine, :] + got
            speed = v_ref[c, 0, j, mine, :] - time_step * m_ref[0, j, mine, :] * force
            v_out[c, 0, pl.ds(j, ey, stride=4), :] = speed
            u_out[c, 0, pl.ds(j, ey, stride=4), :] = u_ref[c, 0, j, mine, :] + time_step * speed
        for i in range(3):
            u_out[c, 1 + i] = u_inner[c, i]
            v_out[c, 1 + i] = v_inner[c, i]


def call(kernel, name, outs, scratch, *args, cost=None):
    shapes = [jax.ShapeDtypeStruct(s, F32) if name == "end" else pltpu.VMEM(s, F32) for s in outs]
    return pl.pallas_call(
        kernel,
        out_shape=shapes,
        scratch_shapes=[pltpu.VMEM(s, F32) for s in scratch],
        compiler_params=pltpu.CompilerParams(vmem_limit_bytes=32 * 1024 * 1024),
        cost_estimate=cost,
        name=name,
    )(*args)


def shards(sizes, displacement, velocity, inverse_mass, lame_first, lame_second, level_map):
    nx, ny = sizes
    _, ex4, ey4, lanes = displacement.shape
    ey = ey4 // 4
    tall, wide, short = 4 * ey, 3 * ey, 2 * ey
    move = functools.partial(swap, sizes)

    def along_x(a, b):
        return move(True, False, a), move(True, True, b)

    def along_y(x):
        return move(False, False, x), move(False, True, x)

    flat = [x.reshape(-1, lanes) for x in (displacement, velocity, inverse_mass)]
    u_e, u_o = along_y(flat[0])
    gradient, divergence = depth_tables(lanes // 4)
    tables = [jnp.asarray(t) for t in (gradient, divergence, weight_table(lanes // 4))]
    sources = flat + [lame_first, lame_second, level_map] + tables
    own_u, own_v, own_m, first, second, level, gradient, divergence, weights, layer = pl.pallas_call(
        functools.partial(load_kernel, len(sources)),
        out_shape=[pltpu.VMEM(x.shape, x.dtype) for x in sources] + [pltpu.VMEM((3, ey4, lanes), F32)],
        in_specs=[pl.BlockSpec(memory_space=pl.ANY)] * len(sources),
        scratch_shapes=[pltpu.SemaphoreType.DMA((len(sources),))],
        name="load",
    )(*sources)
    starts = (0, 128, 256)
    (own,) = call(functools.partial(pack_kernel, starts), "pack", [(264, lanes)], [], first, second, level)
    from_e, from_o = along_y(own)
    (rim,) = call(functools.partial(rim_kernel, ny), "rim", [(3, 3 * ey4, lanes)], [], layer, u_e, u_o)
    rim_a, rim_b = along_x(rim, rim)
    (joined,) = call(join_kernel, "join", [(own_v.shape[0] + own_m.shape[0], lanes)], [], own_v, own_m)
    v_e, v_o = along_y(joined)

    sizes_y, sizes_x = (ny, ey, lanes), (nx, ey, lanes)

    def shape(*lead, rows=tall):
        return (*lead, rows, lanes)

    def gradients(rows):
        return [(45, rows, 2 * lanes), shape(3, 15, rows=rows), shape(3, 25, rows=rows)]

    def scratch(rows):
        return [shape(30, rows=rows), shape(3, 25, rows=rows), (30, rows, 2 * lanes), shape(3, 10, rows=rows)]

    def fluxes(rows, kinds):
        return [shape(5, 25, rows=rows), shape(kinds, 2, 25, rows=rows)]

    u_ends, u_inner = call(
        functools.partial(spread_u_kernel, sizes_y), "spread_u", [shape(3, 4), shape(3, 3, 4)], [], own_u, u_e, u_o
    )
    near = call(first_kernel, "before0", gradients(tall), [shape(45)], u_inner, gradient)
    lame, level = call(
        functools.partial(tables_kernel, sizes_y, starts), "tables", [shape(2, 2, 25), shape(2)], [(3, 264, lanes)],
        own, from_e, from_o, weights,
    )
    v_ends, v_inner, m_ends, m_inner = call(
        functools.partial(spread_v_kernel, sizes_y), "spread_v",
        [shape(3, 4), shape(3, 3, 4), shape(4), shape(3, 4)], [], own_v, own_m, v_e, v_o,
    )

    count = wide - 2
    rim_u, old, flux, total, send_a, send_b = call(
        functools.partial(start_kernel, sizes_x), "stress0",
        [shape(3, 4), shape(6, 2, 25), shape(5, 25), shape(3, 2, 4), (4, 4 * count, lanes), (4, 4 * count, lanes)],
        scratch(tall),
        u_ends, v_ends, m_ends, rim_a, rim_b, *near, lame, level, gradient, divergence,
    )
    got_a, got_b = along_x(send_a, send_b)
    every, window, mine = slice(0, tall), slice(ey - 2, 3 * ey - 2), slice(2, 2 + ey)
    u_inner, v_inner, m_inner, *near = call(
        functools.partial(between_kernel, every, False), "between0",
        [shape(3, 3, 4), shape(3, 3, 4), shape(3, 4)] + gradients(tall), [shape(3, 15), shape(45)],
        flux, old, u_inner, v_inner, m_inner, gradient, divergence,
    )

    ends = shape(3, 2, 4, rows=short)
    message = shape(3, 4, rows=short)
    u_ends, v_ends, m_ends, flux, flux_z, total, send_a, send_b = call(
        functools.partial(second_kernel, sizes_x), "stress1",
        [ends, ends, ends[1:], *fluxes(tall, 3), ends, message, message],
        [shape(2, 4, 4)] + scratch(tall) + [shape(3, 2, 4)],
        u_ends, rim_u, v_ends, m_ends, total, got_a, got_b, *near, old, lame, level, gradient, divergence,
    )
    got_a, got_b = along_x(send_a, send_b)
    inner = shape(3, 3, 4, rows=short)
    u_inner, v_inner, m_inner, *near = call(
        functools.partial(between_kernel, window, False), "between1",
        [inner, inner, inner[1:]] + gradients(short), [shape(3, 15), shape(45, rows=short)],
        flux, flux_z, u_inner, v_inner, m_inner, gradient, divergence,
    )

    u_ends, v_ends, flux, old, total, send_a, send_b = call(
        functools.partial(later_kernel, sizes_x, False), "stress2",
        [ends, ends, *fluxes(short, 6), ends, message, message], scratch(short),
        u_ends, v_ends, m_ends, total, got_a, got_b, *near, old, lame, level, gradient, divergence,
    )
    got_a, got_b = along_x(send_a, send_b)
    every = slice(0, short)
    u_inner, v_inner, m_inner, *near = call(
        functools.partial(between_kernel, every, False), "between2",
        [inner, inner, inner[1:]] + gradients(short), [shape(3, 15, rows=short), shape(45, rows=short)],
        flux, old, u_inner, v_inner, m_inner, gradient, divergence,
    )

    message = (3, 4 * ey, lanes)
    u_ends, v_ends, flux, flux_z, total, send_a, send_b = call(
        functools.partial(later_kernel, sizes_x, True), "stress3",
        [ends, ends, *fluxes(short, 3), ends, message, message], scratch(short),
        u_ends, v_ends, m_ends, total, got_a, got_b, *near, old, lame, level, gradient, divergence,
    )
    got_a, got_b = along_x(send_a, send_b)
    final = (3, 3, ey4, lanes)
    u_inner, v_inner = call(
        functools.partial(between_kernel, mine, True), "between3", [final, final], [shape(3, 15, rows=short)],
        flux, flux_z, u_inner, v_inner, m_inner, gradient, divergence,
    )

    return tuple(call(
        functools.partial(end_kernel, sizes_x), "end", [displacement.shape, velocity.shape], [],
        u_ends, v_ends, m_ends, total, got_a, got_b, u_inner, v_inner,
    ))


def solution(mesh):
    sizes = (mesh.shape["px"], mesh.shape["py"])
    in_specs = (
        P(None, "px", "py", None),
        P(None, "px", "py", None),
        P("px", "py", None),
        P(None, None, None, "px", "py"),
        P(None, None, None, "px", "py"),
        P("px", "py"),
    )
    out_specs = (P(None, "px", "py", None), P(None, "px", "py", None))
    return jax.shard_map(
        functools.partial(shards, sizes), mesh=mesh, in_specs=in_specs, out_specs=out_specs, check_vma=False
    )
```

```python
import functools

import jax
import jax.numpy as jnp
import numpy as np
from jax import lax
from jax.experimental import pallas as pl
from jax.experimental.pallas import tpu as pltpu
from jax.sharding import PartitionSpec as P

time_step = 0.1
LEVELS = 3
F32 = jnp.float32
BF16 = jnp.bfloat16


def gll_tables():
    points = np.array([-1.0, -np.sqrt(3.0 / 7.0), 0.0, np.sqrt(3.0 / 7.0), 1.0])
    weights = np.array([0.1, 49.0 / 90.0, 32.0 / 45.0, 49.0 / 90.0, 0.1])
    legendre = (35.0 * points**4 - 30.0 * points**2 + 3.0) / 8.0
    derivative = np.zeros((5, 5))
    for row_index in range(5):
        for col_index in range(5):
            if row_index != col_index:
                derivative[row_index, col_index] = legendre[row_index] / (
                    legendre[col_index] * (points[row_index] - points[col_index])
                )
    derivative[0, 0] = -5.0
    derivative[4, 4] = 5.0
    return (derivative, weights)


D, W = gll_tables()


def split(table):
    high = np.asarray(table, np.float32).astype(BF16)
    low = (np.asarray(table, np.float64) - high.astype(np.float64)).astype(BF16)
    return high, low


def depth_tables(depth):
    lanes = 4 * depth
    table = np.zeros((lanes, 2 * lanes))
    for c in range(depth):
        for i in range(5):
            if 4 * c + i < lanes:
                for k in range(4):
                    table[4 * c + i, 4 * c + k] = D[k, i]
                table[4 * c + i, lanes + (4 * (c + 1)) % lanes] = D[4, i]
    high, low = split(table)
    gradient = np.concatenate([high, high, low], axis=0)
    divergence = np.concatenate([high.T, high.T, low.T], axis=0)
    return gradient, divergence


def weight_table(depth):
    lanes = 4 * depth
    pair = (W[:, None] * W[None, :]).reshape(25, 1)
    main = pair * np.tile(W[:4], depth)[None, :]
    last = pair * np.where(np.arange(lanes) % 4 == 0, W[4], 0.0)[None, :]
    return np.concatenate([main, last], axis=0).astype(np.float32)


def apply5(matrix, x):
    s0, s1 = x[0] + x[4], x[1] + x[3]
    d0, d1 = x[0] - x[4], x[1] - x[3]

    def even(a):
        p, q = (matrix[a, 0] - matrix[a, 4]) / 2, (matrix[a, 1] - matrix[a, 3]) / 2
        return d0 * float(p) + d1 * float(q)

    def odd(a):
        p, q = (matrix[a, 0] + matrix[a, 4]) / 2, (matrix[a, 1] + matrix[a, 3]) / 2
        return s0 * float(p) + s1 * float(q) + x[2] * float(matrix[a, 2])

    e0, e1, e2 = even(0), even(1), even(2)
    o0, o1 = odd(0), odd(1)
    return [e0 + o0, e1 + o1, e2, e1 - o1, e0 - o0]


def apply5_middle(matrix, x):
    s1, d1 = x[0] + x[2], x[0] - x[2]
    e = [d1 * float((matrix[a, 1] - matrix[a, 3]) / 2) for a in range(3)]
    o = [s1 * float((matrix[a, 1] + matrix[a, 3]) / 2) + x[1] * float(matrix[a, 2]) for a in range(2)]
    return [e[0] + o[0], e[1] + o[1], e[2], e[1] - o[1], e[0] - o[0]]


def apply5_ends(matrix, first, last, middle):
    s0, d0 = first + last, first - last
    e = [d0 * float((matrix[a, 0] - matrix[a, 4]) / 2) for a in range(3)]
    o = [s0 * float((matrix[a, 0] + matrix[a, 4]) / 2) for a in range(2)]
    ends = [e[0] + o[0], e[1] + o[1], e[2], e[1] - o[1], e[0] - o[0]]
    return [middle[a] + ends[a] for a in range(5)]


def halves(x):
    high = x.astype(BF16)
    return high, (x - high.astype(F32)).astype(BF16)


def rolled(x, by):
    return pltpu.roll(x, by % x.shape[0], 0)


def pairs_of(kind, nx, ny):
    pairs = []
    for i in range(nx):
        for j in range(ny):
            if kind == "core":
                target = (i, j ^ 1)
            elif kind == "near":
                target = (i ^ 1, j ^ 1)
            elif kind == "home":
                target = (i ^ 1, j)
            elif kind == "far":
                there = i + 1 if i % 2 else i - 1
                target = (there if 0 <= there < nx else i, j ^ 1)
            elif i % 2:
                there = j + 2 if j % 2 else j - 2
                target = (i, there if 0 <= there < ny else j ^ 1)
            else:
                there = j + 1 if j % 2 else j - 1
                target = (i, there) if 0 <= there < ny else (i ^ 2, j) if nx % 4 == 0 else (i, ny - 1 - j)
            pairs.append((i * ny + j, target[0] * ny + target[1]))
    return pairs


def place(axis, size):
    here = lax.axis_index(axis)
    return lax.rem(here, 2) == 0, here == 0, here == size - 1


def load_kernel(count, *refs):
    sources, targets, sems = refs[:count], refs[count : 2 * count], refs[2 * count]
    copies = [pltpu.make_async_copy(a, b, sems.at[n]) for n, (a, b) in enumerate(zip(sources, targets))]
    for copy in copies:
        copy.start()
    for copy in copies:
        copy.wait()


def pack_kernel(starts, v_ref, m_ref, first_ref, second_ref, level_ref, out):
    out[0 : v_ref.shape[0], :] = v_ref[...]
    out[starts[0] : starts[0] + m_ref.shape[0], :] = m_ref[...]
    for p, table in enumerate((first_ref, second_ref)):
        for row in range(125):
            i, j, k = row // 25, row // 5 % 5, row % 5
            out[starts[1 + p] + row : starts[1 + p] + row + 1, :] = table[i, j, k]
    out[starts[3] : starts[3] + 1, :] = level_ref[...].astype(F32)


def sides(ny):
    here = lax.axis_index("py")
    changed = lax.rem(lax.axis_index("px"), 2) == 1
    even = (lax.rem(here, 2) == 0) != changed
    first = jnp.logical_and(here < 2, even)
    last = jnp.logical_and(here >= ny - 2, jnp.logical_not(even))

    def centre(own, core, chip, at):
        return jnp.where(changed, core[at], own[at])

    def other(own, core, at):
        return jnp.where(changed, own[at], core[at])

    def left(own, core, chip, at):
        return jnp.where(first, 0.0, jnp.where(even, chip[at], other(own, core, at)))

    def right(own, core, chip, at):
        return jnp.where(last, 0.0, jnp.where(even, other(own, core, at), chip[at]))

    return left, centre, right


def rim_kernel(ny, across, own, core, chip, out):
    ahead = across - 3
    for c in range(3):
        base = c * (2 * across + ahead)
        for n, (side, count) in enumerate(zip(sides(ny), (across, across, ahead))):
            at = (slice(4 * c * across, 4 * c * across + count), slice(None))
            out[base + n * across : base + n * across + count, :] = side(own, core, chip, at)


def spread(sizes, own, core, chip, base, out):
    ny, ey, lanes = sizes
    for j in range(4):
        at = (pl.ds(base + j, ey, stride=4), slice(None))
        for n, side in enumerate(sides(ny)):
            out[j, n * ey : (n + 1) * ey, :] = side(own, core, chip, at)
        out[j, 3 * ey :, :] = jnp.zeros((ey, lanes), F32)


def segments(low, high):
    found, offset = [], 0
    for j in range(4):
        stop = high + (j == 0)
        found.append((offset, slice(low, stop)))
        offset += stop - low
    return found, offset


def message_rows(low, high, fields):
    return -(-segments(low, high)[1] * fields // 8) * 8


def write_message(ref, low, high, field, rows_of):
    found, total = segments(low, high)
    for j, (offset, rows) in enumerate(found):
        start = field * total + offset
        ref[start : start + rows.stop - rows.start, :] = rows_of(j, rows)


def read_message(out, low, high, field, one_ref, other_ref, even, none):
    found, total = segments(low, high)
    for j, (offset, rows) in enumerate(found):
        at = (slice(field * total + offset, field * total + offset + rows.stop - rows.start), slice(None))
        out[j, rows, :] = jnp.where(none, 0.0, jnp.where(even, one_ref[at], other_ref[at]))


def spread_u_kernel(sizes, own, e, o, ends, inner):
    tall = 4 * sizes[1]
    for c in range(3):
        spread(sizes, own, e, o, 4 * c * tall, ends.at[c])
        for i in range(3):
            spread(sizes, own, e, o, (4 * c + 1 + i) * tall, inner.at[c, i])


def spread_v_kernel(sizes, start, own, e, o, v_ends, v_inner, m_ends, m_inner):
    tall = 4 * sizes[1]
    for c in range(3):
        spread(sizes, own, e, o, 4 * c * tall, v_ends.at[c])
        for i in range(3):
            spread(sizes, own, e, o, (4 * c + 1 + i) * tall, v_inner.at[c, i])
    spread(sizes, own, e, o, start, m_ends)
    for i in range(3):
        spread(sizes, own, e, o, start + (1 + i) * tall, m_inner.at[i])


def tables_kernel(sizes, starts, own_ref, e_ref, o_ref, weight_ref, lame_ref, level_ref, sel):
    ny, ey, lanes = sizes
    for n, side in enumerate(sides(ny)):
        sel[n] = side(own_ref, e_ref, o_ref, (slice(starts[1], own_ref.shape[0]), slice(None)))

    shape = (2 * ey, lanes)
    sub = lax.broadcasted_iota(jnp.int32, shape, 0)
    lane = lax.broadcasted_iota(jnp.int32, shape, 1)
    ez = lanes // 4
    column = lax.rem(sub, ey) * ez
    main_at = column + lane // 4
    last_at = column + lax.rem(lane // 4 + ez - 1, ez)
    point = lax.rem(lane, 4)
    upper = sub < ey

    def both(row):
        zero = jnp.zeros(shape, F32)
        a = jnp.broadcast_to(sel[0, pl.ds(row, 1), :], shape)
        b = jnp.broadcast_to(sel[1, pl.ds(row, 1), :], shape)
        c = jnp.broadcast_to(sel[2, pl.ds(row, 1), :], shape)
        return jnp.where(upper, a, b), jnp.where(upper, c, zero)

    def gather(x, at):
        return jnp.take_along_axis(x, at, axis=1, mode="promise_in_bounds")

    for ij in range(25):
        weight = jnp.broadcast_to(weight_ref[ij : ij + 1, :], shape)
        weight_last = jnp.broadcast_to(weight_ref[25 + ij : 26 + ij, :], shape)
        for p in range(2):
            points = [both(starts[1 + p] - starts[1] + ij * 5 + k) for k in range(5)]
            for h in range(2):
                got = [gather(points[k][h], main_at) for k in range(4)]
                main = jnp.where(
                    point < 2, jnp.where(point == 0, got[0], got[1]), jnp.where(point == 2, got[2], got[3])
                )
                lame_ref[p, 0, ij, 2 * ey * h : 2 * ey * (h + 1), :] = main * weight
                lame_ref[p, 1, ij, 2 * ey * h : 2 * ey * (h + 1), :] = gather(points[4][h], last_at) * weight_last
    levels = both(starts[3] - starts[1])
    for h in range(2):
        level_ref[0, 2 * ey * h : 2 * ey * (h + 1), :] = gather(levels[h], main_at)
        level_ref[1, 2 * ey * h : 2 * ey * (h + 1), :] = gather(levels[h], last_at)


def five(values):
    return list(values) + [rolled(values[0], -1)]


def grad_z(points, grad_ref, out):
    count, tall, lanes = points.shape
    high, low = halves(points[...].reshape(count * tall, lanes))
    lhs = jnp.concatenate([high, low, high], axis=1)
    out[...] = jnp.dot(lhs, grad_ref[...], preferred_element_type=F32).reshape(count, tall, 2 * lanes)


def div_z(flux_z, div_ref, out):
    _, _, count, tall, lanes = flux_z.shape
    parts = [halves(flux_z[:, e].reshape(3 * count * tall, lanes)) for e in range(2)]
    lhs = jnp.concatenate([parts[0][0], parts[1][0], parts[0][1], parts[1][1], parts[0][0], parts[1][0]], axis=1)
    out[...] = jnp.dot(lhs, div_ref[...], preferred_element_type=F32).reshape(out.shape)


def inside(lanes):
    return (lax.broadcasted_iota(jnp.int32, (8, lanes), 1) > 0).astype(F32)


def stress_of(first, second, x, y, z):
    trace = first * (x[0] + y[1] + z[2])
    twice = second + second
    return [
        trace + twice * x[0],
        trace + twice * y[1],
        second * (y[0] + x[1]),
        second * (z[0] + x[2]),
        second * (z[1] + y[2]),
        trace + twice * z[2],
    ]


def before(inner, tall, window, keep, lame, level, old, old_window, grad_ref, gz, gy, px, part, scale, us):
    lanes = gy.shape[-1]
    for c in range(3):
        points = [five(inner[c][i]) for i in range(3)]
        for i in range(3):
            for j in range(5):
                us[15 * c + 5 * i + j] = points[i][j]
        for i in range(3):
            y = apply5(D, points[i])
            for j in range(5):
                gy[c, 5 * i + j] = y[j]
        for j in range(5):
            y = apply5_middle(D, [points[i][j] for i in range(3)])
            for i in range(5):
                px[c, 5 * i + j] = y[i]
    grad_z(us, grad_ref, gz)
    mask = inside(lanes)
    for h in range(tall // 8):
        at = slice(8 * h, 8 * h + 8)
        table = slice(window + 8 * h, window + 8 * h + 8)
        stored = slice(old_window + 8 * h, old_window + 8 * h + 8)
        if keep is not None:
            fresh = [keep(level[e, table, :]) for e in range(2)]
        for p in range(15):
            y = [gy[c, p, at, :] for c in range(3)]
            sums = []
            for e in range(2):
                span = slice(e * lanes, (e + 1) * lanes)
                z0, z2 = gz[p, at, span], gz[30 + p, at, span]
                first, second = lame[0, e, 5 + p, table, :], lame[1, e, 5 + p, table, :]
                parts = [first * (y[1] + z2), second * y[0], second * z0]
                scales = [first + (second + second), second]
                if keep is not None:
                    parts = [jnp.where(fresh[e], parts[n], old[(0, 2, 3)[n], e, p, stored, :]) for n in range(3)]
                    scales = [jnp.where(fresh[e], x, 0.0) for x in scales]
                both = parts + scales
                sums.append([x * mask for x in both] if e == 1 else both)
            for n in range(3):
                part[n, p, at, :] = sums[0][n] + sums[1][n]
            for n in range(2):
                scale[n, p, at, :] = sums[0][3 + n] + sums[1][3 + n]


def stresses(tall, windows, keep, ends, px, part, scale, lame, level, old, new, flux_x, gx, flux_z, flux_y, us, gz_ends, qz, grad_ref, div_ref, total):
    lanes = px.shape[-1]
    points = [[five(ends[c][side]) for side in range(2)] for c in range(3)]
    for c in range(3):
        for side in range(2):
            for j in range(5):
                us[10 * c + 5 * side + j] = points[c][side][j]
    grad_z(us, grad_ref, gz_ends)
    for c in range(3):
        for j in range(5):
            y = apply5_ends(D, points[c][0][j], points[c][1][j], [px[c, 5 * i + j] for i in range(5)])
            for i in range(5):
                gx[c, 5 * i + j] = y[i]
                if 0 < i < 4:
                    flux_x[c, 5 * i + j] = scale[min(c, 1), 5 * i + j - 5] * y[i] + part[c, 5 * i + j - 5]
    mask = inside(lanes)
    for h in range(tall // 8):
        at = slice(8 * h, 8 * h + 8)
        table = slice(windows[0] + 8 * h, windows[0] + 8 * h + 8)
        stored = slice(windows[1] + 8 * h, windows[1] + 8 * h + 8)
        if keep is not None:
            fresh = [keep(level[e, table, :]) for e in range(2)]
        for side in range(2):
            ends_y = [apply5(D, [us[10 * c + 5 * side + j, at, :] for j in range(5)]) for c in range(3)]
            for j in range(5):
                p, q = 20 * side + j, 5 * side + j
                x = [gx[c, p, at, :] for c in range(3)]
                y = [ends_y[c][j] for c in range(3)]
                sums = []
                for e in range(2):
                    span = slice(e * lanes, (e + 1) * lanes)
                    z = [gz_ends[10 * c + q, at, span] for c in range(3)]
                    if e == 1:
                        x, y = [g * mask for g in x], [g * mask for g in y]
                    stress = stress_of(lame[0, e, p, table, :], lame[1, e, p, table, :], x, y, z)
                    if keep is not None:
                        stress = [jnp.where(fresh[e], stress[n], old[n, e, q, stored, :]) for n in range(6)]
                    if new is not None:
                        for n in range(6):
                            new[n, e, q, at, :] = stress[n]
                    else:
                        for n in range(3):
                            flux_z[n, e, q, at, :] = stress[3 + n]
                    sums.append([v * mask for v in stress[:5]] if e == 1 else stress[:5])
                xx, yy, xy, xz, yz = [sums[0][n] + sums[1][n] for n in range(5)]
                for c in range(3):
                    flux_x[c, p, at, :] = (xx, xy, xz)[c]
                    flux_y[c, q, at, :] = (xy, yy, yz)[c]
    if new is not None:
        flux_z = new.at[3:6]
    div_z(flux_z, div_ref, qz)
    assemble((0, 4), flux_x, flux_y, qz, lambda c, side, j, value: total.__setitem__((c, side, j), value))


def assemble(layers, flux_x, flux_y, qz, put):
    for c in range(3):
        pieces = []
        for j in range(5):
            x = apply5(D.T, [flux_x[c, 5 * i + j] for i in range(5)])
            pieces.append([x[i] for i in layers])
        for n in range(len(layers)):
            y = apply5(D.T, [flux_y[c, 5 * n + j] for j in range(5)])
            z = [pieces[j][n] + (y[j] + qz[c, 5 * n + j]) for j in range(5)]
            put(c, n, 0, z[0] + rolled(z[4], 1))
            for j in range(1, 4):
                put(c, n, j, z[j])


def first_kernel(u_inner, lame, grad_ref, gz, gy, px, part, scale, us):
    tall = u_inner.shape[3]
    inner = [[[u_inner[c, i, j] for j in range(4)] for i in range(3)] for c in range(3)]
    before(inner, tall, 0, None, lame, None, None, 0, grad_ref, gz, gy, px, part, scale, us)


def between_kernel(rows, last, keep, windows, stores, keep_next, windows_next, flux_x, gx, gz, gy, u_ref, v_ref, m_ref, old,
                   lame, level, grad_ref, div_ref, *refs):
    refs = list(refs)
    new = None
    if last:
        u_ends, v_ends, m_ends, total, send = refs[:5]
        count = rows.stop - rows.start
        for j in range(4):
            mass = m_ends[0, j, rows, :]
            send[pl.ds(final_rows(count, 4, 0) + j, count, stride=4), :] = mass
            for c in range(3):
                speed = v_ends[c, 0, j, rows, :] - time_step * mass * total[c, 0, j, rows, :]
                send[pl.ds(final_rows(count, 2, c) + j, count, stride=4), :] = u_ends[c, 0, j, rows, :]
                send[pl.ds(final_rows(count, 3, c) + j, count, stride=4), :] = speed
    else:
        u_out, v_out = refs[:2]
        m_out, gz_out, gy_out, px_out, part, scale = refs[2:8]
    if stores:
        new = refs[8]
    flux_y, flux_z, qz = refs[-4:-1] if not last else refs[-3:]
    us = None if last else refs[-1]
    _, _, tall, lanes = gx.shape
    mask = inside(lanes)
    for h in range(tall // 8):
        at = slice(8 * h, 8 * h + 8)
        table = slice(windows[0] + 8 * h, windows[0] + 8 * h + 8)
        stored = slice(windows[1] + 8 * h, windows[1] + 8 * h + 8)
        if keep is not None:
            fresh = [keep(level[e, table, :]) for e in range(2)]
        for p in range(15):
            x = [gx[c, 5 + p, at, :] for c in range(3)]
            y = [gy[c, p, at, :] for c in range(3)]
            sums = []
            for e in range(2):
                z = [gz[15 * c + p, at, e * lanes : (e + 1) * lanes] for c in range(3)]
                if e == 1:
                    x, y = [g * mask for g in x], [g * mask for g in y]
                stress = stress_of(lame[0, e, 5 + p, table, :], lame[1, e, 5 + p, table, :], x, y, z)
                if keep is not None:
                    stress = [jnp.where(fresh[e], stress[n], old[n, e, p, stored, :]) for n in range(6)]
                if stores:
                    for n in range(6):
                        new[n, e, p, at, :] = stress[n]
                else:
                    for n in range(3):
                        flux_z[n, e, p, at, :] = stress[3 + n]
                sums.append([v * mask for v in stress[:5]] if e == 1 else stress[:5])
            for c, n in enumerate((2, 1, 4)):
                flux_y[c, p, at, :] = sums[0][n] + sums[1][n]
    div_z(new.at[3:6] if stores else flux_z, div_ref, qz)
    inner = [[[None] * 4 for _ in range(3)] for _ in range(3)]

    def put(c, n, j, force):
        mass = m_ref[n, j, rows, :]
        speed = v_ref[c, n, j, rows, :] - time_step * mass * force[rows]
        position = u_ref[c, n, j, rows, :] + time_step * speed
        if last:
            send[pl.ds(final_rows(count, 0, c, n) + j, count, stride=4), :] = position
            send[pl.ds(final_rows(count, 1, c, n) + j, count, stride=4), :] = speed
            return
        u_out[c, n, j], v_out[c, n, j] = position, speed
        if c == 0:
            m_out[n, j] = mass
        inner[c][n][j] = position

    assemble((1, 2, 3), flux_x, flux_y, qz, put)
    if not last:
        before(inner, rows.stop - rows.start, windows_next[0], keep_next, lame, level, new if stores else old, windows_next[1],
               grad_ref, gz_out, gy_out, px_out, part, scale, us)


def newest(level_of):
    return level_of > LEVELS - 1.5


def newer(level_of):
    return level_of > LEVELS - 2.5


def start_kernel(sizes, u_ref, v_ref, m_ref, a_ref, b_ref, px, part, scale, lame, level, grad_ref, div_ref,
                 rim_ref, new, flux_x, gx, total, send_a, send_b, flux_y, us, gz_ends, qz):
    nx, ey, lanes = sizes
    even, _, last = place("px", nx)
    tall = 4 * ey
    rim_ref[...] = jnp.zeros(rim_ref.shape, F32)
    for c in range(3):
        for j in range(4):
            count = 3 * ey - (j > 0)
            at = (pl.ds(c * (12 * ey - 3) + j, count, stride=4), slice(None))
            rim_ref[c, j, 0:count, :] = jnp.where(last, 0.0, jnp.where(even, a_ref[at], b_ref[at]))
    ends = [[[u_ref[c, j] for j in range(4)], [rim_ref[c, j] for j in range(4)]] for c in range(3)]
    stresses(tall, (0, 0), None, ends, px, part, scale, lame, level, None, new, flux_x, gx, None, flux_y, us, gz_ends, qz,
             grad_ref, div_ref, total)
    low, high = 1, 3 * ey - 2
    for c in range(3):

        def back(j, rows):
            return v_ref[c, j, rows, :] - time_step * m_ref[j, rows, :] * total[c, 0, j, rows, :]

        def ahead(j, rows):
            return total[c, 1, j, rows, :]

        write_message(send_a, low, high, c, lambda j, rows: jnp.where(even, ahead(j, rows), back(j, rows)))
        write_message(send_b, low, high, c, lambda j, rows: jnp.where(even, back(j, rows), ahead(j, rows)))
    for send in (send_a, send_b):
        write_message(send, low, high, 3, lambda j, rows: m_ref[j, rows, :])


def second_kernel(sizes, u_ref, rim_ref, v_ref, m_ref, total_ref, a_ref, b_ref, px, part, scale, old, lame, level, grad_ref, div_ref,
                  u_out, v_out, m_out, flux_x, gx, total_out, send_a, send_b, got, flux_z, total, flux_y, us, gz_ends, qz):
    nx, ey, lanes = sizes
    even, first, last = place("px", nx)
    tall = 4 * ey
    window = slice(ey - 2, 3 * ey - 2)
    got[...] = jnp.zeros(got.shape, F32)
    for c in range(4):
        read_message(got.at[0, c], 1, 3 * ey - 2, c, a_ref, b_ref, even, last)
    for c in range(3):
        read_message(got.at[1, c], 1, 3 * ey - 2, c, b_ref, a_ref, even, first)
    ends = [[[], []] for _ in range(3)]
    for c in range(3):
        for side in range(2):
            for j in range(4):
                if side == 0:
                    mass, speed, position = m_ref[j], v_ref[c, j], u_ref[c, j]
                    force = total_ref[c, 0, j] + got[1, c, j]
                else:
                    mass, speed, position = got[0, 3, j], got[0, c, j], rim_ref[c, j]
                    force = total_ref[c, 1, j]
                speed = speed - time_step * mass * force
                position = position + time_step * speed
                u_out[c, side, j], v_out[c, side, j] = position[window], speed[window]
                if c == 0:
                    m_out[side, j] = mass[window]
                ends[c][side].append(position)
    stresses(tall, (0, 0), newest, ends, px, part, scale, lame, level, old, None, flux_x, gx, flux_z, flux_y, us, gz_ends, qz,
             grad_ref, div_ref, total)
    for c in range(3):
        for side in range(2):
            for j in range(4):
                total_out[c, side, j] = total[c, side, j, window, :]
    send_faces(even, total_out, 0, 2 * ey - 1, send_a, send_b)


def send_faces(even, total, low, high, send_a, send_b):
    for c in range(3):

        def back(j, rows):
            return total[c, 0, j, rows, :]

        def ahead(j, rows):
            return total[c, 1, j, rows, :]

        write_message(send_a, low, high, c, lambda j, rows: jnp.where(even, ahead(j, rows), back(j, rows)))
        write_message(send_b, low, high, c, lambda j, rows: jnp.where(even, back(j, rows), ahead(j, rows)))


def later_kernel(sizes, final, u_ref, v_ref, m_ref, total_ref, a_ref, b_ref, px, part, scale, old, lame, level, grad_ref, div_ref, *refs):
    nx, ey, lanes = sizes
    if final:
        u_out, v_out, flux_x, gx, total, send_a, send_b, got, flux_z, flux_y, us, gz_ends, qz = refs
        new, keep, windows, low, high = None, newest, (ey - 2, 0), 1, 2 + ey
    else:
        u_out, v_out, new, flux_x, gx, total, send_a, send_b, got, flux_y, us, gz_ends, qz = refs
        flux_z, keep, windows, low, high = None, newer, (ey - 2, ey - 2), 0, 2 * ey - 1
    even, first, last = place("px", nx)
    got[...] = jnp.zeros(got.shape, F32)
    for c in range(3):
        read_message(got.at[1, c], low, high, c, a_ref, b_ref, even, last)
        read_message(got.at[0, c], low, high, c, b_ref, a_ref, even, first)
    ends = [[[], []] for _ in range(3)]
    for c in range(3):
        for side in range(2):
            for j in range(4):
                speed = v_ref[c, side, j] - time_step * m_ref[side, j] * (total_ref[c, side, j] + got[side, c, j])
                position = u_ref[c, side, j] + time_step * speed
                u_out[c, side, j], v_out[c, side, j] = position, speed
                ends[c][side].append(position)
    stresses(2 * ey, windows, keep, ends, px, part, scale, lame, level, old, new, flux_x, gx, flux_z, flux_y, us, gz_ends, qz,
             grad_ref, div_ref, total)
    if not final:
        send_faces(even, total, 1, 2 + ey, send_a, send_b)
        return
    for c in range(3):
        for j in range(4):
            at = slice((4 * c + j) * ey, (4 * c + j + 1) * ey)
            ahead = total[c, 1, j, 2 : 2 + ey, :]
            send_a[at, :] = ahead
            send_b[at, :] = ahead


def final_rows(ey, field, c, i=0):
    across = 4 * ey
    if field < 2:
        return (9 * field + 3 * c + i) * across
    return (18 + 3 * (field - 2) + c) * across


def pick_kernel(nx, a_ref, b_ref, out):
    even, first, _ = place("px", nx)
    out[...] = jnp.where(first, 0.0, jnp.where(even, b_ref[...], a_ref[...]))


def end_kernel(sizes, mine, core, force_ref, u_out, v_out):
    nx, ey, lanes = sizes
    even, _, _ = place("px", nx)

    def at(start, j=None):
        rows = (slice(start, start + 4 * ey) if j is None else pl.ds(start + j, ey, stride=4), slice(None))
        return jnp.where(even, mine[rows], core[rows])

    for c in range(3):
        for j in range(4):
            rows = (slice((4 * c + j) * ey, (4 * c + j + 1) * ey), slice(None))
            mass = at(final_rows(ey, 4, 0), j)
            speed = at(final_rows(ey, 3, c), j) - time_step * mass * force_ref[rows]
            v_out[c, 0, pl.ds(j, ey, stride=4), :] = speed
            u_out[c, 0, pl.ds(j, ey, stride=4), :] = at(final_rows(ey, 2, c), j) + time_step * speed
        for i in range(3):
            u_out[c, 1 + i] = at(final_rows(ey, 0, c, i))
            v_out[c, 1 + i] = at(final_rows(ey, 1, c, i))


def call(kernel, name, outs, scratch, *args, cost=None):
    shapes = [jax.ShapeDtypeStruct(s, F32) if name == "end" else pltpu.VMEM(s, F32) for s in outs]
    return pl.pallas_call(
        kernel,
        out_shape=shapes,
        scratch_shapes=[pltpu.VMEM(s, F32) for s in scratch],
        compiler_params=pltpu.CompilerParams(vmem_limit_bytes=32 * 1024 * 1024),
        cost_estimate=cost,
        name=name,
    )(*args)


def shards(sizes, displacement, velocity, inverse_mass, lame_first, lame_second, level_map):
    nx, ny = sizes
    _, ex4, ey4, lanes = displacement.shape
    ey = ey4 // 4
    tall, wide, short = 4 * ey, 3 * ey, 2 * ey

    def move(kind, x):
        return lax.ppermute(x, ("px", "py"), pairs_of(kind, nx, ny))

    def along_x(a, b):
        return move("near", a), move("far", b)

    def along_y(x):
        return move("core", x), move("across", x)

    flat = [x.reshape(-1, lanes) for x in (displacement, velocity, inverse_mass)]
    u_e, u_o = along_y(flat[0])
    gradient, divergence = depth_tables(lanes // 4)
    tables = [jnp.asarray(t) for t in (gradient, divergence, weight_table(lanes // 4))]
    sources = flat + [lame_first, lame_second, level_map] + tables
    own_u, own_v, own_m, first, second, level, gradient, divergence, weights = pl.pallas_call(
        functools.partial(load_kernel, len(sources)),
        out_shape=[pltpu.VMEM(x.shape, x.dtype) for x in sources],
        in_specs=[pl.BlockSpec(memory_space=pl.ANY)] * len(sources),
        scratch_shapes=[pltpu.SemaphoreType.DMA((len(sources),))],
        name="load",
    )(*sources)
    long = pl.CostEstimate(flops=20_000_000_000, bytes_accessed=0, transcendentals=0)
    starts = [int(n) for n in np.cumsum([own_v.shape[0], own_m.shape[0], 128, 128])]
    (own,) = call(functools.partial(pack_kernel, starts), "pack", [(starts[3] + 8, lanes)], [], own_v, own_m, first, second, level)
    from_e, from_o = along_y(own)
    (rim,) = call(functools.partial(rim_kernel, ny, ey4), "rim", [(-(-3 * (3 * ey4 - 3) // 8) * 8, lanes)], [], own_u, u_e, u_o, cost=long)
    rim_a, rim_b = along_x(rim, rim)
    sizes_y, sizes_x = (ny, ey, lanes), (nx, ey, lanes)

    def shape(*lead, rows=tall):
        return (*lead, rows, lanes)

    def near_shapes(rows):
        points = functools.partial(shape, rows=rows)
        return [(45, rows, 2 * lanes), points(3, 15), points(3, 25), points(3, 15), points(2, 15)]

    def ends_scratch(rows):
        points = functools.partial(shape, rows=rows)
        return [points(3, 10), points(30), (30, rows, 2 * lanes), points(3, 10)]

    def between_scratch(rows, rows_next):
        points = functools.partial(shape, rows=rows)
        return [points(3, 15), points(3, 2, 15), points(3, 15)] + ([shape(45, rows=rows_next)] if rows_next else [])

    u_ends, u_inner = call(
        functools.partial(spread_u_kernel, sizes_y), "spread_u", [shape(3, 4), shape(3, 3, 4)], [], own_u, u_e, u_o
    )
    lame, level = call(
        functools.partial(tables_kernel, sizes_y, starts), "tables", [shape(2, 2, 25), shape(2)], [(3, 264, lanes)],
        own, from_e, from_o, weights,
    )
    gz, gy, *near = call(first_kernel, "before0", near_shapes(tall), [shape(45)], u_inner, lame, gradient)
    v_ends, v_inner, m_ends, m_inner = call(
        functools.partial(spread_v_kernel, sizes_y, starts[0]), "spread_v",
        [shape(3, 4), shape(3, 3, 4), shape(4), shape(3, 4)], [], own, from_e, from_o,
    )

    tables = (lame, level, gradient, divergence)
    message = (message_rows(1, 3 * ey - 2, 4), lanes)
    rim_u, old_ends, flux_x, gx, total, send_a, send_b = call(
        functools.partial(start_kernel, sizes_x), "stress0",
        [shape(3, 4), shape(6, 2, 10), shape(3, 25), shape(3, 25), shape(3, 2, 4), message, message],
        ends_scratch(tall),
        u_ends, v_ends, m_ends, rim_a, rim_b, *near, *tables,
    )
    got_a, got_b = along_x(send_a, send_b)
    every, window, mine = slice(0, tall), slice(ey - 2, 3 * ey - 2), slice(2, 2 + ey)
    *state, old_inner = call(
        functools.partial(between_kernel, every, False, None, (0, 0), True, newest, (0, 0)), "between0",
        [shape(3, 3, 4), shape(3, 3, 4), shape(3, 4)] + near_shapes(tall) + [shape(6, 2, 15)], between_scratch(tall, tall),
        flux_x, gx, gz, gy, u_inner, v_inner, m_inner, level, *tables,
    )
    u_inner, v_inner, m_inner, gz, gy, *near = state

    ends = shape(3, 2, 4, rows=short)
    message = (message_rows(0, 2 * ey - 1, 3), lanes)
    u_ends, v_ends, m_ends, flux_x, gx, total, send_a, send_b = call(
        functools.partial(second_kernel, sizes_x), "stress1",
        [ends, ends, ends[1:], shape(3, 25), shape(3, 25), ends, message, message],
        [shape(2, 4, 4), shape(3, 2, 10), shape(3, 2, 4)] + ends_scratch(tall),
        u_ends, rim_u, v_ends, m_ends, total, got_a, got_b, *near, old_ends, *tables,
    )
    got_a, got_b = along_x(send_a, send_b)
    inner = shape(3, 3, 4, rows=short)
    u_inner, v_inner, m_inner, gz, gy, *near = call(
        functools.partial(between_kernel, window, False, newest, (0, 0), False, newer, (ey - 2, ey - 2)), "between1",
        [inner, inner, inner[1:]] + near_shapes(short), between_scratch(tall, short),
        flux_x, gx, gz, gy, u_inner, v_inner, m_inner, old_inner, *tables,
    )

    points, got = shape(3, 25, rows=short), shape(2, 3, 4, rows=short)
    message = (message_rows(1, 2 + ey, 3), lanes)
    u_ends, v_ends, old_ends, flux_x, gx, total, send_a, send_b = call(
        functools.partial(later_kernel, sizes_x, False), "stress2",
        [ends, ends, shape(6, 2, 10, rows=short), points, points, ends, message, message], [got] + ends_scratch(short),
        u_ends, v_ends, m_ends, total, got_a, got_b, *near, old_ends, *tables,
    )
    got_a, got_b = along_x(send_a, send_b)
    every = slice(0, short)
    *state, old_inner = call(
        functools.partial(between_kernel, every, False, newer, (ey - 2, ey - 2), True, newest, (ey - 2, 0)), "between2",
        [inner, inner, inner[1:]] + near_shapes(short) + [shape(6, 2, 15, rows=short)], between_scratch(short, short),
        flux_x, gx, gz, gy, u_inner, v_inner, m_inner, old_inner, *tables,
    )
    u_inner, v_inner, m_inner, gz, gy, *near = state

    message = (12 * ey, lanes)
    u_ends, v_ends, flux_x, gx, total, send_a, send_b = call(
        functools.partial(later_kernel, sizes_x, True), "stress3",
        [ends, ends, points, points, ends, message, message], [got, shape(3, 2, 10, rows=short)] + ends_scratch(short),
        u_ends, v_ends, m_ends, total, got_a, got_b, *near, old_ends, *tables,
    )
    got_a, got_b = move("home", send_a), move("far", send_b)
    (results,) = call(
        functools.partial(between_kernel, mine, True, newest, (ey - 2, 0), False, None, None), "between3",
        [(25 * ey4, lanes)], between_scratch(short, 0),
        flux_x, gx, gz, gy, u_inner, v_inner, m_inner, old_inner, *tables, u_ends, v_ends, m_ends, total,
    )
    (force,) = call(functools.partial(pick_kernel, nx), "pick", [message], [], got_a, got_b, cost=long)
    return tuple(call(
        functools.partial(end_kernel, sizes_x), "end", [displacement.shape, velocity.shape], [],
        results, move("core", results), force,
    ))


def solution(mesh):
    sizes = (mesh.shape["px"], mesh.shape["py"])
    in_specs = (
        P(None, "px", "py", None),
        P(None, "px", "py", None),
        P("px", "py", None),
        P(None, None, None, "px", "py"),
        P(None, None, None, "px", "py"),
        P("px", "py"),
    )
    out_specs = (P(None, "px", "py", None), P(None, "px", "py", None))
    return jax.shard_map(
        functools.partial(shards, sizes), mesh=mesh, in_specs=in_specs, out_specs=out_specs, check_vma=False
    )
```

```python
import functools

import jax
import jax.numpy as jnp
import numpy as np
from jax import lax
from jax.experimental import pallas as pl
from jax.experimental.pallas import tpu as pltpu
from jax.sharding import PartitionSpec as P

time_step = 0.1
LEVELS = 3
F32 = jnp.float32
BF16 = jnp.bfloat16


def gll_tables():
    points = np.array([-1.0, -np.sqrt(3.0 / 7.0), 0.0, np.sqrt(3.0 / 7.0), 1.0])
    weights = np.array([0.1, 49.0 / 90.0, 32.0 / 45.0, 49.0 / 90.0, 0.1])
    legendre = (35.0 * points**4 - 30.0 * points**2 + 3.0) / 8.0
    derivative = np.zeros((5, 5))
    for row_index in range(5):
        for col_index in range(5):
            if row_index != col_index:
                derivative[row_index, col_index] = legendre[row_index] / (
                    legendre[col_index] * (points[row_index] - points[col_index])
                )
    derivative[0, 0] = -5.0
    derivative[4, 4] = 5.0
    return (derivative, weights)


D, W = gll_tables()


def split(table):
    high = np.asarray(table, np.float32).astype(BF16)
    low = (np.asarray(table, np.float64) - high.astype(np.float64)).astype(BF16)
    return high, low


def depth_tables(depth):
    lanes = 4 * depth
    table = np.zeros((lanes, 2 * lanes))
    for c in range(depth):
        for i in range(5):
            if 4 * c + i < lanes:
                for k in range(4):
                    table[4 * c + i, 4 * c + k] = D[k, i]
                table[4 * c + i, lanes + (4 * (c + 1)) % lanes] = D[4, i]
    high, low = split(table)
    gradient = np.concatenate([high, high, low], axis=0)
    divergence = np.concatenate([high.T, low.T], axis=1)
    return gradient, divergence


def weight_table(depth):
    lanes = 4 * depth
    pair = (W[:, None] * W[None, :]).reshape(25, 1)
    main = pair * np.tile(W[:4], depth)[None, :]
    last = pair * np.where(np.arange(lanes) % 4 == 0, W[4], 0.0)[None, :]
    return np.concatenate([main, last], axis=0).astype(np.float32)


def apply5(matrix, x):
    s0, s1 = x[0] + x[4], x[1] + x[3]
    d0, d1 = x[0] - x[4], x[1] - x[3]

    def even(a):
        p, q = (matrix[a, 0] - matrix[a, 4]) / 2, (matrix[a, 1] - matrix[a, 3]) / 2
        return d0 * float(p) + d1 * float(q)

    def odd(a):
        p, q = (matrix[a, 0] + matrix[a, 4]) / 2, (matrix[a, 1] + matrix[a, 3]) / 2
        return s0 * float(p) + s1 * float(q) + x[2] * float(matrix[a, 2])

    e0, e1, e2 = even(0), even(1), even(2)
    o0, o1 = odd(0), odd(1)
    return [e0 + o0, e1 + o1, e2, e1 - o1, e0 - o0]


def apply5_middle(matrix, x):
    s1, d1 = x[0] + x[2], x[0] - x[2]
    e = [d1 * float((matrix[a, 1] - matrix[a, 3]) / 2) for a in range(3)]
    o = [s1 * float((matrix[a, 1] + matrix[a, 3]) / 2) + x[1] * float(matrix[a, 2]) for a in range(2)]
    return [e[0] + o[0], e[1] + o[1], e[2], e[1] - o[1], e[0] - o[0]]


def apply5_ends(matrix, first, last, middle):
    s0, d0 = first + last, first - last
    e = [d0 * float((matrix[a, 0] - matrix[a, 4]) / 2) for a in range(3)]
    o = [s0 * float((matrix[a, 0] + matrix[a, 4]) / 2) for a in range(2)]
    ends = [e[0] + o[0], e[1] + o[1], e[2], e[1] - o[1], e[0] - o[0]]
    return [middle[a] + ends[a] for a in range(5)]


def halves(x):
    high = x.astype(BF16)
    return high, (x - high.astype(F32)).astype(BF16)


def rolled(x, by):
    return pltpu.roll(x, by % x.shape[0], 0)


def pairs_of(kind, nx, ny):
    pairs = []
    for i in range(nx):
        for j in range(ny):
            if kind == "core":
                target = (i, j ^ 1)
            elif kind == "near":
                target = (i ^ 1, j ^ 1)
            elif kind == "home":
                target = (i ^ 1, j)
            elif kind == "far":
                there = i + 1 if i % 2 else i - 1
                target = (there if 0 <= there < nx else i, j ^ 1)
            elif i % 2:
                there = j + 2 if j % 2 else j - 2
                target = (i, there if 0 <= there < ny else j ^ 1)
            else:
                there = j + 1 if j % 2 else j - 1
                target = (i, there) if 0 <= there < ny else (i ^ 2, j) if nx % 4 == 0 else (i, ny - 1 - j)
            pairs.append((i * ny + j, target[0] * ny + target[1]))
    return pairs


def place(axis, size):
    here = lax.axis_index(axis)
    return lax.rem(here, 2) == 0, here == 0, here == size - 1


def load_kernel(count, *refs):
    sources, targets, sems = refs[:count], refs[count : 2 * count], refs[2 * count]
    copies = [pltpu.make_async_copy(a, b, sems.at[n]) for n, (a, b) in enumerate(zip(sources, targets))]
    for copy in copies:
        copy.start()
    for copy in copies:
        copy.wait()


def copy_kernel(x_ref, out):
    out[...] = x_ref[...]


def pack_kernel(starts, v_ref, m_ref, first_ref, second_ref, level_ref, out):
    out[0 : v_ref.shape[0], :] = v_ref[...]
    out[starts[0] : starts[0] + m_ref.shape[0], :] = m_ref[...]
    for p, table in enumerate((first_ref, second_ref)):
        for row in range(125):
            i, j, k = row // 25, row // 5 % 5, row % 5
            out[starts[1 + p] + row : starts[1 + p] + row + 1, :] = table[i, j, k]
    out[starts[3] : starts[3] + 1, :] = level_ref[...].astype(F32)


def sides(ny):
    here = lax.axis_index("py")
    changed = lax.rem(lax.axis_index("px"), 2) == 1
    even = (lax.rem(here, 2) == 0) != changed
    first = jnp.logical_and(here < 2, even)
    last = jnp.logical_and(here >= ny - 2, jnp.logical_not(even))

    def centre(own, core, chip, at):
        return jnp.where(changed, core[at], own[at])

    def other(own, core, at):
        return jnp.where(changed, own[at], core[at])

    def left(own, core, chip, at):
        return jnp.where(first, 0.0, jnp.where(even, chip[at], other(own, core, at)))

    def right(own, core, chip, at):
        return jnp.where(last, 0.0, jnp.where(even, other(own, core, at), chip[at]))

    return left, centre, right


def rim_kernel(ny, across, own, core, chip, out):
    ahead = across - 3
    for c in range(3):
        base = c * (2 * across + ahead)
        for n, (side, count) in enumerate(zip(sides(ny), (across, across, ahead))):
            at = (slice(4 * c * across, 4 * c * across + count), slice(None))
            out[base + n * across : base + n * across + count, :] = side(own, core, chip, at)


def spread(sizes, own, core, chip, base, out):
    ny, ey, lanes = sizes
    for j in range(4):
        at = (pl.ds(base + j, ey, stride=4), slice(None))
        for n, side in enumerate(sides(ny)):
            out[j, n * ey : (n + 1) * ey, :] = side(own, core, chip, at)
        out[j, 3 * ey :, :] = jnp.zeros((ey, lanes), F32)


def segments(low, high):
    found, offset = [], 0
    for j in range(4):
        stop = high + (j == 0)
        found.append((offset, slice(low, stop)))
        offset += stop - low
    return found, offset


def message_rows(low, high, fields):
    return -(-segments(low, high)[1] * fields // 8) * 8


def write_message(ref, low, high, field, rows_of):
    found, total = segments(low, high)
    for j, (offset, rows) in enumerate(found):
        start = field * total + offset
        ref[start : start + rows.stop - rows.start, :] = rows_of(j, rows)


def read_message(out, low, high, field, one_ref, other_ref, even, none):
    found, total = segments(low, high)
    for j, (offset, rows) in enumerate(found):
        at = (slice(field * total + offset, field * total + offset + rows.stop - rows.start), slice(None))
        out[j, rows, :] = jnp.where(none, 0.0, jnp.where(even, one_ref[at], other_ref[at]))


def spread_u_kernel(sizes, own, e, o, ends, inner):
    tall = 4 * sizes[1]
    for c in range(3):
        spread(sizes, own, e, o, 4 * c * tall, ends.at[c])
        for i in range(3):
            spread(sizes, own, e, o, (4 * c + 1 + i) * tall, inner.at[c, i])


def spread_v_kernel(sizes, start, own, e, o, v_ends, v_inner, m_ends, m_inner):
    tall = 4 * sizes[1]
    for c in range(3):
        spread(sizes, own, e, o, 4 * c * tall, v_ends.at[c])
        for i in range(3):
            spread(sizes, own, e, o, (4 * c + 1 + i) * tall, v_inner.at[c, i])
    spread(sizes, own, e, o, start, m_ends)
    for i in range(3):
        spread(sizes, own, e, o, start + (1 + i) * tall, m_inner.at[i])


def tables_kernel(sizes, starts, own_ref, e_ref, o_ref, weight_ref, lame_ref, level_ref, sel):
    ny, ey, lanes = sizes
    for n, side in enumerate(sides(ny)):
        sel[n] = side(own_ref, e_ref, o_ref, (slice(starts[1], own_ref.shape[0]), slice(None)))

    shape = (2 * ey, lanes)
    sub = lax.broadcasted_iota(jnp.int32, shape, 0)
    lane = lax.broadcasted_iota(jnp.int32, shape, 1)
    ez = lanes // 4
    column = lax.rem(sub, ey) * ez
    main_at = column + lane // 4
    last_at = column + lax.rem(lane // 4 + ez - 1, ez)
    point = lax.rem(lane, 4)
    upper = sub < ey

    def both(row):
        zero = jnp.zeros(shape, F32)
        a = jnp.broadcast_to(sel[0, pl.ds(row, 1), :], shape)
        b = jnp.broadcast_to(sel[1, pl.ds(row, 1), :], shape)
        c = jnp.broadcast_to(sel[2, pl.ds(row, 1), :], shape)
        return jnp.where(upper, a, b), jnp.where(upper, c, zero)

    def gather(x, at):
        return jnp.take_along_axis(x, at, axis=1, mode="promise_in_bounds")

    for ij in range(25):
        weight = jnp.broadcast_to(weight_ref[ij : ij + 1, :], shape)
        weight_last = jnp.broadcast_to(weight_ref[25 + ij : 26 + ij, :], shape)
        for p in range(2):
            points = [both(starts[1 + p] - starts[1] + ij * 5 + k) for k in range(5)]
            for h in range(2):
                got = [gather(points[k][h], main_at) for k in range(4)]
                main = jnp.where(
                    point < 2, jnp.where(point == 0, got[0], got[1]), jnp.where(point == 2, got[2], got[3])
                )
                lame_ref[p, 0, ij, 2 * ey * h : 2 * ey * (h + 1), :] = main * weight
                lame_ref[p, 1, ij, 2 * ey * h : 2 * ey * (h + 1), :] = gather(points[4][h], last_at) * weight_last
    levels = both(starts[3] - starts[1])
    for h in range(2):
        level_ref[0, 2 * ey * h : 2 * ey * (h + 1), :] = gather(levels[h], main_at)
        level_ref[1, 2 * ey * h : 2 * ey * (h + 1), :] = gather(levels[h], last_at)


def five(values):
    return list(values) + [rolled(values[0], -1)]


def grad_z(points, grad_ref, out):
    count, tall, lanes = points.shape
    high, low = halves(points[...].reshape(count * tall, lanes))
    lhs = jnp.concatenate([high, low, high], axis=1)
    out[...] = jnp.dot(lhs, grad_ref[...], preferred_element_type=F32).reshape(count, tall, 2 * lanes)


def div_z(main, point, div_ref):
    lanes = main.shape[-1]
    (main_high, main_low), (point_high, point_low) = halves(main), halves(point)
    high = jnp.dot(jnp.concatenate([main_high, point_high], axis=1), div_ref[...], preferred_element_type=F32)
    low = jnp.concatenate([main_low, point_low], axis=1)
    return high[:, :lanes] + (high[:, lanes:] + jnp.dot(low, div_ref[:, :lanes], preferred_element_type=F32))


def inside(lanes):
    return (lax.broadcasted_iota(jnp.int32, (8, lanes), 1) > 0).astype(F32)


def stress_of(first, second, x, y, z):
    trace = first * (x[0] + y[1] + z[2])
    twice = second + second
    return [
        trace + twice * x[0],
        trace + twice * y[1],
        second * (y[0] + x[1]),
        second * (z[0] + x[2]),
        second * (z[1] + y[2]),
        trace + twice * z[2],
    ]


def before(inner, tall, window, keep, lame, level, old, old_window, grad_ref, gz, gy, px, part, scale, us):
    lanes = gy.shape[-1]
    for c in range(3):
        points = [five(inner[c][i]) for i in range(3)]
        for i in range(3):
            for j in range(5):
                us[15 * c + 5 * i + j] = points[i][j]
        for i in range(3):
            y = apply5(D, points[i])
            for j in range(5):
                gy[c, 5 * i + j] = y[j]
        for j in range(5):
            y = apply5_middle(D, [points[i][j] for i in range(3)])
            for i in range(5):
                px[c, 5 * i + j] = y[i]
    grad_z(us, grad_ref, gz)
    mask = inside(lanes)
    for h in range(tall // 8):
        at = slice(8 * h, 8 * h + 8)
        table = slice(window + 8 * h, window + 8 * h + 8)
        stored = slice(old_window + 8 * h, old_window + 8 * h + 8)
        if keep is not None:
            fresh = [keep(level[e, table, :]) for e in range(2)]
        for p in range(15):
            y = [gy[c, p, at, :] for c in range(3)]
            sums = []
            for e in range(2):
                span = slice(e * lanes, (e + 1) * lanes)
                z0, z2 = gz[p, at, span], gz[30 + p, at, span]
                first, second = lame[0, e, 5 + p, table, :], lame[1, e, 5 + p, table, :]
                parts = [first * (y[1] + z2), second * y[0], second * z0]
                scales = [first + (second + second), second]
                if keep is not None:
                    parts = [jnp.where(fresh[e], parts[n], old[(0, 2, 3)[n], e, p, stored, :]) for n in range(3)]
                    scales = [jnp.where(fresh[e], x, 0.0) for x in scales]
                both = parts + scales
                sums.append([x * mask for x in both] if e == 1 else both)
            for n in range(3):
                part[n, p, at, :] = sums[0][n] + sums[1][n]
            for n in range(2):
                scale[n, p, at, :] = sums[0][3 + n] + sums[1][3 + n]


def stresses(tall, windows, keep, ends, px, part, scale, lame, level, old, new, flux_x, gx, flux_z, flux_y, us, gz_ends, last_z, qz, grad_ref, div_ref, total):
    lanes = px.shape[-1]
    points = [[five(ends[c][side]) for side in range(2)] for c in range(3)]
    for c in range(3):
        for side in range(2):
            for j in range(4):
                us[8 * c + 4 * side + j] = points[c][side][j]
    grad_z(us, grad_ref, gz_ends)
    for n in range(6):
        last_z[n] = rolled(gz_ends[4 * n], -1)
    for c in range(3):
        for j in range(5):
            y = apply5_ends(D, points[c][0][j], points[c][1][j], [px[c, 5 * i + j] for i in range(5)])
            for i in range(5):
                gx[c, 5 * i + j] = y[i]
                if 0 < i < 4:
                    flux_x[c, 5 * i + j] = scale[min(c, 1), 5 * i + j - 5] * y[i] + part[c, 5 * i + j - 5]
    mask = inside(lanes)
    for h in range(tall // 8):
        at = slice(8 * h, 8 * h + 8)
        table = slice(windows[0] + 8 * h, windows[0] + 8 * h + 8)
        stored = slice(windows[1] + 8 * h, windows[1] + 8 * h + 8)
        if keep is not None:
            fresh = [keep(level[e, table, :]) for e in range(2)]
        for side in range(2):
            ends_y = [apply5(D, [points[c][side][j][at] for j in range(5)]) for c in range(3)]
            for j in range(5):
                p, q = 20 * side + j, 5 * side + j
                x = [gx[c, p, at, :] for c in range(3)]
                y = [ends_y[c][j] for c in range(3)]
                sums = []
                for e in range(2):
                    span = slice(e * lanes, (e + 1) * lanes)
                    if j < 4:
                        z = [gz_ends[8 * c + 4 * side + j, at, span] for c in range(3)]
                    else:
                        z = [last_z[2 * c + side, at, span] for c in range(3)]
                    if e == 1:
                        x, y = [g * mask for g in x], [g * mask for g in y]
                    stress = stress_of(lame[0, e, p, table, :], lame[1, e, p, table, :], x, y, z)
                    if keep is not None:
                        stress = [jnp.where(fresh[e], stress[n], old[n, e, q, stored, :]) for n in range(6)]
                    if new is not None:
                        for n in range(6):
                            new[n, e, q, at, :] = stress[n]
                    for n in range(3):
                        flux_z[n, e, q, at, :] = stress[3 + n]
                    sums.append([v * mask for v in stress[:5]] if e == 1 else stress[:5])
                xx, yy, xy, xz, yz = [sums[0][n] + sums[1][n] for n in range(5)]
                for c in range(3):
                    flux_x[c, p, at, :] = (xx, xy, xz)[c]
                    flux_y[c, q, at, :] = (xy, yy, yz)[c]
    parts = []
    for e in range(2):
        rows = []
        for c in range(3):
            for side in range(2):
                first = 5 * side
                rows.append(flux_z[c, e, first] + rolled(flux_z[c, e, first + 4], 1))
                rows.append(flux_z[c, e, first + 1 : first + 4].reshape(3 * tall, lanes))
        parts.append(jnp.concatenate(rows, axis=0))
    qz[...] = div_z(*parts, div_ref).reshape(qz.shape)
    assemble((0, 4), flux_x, flux_y, qz, lambda c, side, j, value: total.__setitem__((c, side, j), value))


def assemble(layers, flux_x, flux_y, qz, put):
    count = qz.shape[1] // len(layers)
    for c in range(3):
        pieces = []
        for j in range(5):
            x = apply5(D.T, [flux_x[c, 5 * i + j] for i in range(5)])
            pieces.append([x[i] for i in layers])
        for n in range(len(layers)):
            y = apply5(D.T, [flux_y[c, 5 * n + j] for j in range(5)])
            z = [pieces[j][n] + (y[j] + qz[c, count * n + j] if j < count else y[j]) for j in range(5)]
            put(c, n, 0, z[0] + rolled(z[4], 1))
            for j in range(1, 4):
                put(c, n, j, z[j])


def first_kernel(u_inner, lame, grad_ref, gz, gy, px, part, scale, us):
    tall = u_inner.shape[3]
    inner = [[[u_inner[c, i, j] for j in range(4)] for i in range(3)] for c in range(3)]
    before(inner, tall, 0, None, lame, None, None, 0, grad_ref, gz, gy, px, part, scale, us)


def between_kernel(rows, last, keep, windows, stores, keep_next, windows_next, flux_x, gx, gz, gy, u_ref, v_ref, m_ref, old,
                   lame, level, grad_ref, div_ref, *refs):
    refs = list(refs)
    new = None
    if last:
        u_ends, v_ends, m_ends, total, send = refs[:5]
        count = rows.stop - rows.start
        for j in range(4):
            mass = m_ends[0, j, rows, :]
            send[pl.ds(final_rows(count, 4, 0) + j, count, stride=4), :] = mass
            for c in range(3):
                speed = v_ends[c, 0, j, rows, :] - time_step * mass * total[c, 0, j, rows, :]
                send[pl.ds(final_rows(count, 2, c) + j, count, stride=4), :] = u_ends[c, 0, j, rows, :]
                send[pl.ds(final_rows(count, 3, c) + j, count, stride=4), :] = speed
    else:
        u_out, v_out = refs[:2]
        m_out, gz_out, gy_out, px_out, part, scale = refs[2:8]
    if stores:
        new = refs[8]
    flux_y, flux_z, qz = refs[-4:-1] if not last else refs[-3:]
    us = None if last else refs[-1]
    _, _, tall, lanes = gx.shape
    mask = inside(lanes)
    for h in range(tall // 8):
        at = slice(8 * h, 8 * h + 8)
        table = slice(windows[0] + 8 * h, windows[0] + 8 * h + 8)
        stored = slice(windows[1] + 8 * h, windows[1] + 8 * h + 8)
        if keep is not None:
            fresh = [keep(level[e, table, :]) for e in range(2)]
        for p in range(15):
            x = [gx[c, 5 + p, at, :] for c in range(3)]
            y = [gy[c, p, at, :] for c in range(3)]
            sums = []
            for e in range(2):
                z = [gz[15 * c + p, at, e * lanes : (e + 1) * lanes] for c in range(3)]
                if e == 1:
                    x, y = [g * mask for g in x], [g * mask for g in y]
                stress = stress_of(lame[0, e, 5 + p, table, :], lame[1, e, 5 + p, table, :], x, y, z)
                if keep is not None:
                    stress = [jnp.where(fresh[e], stress[n], old[n, e, p, stored, :]) for n in range(6)]
                if stores:
                    for n in range(6):
                        new[n, e, p, at, :] = stress[n]
                else:
                    for n in range(3):
                        flux_z[n, e, p, at, :] = stress[3 + n]
                sums.append([v * mask for v in stress[:5]] if e == 1 else stress[:5])
            for c, n in enumerate((2, 1, 4)):
                flux_y[c, p, at, :] = sums[0][n] + sums[1][n]
    if stores:
        flux_z = new.at[3:6]
    qz[...] = div_z(*(flux_z[:, e].reshape(45 * tall, lanes) for e in range(2)), div_ref).reshape(qz.shape)
    inner = [[[None] * 4 for _ in range(3)] for _ in range(3)]

    def put(c, n, j, force):
        mass = m_ref[n, j, rows, :]
        speed = v_ref[c, n, j, rows, :] - time_step * mass * force[rows]
        position = u_ref[c, n, j, rows, :] + time_step * speed
        if last:
            send[pl.ds(final_rows(count, 0, c, n) + j, count, stride=4), :] = position
            send[pl.ds(final_rows(count, 1, c, n) + j, count, stride=4), :] = speed
            return
        u_out[c, n, j], v_out[c, n, j] = position, speed
        if c == 0:
            m_out[n, j] = mass
        inner[c][n][j] = position

    assemble((1, 2, 3), flux_x, flux_y, qz, put)
    if not last:
        before(inner, rows.stop - rows.start, windows_next[0], keep_next, lame, level, new if stores else old, windows_next[1],
               grad_ref, gz_out, gy_out, px_out, part, scale, us)


def newest(level_of):
    return level_of > LEVELS - 1.5


def newer(level_of):
    return level_of > LEVELS - 2.5


def start_kernel(sizes, u_ref, v_ref, m_ref, a_ref, b_ref, px, part, scale, lame, level, grad_ref, div_ref,
                 rim_ref, new, flux_x, gx, total, send_a, send_b, flux_z, flux_y, us, gz_ends, last_z, qz):
    nx, ey, lanes = sizes
    even, _, last = place("px", nx)
    tall = 4 * ey
    rim_ref[...] = jnp.zeros(rim_ref.shape, F32)
    for c in range(3):
        for j in range(4):
            count = 3 * ey - (j > 0)
            at = (pl.ds(c * (12 * ey - 3) + j, count, stride=4), slice(None))
            rim_ref[c, j, 0:count, :] = jnp.where(last, 0.0, jnp.where(even, a_ref[at], b_ref[at]))
    ends = [[[u_ref[c, j] for j in range(4)], [rim_ref[c, j] for j in range(4)]] for c in range(3)]
    stresses(tall, (0, 0), None, ends, px, part, scale, lame, level, None, new, flux_x, gx, flux_z, flux_y, us, gz_ends, last_z, qz,
             grad_ref, div_ref, total)
    low, high = 1, 3 * ey - 2
    for c in range(3):

        def back(j, rows):
            return v_ref[c, j, rows, :] - time_step * m_ref[j, rows, :] * total[c, 0, j, rows, :]

        def ahead(j, rows):
            return total[c, 1, j, rows, :]

        write_message(send_a, low, high, c, lambda j, rows: jnp.where(even, ahead(j, rows), back(j, rows)))
        write_message(send_b, low, high, c, lambda j, rows: jnp.where(even, back(j, rows), ahead(j, rows)))
    for send in (send_a, send_b):
        write_message(send, low, high, 3, lambda j, rows: m_ref[j, rows, :])


def second_kernel(sizes, u_ref, rim_ref, v_ref, m_ref, total_ref, a_ref, b_ref, px, part, scale, old, lame, level, grad_ref, div_ref,
                  u_out, v_out, m_out, flux_x, gx, total_out, send_a, send_b, got, total, flux_z, flux_y, us, gz_ends, last_z, qz):
    nx, ey, lanes = sizes
    even, first, last = place("px", nx)
    tall = 4 * ey
    window = slice(ey - 2, 3 * ey - 2)
    got[...] = jnp.zeros(got.shape, F32)
    for c in range(4):
        read_message(got.at[0, c], 1, 3 * ey - 2, c, a_ref, b_ref, even, last)
    for c in range(3):
        read_message(got.at[1, c], 1, 3 * ey - 2, c, b_ref, a_ref, even, first)
    ends = [[[], []] for _ in range(3)]
    for c in range(3):
        for side in range(2):
            for j in range(4):
                if side == 0:
                    mass, speed, position = m_ref[j], v_ref[c, j], u_ref[c, j]
                    force = total_ref[c, 0, j] + got[1, c, j]
                else:
                    mass, speed, position = got[0, 3, j], got[0, c, j], rim_ref[c, j]
                    force = total_ref[c, 1, j]
                speed = speed - time_step * mass * force
                position = position + time_step * speed
                u_out[c, side, j], v_out[c, side, j] = position[window], speed[window]
                if c == 0:
                    m_out[side, j] = mass[window]
                ends[c][side].append(position)
    stresses(tall, (0, 0), newest, ends, px, part, scale, lame, level, old, None, flux_x, gx, flux_z, flux_y, us, gz_ends, last_z, qz,
             grad_ref, div_ref, total)
    for c in range(3):
        for side in range(2):
            for j in range(4):
                total_out[c, side, j] = total[c, side, j, window, :]
    send_faces(even, total_out, 0, 2 * ey - 1, send_a, send_b)


def send_faces(even, total, low, high, send_a, send_b):
    for c in range(3):

        def back(j, rows):
            return total[c, 0, j, rows, :]

        def ahead(j, rows):
            return total[c, 1, j, rows, :]

        write_message(send_a, low, high, c, lambda j, rows: jnp.where(even, ahead(j, rows), back(j, rows)))
        write_message(send_b, low, high, c, lambda j, rows: jnp.where(even, back(j, rows), ahead(j, rows)))


def later_kernel(sizes, final, u_ref, v_ref, m_ref, total_ref, a_ref, b_ref, px, part, scale, old, lame, level, grad_ref, div_ref, *refs):
    nx, ey, lanes = sizes
    if final:
        u_out, v_out, flux_x, gx, total, send_a, send_b, got, flux_z, flux_y, us, gz_ends, last_z, qz = refs
        new, keep, windows, low, high = None, newest, (ey - 2, 0), 1, 2 + ey
    else:
        u_out, v_out, new, flux_x, gx, total, send_a, send_b, got, flux_z, flux_y, us, gz_ends, last_z, qz = refs
        keep, windows, low, high = newer, (ey - 2, ey - 2), 0, 2 * ey - 1
    even, first, last = place("px", nx)
    got[...] = jnp.zeros(got.shape, F32)
    for c in range(3):
        read_message(got.at[1, c], low, high, c, a_ref, b_ref, even, last)
        read_message(got.at[0, c], low, high, c, b_ref, a_ref, even, first)
    ends = [[[], []] for _ in range(3)]
    for c in range(3):
        for side in range(2):
            for j in range(4):
                speed = v_ref[c, side, j] - time_step * m_ref[side, j] * (total_ref[c, side, j] + got[side, c, j])
                position = u_ref[c, side, j] + time_step * speed
                u_out[c, side, j], v_out[c, side, j] = position, speed
                ends[c][side].append(position)
    stresses(2 * ey, windows, keep, ends, px, part, scale, lame, level, old, new, flux_x, gx, flux_z, flux_y, us, gz_ends, last_z, qz,
             grad_ref, div_ref, total)
    if not final:
        send_faces(even, total, 1, 2 + ey, send_a, send_b)
        return
    for c in range(3):
        for j in range(4):
            at = slice((4 * c + j) * ey, (4 * c + j + 1) * ey)
            ahead = total[c, 1, j, 2 : 2 + ey, :]
            send_a[at, :] = ahead
            send_b[at, :] = ahead


def final_rows(ey, field, c, i=0):
    across = 4 * ey
    if field < 2:
        return (9 * field + 3 * c + i) * across
    return (18 + 3 * (field - 2) + c) * across


def pick_kernel(nx, a_ref, b_ref, out):
    even, first, _ = place("px", nx)
    out[...] = jnp.where(first, 0.0, jnp.where(even, b_ref[...], a_ref[...]))


def end_kernel(sizes, mine, core, force_ref, u_out, v_out):
    nx, ey, lanes = sizes
    even, _, _ = place("px", nx)

    def at(start, j=None):
        rows = (slice(start, start + 4 * ey) if j is None else pl.ds(start + j, ey, stride=4), slice(None))
        return jnp.where(even, mine[rows], core[rows])

    for c in range(3):
        for j in range(4):
            rows = (slice((4 * c + j) * ey, (4 * c + j + 1) * ey), slice(None))
            mass = at(final_rows(ey, 4, 0), j)
            speed = at(final_rows(ey, 3, c), j) - time_step * mass * force_ref[rows]
            v_out[c, 0, pl.ds(j, ey, stride=4), :] = speed
            u_out[c, 0, pl.ds(j, ey, stride=4), :] = at(final_rows(ey, 2, c), j) + time_step * speed
        for i in range(3):
            u_out[c, 1 + i] = at(final_rows(ey, 0, c, i))
            v_out[c, 1 + i] = at(final_rows(ey, 1, c, i))


def call(kernel, name, outs, scratch, *args, cost=None):
    shapes = [jax.ShapeDtypeStruct(s, F32) if name == "end" else pltpu.VMEM(s, F32) for s in outs]
    return pl.pallas_call(
        kernel,
        out_shape=shapes,
        scratch_shapes=[pltpu.VMEM(s, F32) for s in scratch],
        compiler_params=pltpu.CompilerParams(vmem_limit_bytes=32 * 1024 * 1024),
        cost_estimate=cost,
        name=name,
    )(*args)


def shards(sizes, displacement, velocity, inverse_mass, lame_first, lame_second, level_map):
    nx, ny = sizes
    _, ex4, ey4, lanes = displacement.shape
    ey = ey4 // 4
    tall, wide, short = 4 * ey, 3 * ey, 2 * ey

    def move(kind, x):
        return lax.ppermute(x, ("px", "py"), pairs_of(kind, nx, ny))

    def along_x(a, b):
        return move("near", a), move("far", b)

    def along_y(x):
        return move("core", x), move("across", x)

    flat = [x.reshape(-1, lanes) for x in (displacement, velocity, inverse_mass)]
    u_e, u_o = along_y(flat[0])
    gradient, divergence = depth_tables(lanes // 4)
    tables = [jnp.asarray(t) for t in (gradient, divergence, weight_table(lanes // 4))]
    sources = flat + [lame_first, lame_second, level_map] + tables
    own_u, own_v, own_m, first, second, level, gradient, divergence, weights = pl.pallas_call(
        functools.partial(load_kernel, len(sources)),
        out_shape=[pltpu.VMEM(x.shape, x.dtype) for x in sources],
        in_specs=[pl.BlockSpec(memory_space=pl.ANY)] * len(sources),
        scratch_shapes=[pltpu.SemaphoreType.DMA((len(sources),))],
        name="load",
    )(*sources)
    long = pl.CostEstimate(flops=20_000_000_000, bytes_accessed=0, transcendentals=0)
    starts = [int(n) for n in np.cumsum([own_v.shape[0], own_m.shape[0], 128, 128])]
    (own,) = call(functools.partial(pack_kernel, starts), "pack", [(starts[3] + 8, lanes)], [], own_v, own_m, first, second, level)
    from_e, from_o = along_y(own)
    (rim,) = call(functools.partial(rim_kernel, ny, ey4), "rim", [(-(-3 * (3 * ey4 - 3) // 8) * 8, lanes)], [], own_u, u_e, u_o, cost=long)
    (rim_1,) = call(copy_kernel, "face", [rim.shape], [], rim, cost=long)
    rim_a, rim_b = along_x(rim_1, rim)
    sizes_y, sizes_x = (ny, ey, lanes), (nx, ey, lanes)

    def shape(*lead, rows=tall):
        return (*lead, rows, lanes)

    def near_shapes(rows):
        points = functools.partial(shape, rows=rows)
        return [(45, rows, 2 * lanes), points(3, 15), points(3, 25), points(3, 15), points(2, 15)]

    def ends_scratch(rows):
        points = functools.partial(shape, rows=rows)
        return [points(3, 2, 10), points(3, 10), points(24), (24, rows, 2 * lanes), (6, rows, 2 * lanes), points(3, 8)]

    def between_scratch(rows, rows_next):
        points = functools.partial(shape, rows=rows)
        return [points(3, 15), points(3, 2, 15), points(3, 15)] + ([shape(45, rows=rows_next)] if rows_next else [])

    u_ends, u_inner = call(
        functools.partial(spread_u_kernel, sizes_y), "spread_u", [shape(3, 4), shape(3, 3, 4)], [], own_u, u_e, u_o
    )
    lame, level = call(
        functools.partial(tables_kernel, sizes_y, starts), "tables", [shape(2, 2, 25), shape(2)], [(3, 264, lanes)],
        own, from_e, from_o, weights,
    )
    gz, gy, *near = call(first_kernel, "before0", near_shapes(tall), [shape(45)], u_inner, lame, gradient)
    v_ends, v_inner, m_ends, m_inner = call(
        functools.partial(spread_v_kernel, sizes_y, starts[0]), "spread_v",
        [shape(3, 4), shape(3, 3, 4), shape(4), shape(3, 4)], [], own, from_e, from_o,
    )

    tables = (lame, level, gradient, divergence)
    message = (message_rows(1, 3 * ey - 2, 4), lanes)
    rim_u, old_ends, flux_x, gx, total, send_a, send_b = call(
        functools.partial(start_kernel, sizes_x), "stress0",
        [shape(3, 4), shape(6, 2, 10), shape(3, 25), shape(3, 25), shape(3, 2, 4), message, message],
        ends_scratch(tall),
        u_ends, v_ends, m_ends, rim_a, rim_b, *near, *tables,
    )
    got_a, got_b = along_x(send_a, send_b)
    every, window, mine = slice(0, tall), slice(ey - 2, 3 * ey - 2), slice(2, 2 + ey)
    *state, old_inner = call(
        functools.partial(between_kernel, every, False, None, (0, 0), True, newest, (0, 0)), "between0",
        [shape(3, 3, 4), shape(3, 3, 4), shape(3, 4)] + near_shapes(tall) + [shape(6, 2, 15)], between_scratch(tall, tall),
        flux_x, gx, gz, gy, u_inner, v_inner, m_inner, level, *tables,
    )
    u_inner, v_inner, m_inner, gz, gy, *near = state

    ends = shape(3, 2, 4, rows=short)
    message = (message_rows(0, 2 * ey - 1, 3), lanes)
    u_ends, v_ends, m_ends, flux_x, gx, total, send_a, send_b = call(
        functools.partial(second_kernel, sizes_x), "stress1",
        [ends, ends, ends[1:], shape(3, 25), shape(3, 25), ends, message, message],
        [shape(2, 4, 4), shape(3, 2, 4)] + ends_scratch(tall),
        u_ends, rim_u, v_ends, m_ends, total, got_a, got_b, *near, old_ends, *tables,
    )
    got_a, got_b = along_x(send_a, send_b)
    inner = shape(3, 3, 4, rows=short)
    u_inner, v_inner, m_inner, gz, gy, *near = call(
        functools.partial(between_kernel, window, False, newest, (0, 0), False, newer, (ey - 2, ey - 2)), "between1",
        [inner, inner, inner[1:]] + near_shapes(short), between_scratch(tall, short),
        flux_x, gx, gz, gy, u_inner, v_inner, m_inner, old_inner, *tables,
    )

    points, got = shape(3, 25, rows=short), shape(2, 3, 4, rows=short)
    message = (message_rows(1, 2 + ey, 3), lanes)
    u_ends, v_ends, old_ends, flux_x, gx, total, send_a, send_b = call(
        functools.partial(later_kernel, sizes_x, False), "stress2",
        [ends, ends, shape(6, 2, 10, rows=short), points, points, ends, message, message], [got] + ends_scratch(short),
        u_ends, v_ends, m_ends, total, got_a, got_b, *near, old_ends, *tables,
    )
    got_a, got_b = along_x(send_a, send_b)
    every = slice(0, short)
    *state, old_inner = call(
        functools.partial(between_kernel, every, False, newer, (ey - 2, ey - 2), True, newest, (ey - 2, 0)), "between2",
        [inner, inner, inner[1:]] + near_shapes(short) + [shape(6, 2, 15, rows=short)], between_scratch(short, short),
        flux_x, gx, gz, gy, u_inner, v_inner, m_inner, old_inner, *tables,
    )
    u_inner, v_inner, m_inner, gz, gy, *near = state

    message = (12 * ey, lanes)
    u_ends, v_ends, flux_x, gx, total, send_a, send_b = call(
        functools.partial(later_kernel, sizes_x, True), "stress3",
        [ends, ends, points, points, ends, message, message], [got] + ends_scratch(short),
        u_ends, v_ends, m_ends, total, got_a, got_b, *near, old_ends, *tables,
    )
    got_a, got_b = move("home", send_a), move("far", send_b)
    (results,) = call(
        functools.partial(between_kernel, mine, True, newest, (ey - 2, 0), False, None, None), "between3",
        [(25 * ey4, lanes)], between_scratch(short, 0),
        flux_x, gx, gz, gy, u_inner, v_inner, m_inner, old_inner, *tables, u_ends, v_ends, m_ends, total,
    )
    (force,) = call(functools.partial(pick_kernel, nx), "pick", [message], [], got_a, got_b, cost=long)
    return tuple(call(
        functools.partial(end_kernel, sizes_x), "end", [displacement.shape, velocity.shape], [],
        results, move("core", results), force,
    ))


def solution(mesh):
    sizes = (mesh.shape["px"], mesh.shape["py"])
    in_specs = (
        P(None, "px", "py", None),
        P(None, "px", "py", None),
        P("px", "py", None),
        P(None, None, None, "px", "py"),
        P(None, None, None, "px", "py"),
        P("px", "py"),
    )
    out_specs = (P(None, "px", "py", None), P(None, "px", "py", None))
    return jax.shard_map(
        functools.partial(shards, sizes), mesh=mesh, in_specs=in_specs, out_specs=out_specs, check_vma=False
    )
```

```python
import functools

import jax
import jax.numpy as jnp
import numpy as np
from jax import lax
from jax.experimental import pallas as pl
from jax.experimental.pallas import tpu as pltpu
from jax.sharding import PartitionSpec as P

time_step = 0.1
LEVELS = 3
F32 = jnp.float32
BF16 = jnp.bfloat16


def gll_tables():
    points = np.array([-1.0, -np.sqrt(3.0 / 7.0), 0.0, np.sqrt(3.0 / 7.0), 1.0])
    weights = np.array([0.1, 49.0 / 90.0, 32.0 / 45.0, 49.0 / 90.0, 0.1])
    legendre = (35.0 * points**4 - 30.0 * points**2 + 3.0) / 8.0
    derivative = np.zeros((5, 5))
    for row_index in range(5):
        for col_index in range(5):
            if row_index != col_index:
                derivative[row_index, col_index] = legendre[row_index] / (
                    legendre[col_index] * (points[row_index] - points[col_index])
                )
    derivative[0, 0] = -5.0
    derivative[4, 4] = 5.0
    return (derivative, weights)


D, W = gll_tables()


def split(table):
    high = np.asarray(table, np.float32).astype(BF16)
    low = (np.asarray(table, np.float64) - high.astype(np.float64)).astype(BF16)
    return high, low


def depth_tables(depth):
    lanes = 4 * depth
    table = np.zeros((lanes, 2 * lanes))
    for c in range(depth):
        for i in range(5):
            if 4 * c + i < lanes:
                for k in range(4):
                    table[4 * c + i, 4 * c + k] = D[k, i]
                table[4 * c + i, lanes + (4 * (c + 1)) % lanes] = D[4, i]
    high, low = split(table)
    gradient = np.concatenate([high, high, low], axis=0)
    divergence = np.concatenate([high.T, low.T], axis=1)
    return gradient, divergence


def weight_table(depth):
    lanes = 4 * depth
    pair = (W[:, None] * W[None, :]).reshape(25, 1)
    main = pair * np.tile(W[:4], depth)[None, :]
    last = pair * np.where(np.arange(lanes) % 4 == 0, W[4], 0.0)[None, :]
    return np.concatenate([main, last], axis=0).astype(np.float32)


def apply5(matrix, x):
    s0, s1 = x[0] + x[4], x[1] + x[3]
    d0, d1 = x[0] - x[4], x[1] - x[3]

    def even(a):
        p, q = (matrix[a, 0] - matrix[a, 4]) / 2, (matrix[a, 1] - matrix[a, 3]) / 2
        return d0 * float(p) + d1 * float(q)

    def odd(a):
        p, q = (matrix[a, 0] + matrix[a, 4]) / 2, (matrix[a, 1] + matrix[a, 3]) / 2
        return s0 * float(p) + s1 * float(q) + x[2] * float(matrix[a, 2])

    e0, e1, e2 = even(0), even(1), even(2)
    o0, o1 = odd(0), odd(1)
    return [e0 + o0, e1 + o1, e2, e1 - o1, e0 - o0]


def apply5_middle(matrix, x):
    s1, d1 = x[0] + x[2], x[0] - x[2]
    e = [d1 * float((matrix[a, 1] - matrix[a, 3]) / 2) for a in range(3)]
    o = [s1 * float((matrix[a, 1] + matrix[a, 3]) / 2) + x[1] * float(matrix[a, 2]) for a in range(2)]
    return [e[0] + o[0], e[1] + o[1], e[2], e[1] - o[1], e[0] - o[0]]


def apply5_ends(matrix, first, last, middle):
    s0, d0 = first + last, first - last
    e = [d0 * float((matrix[a, 0] - matrix[a, 4]) / 2) for a in range(3)]
    o = [s0 * float((matrix[a, 0] + matrix[a, 4]) / 2) for a in range(2)]
    ends = [e[0] + o[0], e[1] + o[1], e[2], e[1] - o[1], e[0] - o[0]]
    return [middle[a] + ends[a] for a in range(5)]


def halves(x):
    high = x.astype(BF16)
    return high, (x - high.astype(F32)).astype(BF16)


def rolled(x, by):
    return pltpu.roll(x, by % x.shape[0], 0)


def pairs_of(kind, nx, ny):
    pairs = []
    for i in range(nx):
        for j in range(ny):
            if kind == "core":
                target = (i, j ^ 1)
            elif kind == "near":
                target = (i ^ 1, j ^ 1)
            elif kind == "home":
                target = (i ^ 1, j)
            elif kind == "far":
                there = i + 1 if i % 2 else i - 1
                target = (there if 0 <= there < nx else i, j ^ 1)
            elif i % 2:
                there = j + 2 if j % 2 else j - 2
                target = (i, there if 0 <= there < ny else j ^ 1)
            else:
                there = j + 1 if j % 2 else j - 1
                target = (i, there) if 0 <= there < ny else (i ^ 2, j) if nx % 4 == 0 else (i, ny - 1 - j)
            pairs.append((i * ny + j, target[0] * ny + target[1]))
    return pairs


def place(axis, size):
    here = lax.axis_index(axis)
    return lax.rem(here, 2) == 0, here == 0, here == size - 1


def load_kernel(count, *refs):
    sources, targets, sems = refs[:count], refs[count : 2 * count], refs[2 * count]
    copies = [pltpu.make_async_copy(a, b, sems.at[n]) for n, (a, b) in enumerate(zip(sources, targets))]
    for copy in copies:
        copy.start()
    for copy in copies:
        copy.wait()


def copy_kernel(x_ref, out):
    out[...] = x_ref[...]


def pack_kernel(starts, v_ref, m_ref, first_ref, second_ref, level_ref, out):
    out[0 : v_ref.shape[0], :] = v_ref[...]
    out[starts[0] : starts[0] + m_ref.shape[0], :] = m_ref[...]
    for p, table in enumerate((first_ref, second_ref)):
        for row in range(125):
            i, j, k = row // 25, row // 5 % 5, row % 5
            out[starts[1 + p] + row : starts[1 + p] + row + 1, :] = table[i, j, k]
    out[starts[3] : starts[3] + 1, :] = level_ref[...].astype(F32)


def sides(ny):
    here = lax.axis_index("py")
    changed = lax.rem(lax.axis_index("px"), 2) == 1
    even = (lax.rem(here, 2) == 0) != changed
    first = jnp.logical_and(here < 2, even)
    last = jnp.logical_and(here >= ny - 2, jnp.logical_not(even))

    def centre(own, core, chip, at):
        return jnp.where(changed, core[at], own[at])

    def other(own, core, at):
        return jnp.where(changed, own[at], core[at])

    def left(own, core, chip, at):
        return jnp.where(first, 0.0, jnp.where(even, chip[at], other(own, core, at)))

    def right(own, core, chip, at):
        return jnp.where(last, 0.0, jnp.where(even, other(own, core, at), chip[at]))

    return left, centre, right


def rim_kernel(ny, across, own, core, chip, out):
    ahead = across - 3
    for c in range(3):
        base = c * (2 * across + ahead)
        for n, (side, count) in enumerate(zip(sides(ny), (across, across, ahead))):
            at = (slice(4 * c * across, 4 * c * across + count), slice(None))
            out[base + n * across : base + n * across + count, :] = side(own, core, chip, at)


def spread(sizes, own, core, chip, base, outs):
    ny, ey, lanes = sizes
    for j in range(4):
        at = (pl.ds(base + j, 2 * ey, stride=4), slice(None))
        for n, side in enumerate(sides(ny)):
            both = side(own, core, chip, at)
            for half, out in enumerate(outs):
                out[j, n * ey : (n + 1) * ey, :] = both[half * ey : (half + 1) * ey]
        for out in outs:
            out[j, 3 * ey :, :] = jnp.zeros((ey, lanes), F32)


def spread_layers(sizes, own, core, chip, base, ends, inner):
    tall = 4 * sizes[1]
    spread(sizes, own, core, chip, base, (ends, inner.at[0]))
    spread(sizes, own, core, chip, base + 2 * tall, (inner.at[1], inner.at[2]))


def segments(low, high):
    found, offset = [], 0
    for j in range(4):
        stop = high + (j == 0)
        found.append((offset, slice(low, stop)))
        offset += stop - low
    return found, offset


def message_rows(low, high, fields):
    return -(-segments(low, high)[1] * fields // 8) * 8


def write_message(ref, low, high, field, rows_of):
    found, total = segments(low, high)
    for j, (offset, rows) in enumerate(found):
        start = field * total + offset
        ref[start : start + rows.stop - rows.start, :] = rows_of(j, rows)


def read_message(out, low, high, field, one_ref, other_ref, even, none):
    found, total = segments(low, high)
    for j, (offset, rows) in enumerate(found):
        at = (slice(field * total + offset, field * total + offset + rows.stop - rows.start), slice(None))
        out[j, rows, :] = jnp.where(none, 0.0, jnp.where(even, one_ref[at], other_ref[at]))


def spread_u_kernel(sizes, own, e, o, ends, inner):
    for c in range(3):
        spread_layers(sizes, own, e, o, 16 * c * sizes[1], ends.at[c], inner.at[c])


def spread_v_kernel(sizes, start, own, e, o, v_ends, v_inner, m_ends, m_inner):
    for c in range(3):
        spread_layers(sizes, own, e, o, 16 * c * sizes[1], v_ends.at[c], v_inner.at[c])
    spread_layers(sizes, own, e, o, start, m_ends, m_inner)


def tables_kernel(sizes, starts, own_ref, e_ref, o_ref, weight_ref, lame_ref, level_ref, sel):
    ny, ey, lanes = sizes
    for n, side in enumerate(sides(ny)):
        sel[n] = side(own_ref, e_ref, o_ref, (slice(starts[1], own_ref.shape[0]), slice(None)))

    shape = (2 * ey, lanes)
    sub = lax.broadcasted_iota(jnp.int32, shape, 0)
    lane = lax.broadcasted_iota(jnp.int32, shape, 1)
    ez = lanes // 4
    column = lax.rem(sub, ey) * ez
    main_at = column + lane // 4
    last_at = column + lax.rem(lane // 4 + ez - 1, ez)
    point = lax.rem(lane, 4)
    upper = sub < ey

    def both(row):
        zero = jnp.zeros(shape, F32)
        a = jnp.broadcast_to(sel[0, pl.ds(row, 1), :], shape)
        b = jnp.broadcast_to(sel[1, pl.ds(row, 1), :], shape)
        c = jnp.broadcast_to(sel[2, pl.ds(row, 1), :], shape)
        return jnp.where(upper, a, b), jnp.where(upper, c, zero)

    def gather(x, at):
        return jnp.take_along_axis(x, at, axis=1, mode="promise_in_bounds")

    for ij in range(25):
        weight = jnp.broadcast_to(weight_ref[ij : ij + 1, :], shape)
        weight_last = jnp.broadcast_to(weight_ref[25 + ij : 26 + ij, :], shape)
        for p in range(2):
            points = [both(starts[1 + p] - starts[1] + ij * 5 + k) for k in range(5)]
            for h in range(2):
                got = [gather(points[k][h], main_at) for k in range(4)]
                main = jnp.where(
                    point < 2, jnp.where(point == 0, got[0], got[1]), jnp.where(point == 2, got[2], got[3])
                )
                lame_ref[p, 0, ij, 2 * ey * h : 2 * ey * (h + 1), :] = main * weight
                lame_ref[p, 1, ij, 2 * ey * h : 2 * ey * (h + 1), :] = gather(points[4][h], last_at) * weight_last
    levels = both(starts[3] - starts[1])
    for h in range(2):
        level_ref[0, 2 * ey * h : 2 * ey * (h + 1), :] = gather(levels[h], main_at)
        level_ref[1, 2 * ey * h : 2 * ey * (h + 1), :] = gather(levels[h], last_at)


def five(values):
    return list(values) + [rolled(values[0], -1)]


def grad_z(points, grad_ref, out):
    count, tall, lanes = points.shape
    high, low = halves(points[...].reshape(count * tall, lanes))
    lhs = jnp.concatenate([high, low, high], axis=1)
    out[...] = jnp.dot(lhs, grad_ref[...], preferred_element_type=F32).reshape(count, tall, 2 * lanes)


def div_z(main, point, div_ref):
    lanes = main.shape[-1]
    (main_high, main_low), (point_high, point_low) = halves(main), halves(point)
    high = jnp.dot(jnp.concatenate([main_high, point_high], axis=1), div_ref[...], preferred_element_type=F32)
    low = jnp.concatenate([main_low, point_low], axis=1)
    return high[:, :lanes] + (high[:, lanes:] + jnp.dot(low, div_ref[:, :lanes], preferred_element_type=F32))


def inside(lanes):
    return (lax.broadcasted_iota(jnp.int32, (8, lanes), 1) > 0).astype(F32)


def stress_of(first, second, x, y, z):
    trace = first * (x[0] + y[1] + z[2])
    twice = second + second
    return [
        trace + twice * x[0],
        trace + twice * y[1],
        second * (y[0] + x[1]),
        second * (z[0] + x[2]),
        second * (z[1] + y[2]),
        trace + twice * z[2],
    ]


def before(inner, tall, window, keep, lame, level, old, old_window, grad_ref, gz, gy, px, part, scale, us):
    lanes = gy.shape[-1]
    for c in range(3):
        points = [five(inner[c][i]) for i in range(3)]
        for i in range(3):
            for j in range(5):
                us[15 * c + 5 * i + j] = points[i][j]
        for i in range(3):
            y = apply5(D, points[i])
            for j in range(5):
                gy[c, 5 * i + j] = y[j]
        for j in range(5):
            y = apply5_middle(D, [points[i][j] for i in range(3)])
            for i in range(5):
                px[c, 5 * i + j] = y[i]
    grad_z(us, grad_ref, gz)
    mask = inside(lanes)
    for h in range(tall // 8):
        at = slice(8 * h, 8 * h + 8)
        table = slice(window + 8 * h, window + 8 * h + 8)
        stored = slice(old_window + 8 * h, old_window + 8 * h + 8)
        if keep is not None:
            fresh = [keep(level[e, table, :]) for e in range(2)]
        for p in range(15):
            y = [gy[c, p, at, :] for c in range(3)]
            sums = []
            for e in range(2):
                span = slice(e * lanes, (e + 1) * lanes)
                z0, z2 = gz[p, at, span], gz[30 + p, at, span]
                first, second = lame[0, e, 5 + p, table, :], lame[1, e, 5 + p, table, :]
                parts = [first * (y[1] + z2), second * y[0], second * z0]
                scales = [first + (second + second), second]
                if keep is not None:
                    parts = [jnp.where(fresh[e], parts[n], old[(0, 2, 3)[n], e, p, stored, :]) for n in range(3)]
                    scales = [jnp.where(fresh[e], x, 0.0) for x in scales]
                both = parts + scales
                sums.append([x * mask for x in both] if e == 1 else both)
            for n in range(3):
                part[n, p, at, :] = sums[0][n] + sums[1][n]
            for n in range(2):
                scale[n, p, at, :] = sums[0][3 + n] + sums[1][3 + n]


def stresses(tall, windows, keep, ends, px, part, scale, lame, level, old, new, flux_x, gx, flux_z, flux_y, us, gz_ends, last_z, qz, grad_ref, div_ref, total):
    lanes = px.shape[-1]
    points = [[five(ends[c][side]) for side in range(2)] for c in range(3)]
    for c in range(3):
        for side in range(2):
            for j in range(4):
                us[8 * c + 4 * side + j] = points[c][side][j]
    grad_z(us, grad_ref, gz_ends)
    for n in range(6):
        last_z[n] = rolled(gz_ends[4 * n], -1)
    for c in range(3):
        for j in range(5):
            y = apply5_ends(D, points[c][0][j], points[c][1][j], [px[c, 5 * i + j] for i in range(5)])
            for i in range(5):
                gx[c, 5 * i + j] = y[i]
                if 0 < i < 4:
                    flux_x[c, 5 * i + j] = scale[min(c, 1), 5 * i + j - 5] * y[i] + part[c, 5 * i + j - 5]
    mask = inside(lanes)
    for h in range(tall // 8):
        at = slice(8 * h, 8 * h + 8)
        table = slice(windows[0] + 8 * h, windows[0] + 8 * h + 8)
        stored = slice(windows[1] + 8 * h, windows[1] + 8 * h + 8)
        if keep is not None:
            fresh = [keep(level[e, table, :]) for e in range(2)]
        for side in range(2):
            ends_y = [apply5(D, [points[c][side][j][at] for j in range(5)]) for c in range(3)]
            for j in range(5):
                p, q = 20 * side + j, 5 * side + j
                x = [gx[c, p, at, :] for c in range(3)]
                y = [ends_y[c][j] for c in range(3)]
                sums = []
                for e in range(2):
                    span = slice(e * lanes, (e + 1) * lanes)
                    if j < 4:
                        z = [gz_ends[8 * c + 4 * side + j, at, span] for c in range(3)]
                    else:
                        z = [last_z[2 * c + side, at, span] for c in range(3)]
                    if e == 1:
                        x, y = [g * mask for g in x], [g * mask for g in y]
                    stress = stress_of(lame[0, e, p, table, :], lame[1, e, p, table, :], x, y, z)
                    if keep is not None:
                        stress = [jnp.where(fresh[e], stress[n], old[n, e, q, stored, :]) for n in range(6)]
                    if new is not None:
                        for n in range(6):
                            new[n, e, q, at, :] = stress[n]
                    for n in range(3):
                        flux_z[n, e, q, at, :] = stress[3 + n]
                    sums.append([v * mask for v in stress[:5]] if e == 1 else stress[:5])
                xx, yy, xy, xz, yz = [sums[0][n] + sums[1][n] for n in range(5)]
                for c in range(3):
                    flux_x[c, p, at, :] = (xx, xy, xz)[c]
                    flux_y[c, q, at, :] = (xy, yy, yz)[c]
    parts = []
    for e in range(2):
        rows = []
        for c in range(3):
            for side in range(2):
                first = 5 * side
                rows.append(flux_z[c, e, first] + rolled(flux_z[c, e, first + 4], 1))
                rows.append(flux_z[c, e, first + 1 : first + 4].reshape(3 * tall, lanes))
        parts.append(jnp.concatenate(rows, axis=0))
    qz[...] = div_z(*parts, div_ref).reshape(qz.shape)
    assemble((0, 4), flux_x, flux_y, qz, lambda c, side, j, value: total.__setitem__((c, side, j), value))


def assemble(layers, flux_x, flux_y, qz, put):
    count = qz.shape[1] // len(layers)
    for c in range(3):
        pieces = []
        for j in range(5):
            x = apply5(D.T, [flux_x[c, 5 * i + j] for i in range(5)])
            pieces.append([x[i] for i in layers])
        for n in range(len(layers)):
            y = apply5(D.T, [flux_y[c, 5 * n + j] for j in range(5)])
            z = [pieces[j][n] + (y[j] + qz[c, count * n + j] if j < count else y[j]) for j in range(5)]
            put(c, n, 0, z[0] + rolled(z[4], 1))
            for j in range(1, 4):
                put(c, n, j, z[j])


def first_kernel(u_inner, lame, grad_ref, gz, gy, px, part, scale, us):
    tall = u_inner.shape[3]
    inner = [[[u_inner[c, i, j] for j in range(4)] for i in range(3)] for c in range(3)]
    before(inner, tall, 0, None, lame, None, None, 0, grad_ref, gz, gy, px, part, scale, us)


def between_kernel(rows, last, keep, windows, stores, keep_next, windows_next, flux_x, gx, gz, gy, u_ref, v_ref, m_ref, old,
                   lame, level, grad_ref, div_ref, *refs):
    refs = list(refs)
    new = None
    if last:
        u_ends, v_ends, m_ends, total, send = refs[:5]
        count = rows.stop - rows.start
        for j in range(4):
            mass = m_ends[0, j, rows, :]
            send[pl.ds(final_rows(count, 4, 0) + j, count, stride=4), :] = mass
            for c in range(3):
                speed = v_ends[c, 0, j, rows, :] - time_step * mass * total[c, 0, j, rows, :]
                send[pl.ds(final_rows(count, 2, c) + j, count, stride=4), :] = u_ends[c, 0, j, rows, :]
                send[pl.ds(final_rows(count, 3, c) + j, count, stride=4), :] = speed
    else:
        u_out, v_out = refs[:2]
        m_out, gz_out, gy_out, px_out, part, scale = refs[2:8]
    if stores:
        new = refs[8]
    flux_y, flux_z, qz = refs[-4:-1] if not last else refs[-3:]
    us = None if last else refs[-1]
    _, _, tall, lanes = gx.shape
    mask = inside(lanes)
    for h in range(tall // 8):
        at = slice(8 * h, 8 * h + 8)
        table = slice(windows[0] + 8 * h, windows[0] + 8 * h + 8)
        stored = slice(windows[1] + 8 * h, windows[1] + 8 * h + 8)
        if keep is not None:
            fresh = [keep(level[e, table, :]) for e in range(2)]
        for p in range(15):
            x = [gx[c, 5 + p, at, :] for c in range(3)]
            y = [gy[c, p, at, :] for c in range(3)]
            sums = []
            for e in range(2):
                z = [gz[15 * c + p, at, e * lanes : (e + 1) * lanes] for c in range(3)]
                if e == 1:
                    x, y = [g * mask for g in x], [g * mask for g in y]
                stress = stress_of(lame[0, e, 5 + p, table, :], lame[1, e, 5 + p, table, :], x, y, z)
                if keep is not None:
                    stress = [jnp.where(fresh[e], stress[n], old[n, e, p, stored, :]) for n in range(6)]
                if stores:
                    for n in range(6):
                        new[n, e, p, at, :] = stress[n]
                else:
                    for n in range(3):
                        flux_z[n, e, p, at, :] = stress[3 + n]
                sums.append([v * mask for v in stress[:5]] if e == 1 else stress[:5])
            for c, n in enumerate((2, 1, 4)):
                flux_y[c, p, at, :] = sums[0][n] + sums[1][n]
    if stores:
        flux_z = new.at[3:6]
    qz[...] = div_z(*(flux_z[:, e].reshape(45 * tall, lanes) for e in range(2)), div_ref).reshape(qz.shape)
    inner = [[[None] * 4 for _ in range(3)] for _ in range(3)]

    def put(c, n, j, force):
        mass = m_ref[n, j, rows, :]
        speed = v_ref[c, n, j, rows, :] - time_step * mass * force[rows]
        position = u_ref[c, n, j, rows, :] + time_step * speed
        if last:
            send[pl.ds(final_rows(count, 0, c, n) + j, count, stride=4), :] = position
            send[pl.ds(final_rows(count, 1, c, n) + j, count, stride=4), :] = speed
            return
        u_out[c, n, j], v_out[c, n, j] = position, speed
        if c == 0:
            m_out[n, j] = mass
        inner[c][n][j] = position

    assemble((1, 2, 3), flux_x, flux_y, qz, put)
    if not last:
        before(inner, rows.stop - rows.start, windows_next[0], keep_next, lame, level, new if stores else old, windows_next[1],
               grad_ref, gz_out, gy_out, px_out, part, scale, us)


def newest(level_of):
    return level_of > LEVELS - 1.5


def newer(level_of):
    return level_of > LEVELS - 2.5


def start_kernel(sizes, u_ref, v_ref, m_ref, a_ref, b_ref, px, part, scale, lame, level, grad_ref, div_ref,
                 rim_ref, new, flux_x, gx, total, send_a, send_b, layer, flux_z, flux_y, us, gz_ends, last_z, qz):
    nx, ey, lanes = sizes
    even, _, last = place("px", nx)
    tall = 4 * ey
    count = 12 * ey - 3
    layer[...] = jnp.zeros(layer.shape, F32)
    for c in range(3):
        at = (slice(c * count, (c + 1) * count), slice(None))
        layer[c, 0:count, :] = jnp.where(last, 0.0, jnp.where(even, a_ref[at], b_ref[at]))
        for j in range(4):
            rim_ref[c, j] = layer[c, pl.ds(j, tall, stride=4), :]
    ends = [[[u_ref[c, j] for j in range(4)], [rim_ref[c, j] for j in range(4)]] for c in range(3)]
    stresses(tall, (0, 0), None, ends, px, part, scale, lame, level, None, new, flux_x, gx, flux_z, flux_y, us, gz_ends, last_z, qz,
             grad_ref, div_ref, total)
    low, high = 1, 3 * ey - 2
    for c in range(3):

        def back(j, rows):
            return v_ref[c, j, rows, :] - time_step * m_ref[j, rows, :] * total[c, 0, j, rows, :]

        def ahead(j, rows):
            return total[c, 1, j, rows, :]

        write_message(send_a, low, high, c, lambda j, rows: jnp.where(even, ahead(j, rows), back(j, rows)))
        write_message(send_b, low, high, c, lambda j, rows: jnp.where(even, back(j, rows), ahead(j, rows)))
    for send in (send_a, send_b):
        write_message(send, low, high, 3, lambda j, rows: m_ref[j, rows, :])


def second_kernel(sizes, u_ref, rim_ref, v_ref, m_ref, total_ref, a_ref, b_ref, px, part, scale, old, lame, level, grad_ref, div_ref,
                  u_out, v_out, m_out, flux_x, gx, total_out, send_a, send_b, got, total, flux_z, flux_y, us, gz_ends, last_z, qz):
    nx, ey, lanes = sizes
    even, first, last = place("px", nx)
    tall = 4 * ey
    window = slice(ey - 2, 3 * ey - 2)
    got[...] = jnp.zeros(got.shape, F32)
    for c in range(4):
        read_message(got.at[0, c], 1, 3 * ey - 2, c, a_ref, b_ref, even, last)
    for c in range(3):
        read_message(got.at[1, c], 1, 3 * ey - 2, c, b_ref, a_ref, even, first)
    ends = [[[], []] for _ in range(3)]
    for c in range(3):
        for side in range(2):
            for j in range(4):
                if side == 0:
                    mass, speed, position = m_ref[j], v_ref[c, j], u_ref[c, j]
                    force = total_ref[c, 0, j] + got[1, c, j]
                else:
                    mass, speed, position = got[0, 3, j], got[0, c, j], rim_ref[c, j]
                    force = total_ref[c, 1, j]
                speed = speed - time_step * mass * force
                position = position + time_step * speed
                u_out[c, side, j], v_out[c, side, j] = position[window], speed[window]
                if c == 0:
                    m_out[side, j] = mass[window]
                ends[c][side].append(position)
    stresses(tall, (0, 0), newest, ends, px, part, scale, lame, level, old, None, flux_x, gx, flux_z, flux_y, us, gz_ends, last_z, qz,
             grad_ref, div_ref, total)
    for c in range(3):
        for side in range(2):
            for j in range(4):
                total_out[c, side, j] = total[c, side, j, window, :]
    send_faces(even, total_out, 0, 2 * ey - 1, send_a, send_b)


def send_faces(even, total, low, high, send_a, send_b):
    for c in range(3):

        def back(j, rows):
            return total[c, 0, j, rows, :]

        def ahead(j, rows):
            return total[c, 1, j, rows, :]

        write_message(send_a, low, high, c, lambda j, rows: jnp.where(even, ahead(j, rows), back(j, rows)))
        write_message(send_b, low, high, c, lambda j, rows: jnp.where(even, back(j, rows), ahead(j, rows)))


def later_kernel(sizes, final, u_ref, v_ref, m_ref, total_ref, a_ref, b_ref, px, part, scale, old, lame, level, grad_ref, div_ref, *refs):
    nx, ey, lanes = sizes
    if final:
        u_out, v_out, flux_x, gx, total, send_a, send_b, got, flux_z, flux_y, us, gz_ends, last_z, qz = refs
        new, keep, windows, low, high = None, newest, (ey - 2, 0), 1, 2 + ey
    else:
        u_out, v_out, new, flux_x, gx, total, send_a, send_b, got, flux_z, flux_y, us, gz_ends, last_z, qz = refs
        keep, windows, low, high = newer, (ey - 2, ey - 2), 0, 2 * ey - 1
    even, first, last = place("px", nx)
    got[...] = jnp.zeros(got.shape, F32)
    for c in range(3):
        read_message(got.at[1, c], low, high, c, a_ref, b_ref, even, last)
        read_message(got.at[0, c], low, high, c, b_ref, a_ref, even, first)
    ends = [[[], []] for _ in range(3)]
    for c in range(3):
        for side in range(2):
            for j in range(4):
                speed = v_ref[c, side, j] - time_step * m_ref[side, j] * (total_ref[c, side, j] + got[side, c, j])
                position = u_ref[c, side, j] + time_step * speed
                u_out[c, side, j], v_out[c, side, j] = position, speed
                ends[c][side].append(position)
    stresses(2 * ey, windows, keep, ends, px, part, scale, lame, level, old, new, flux_x, gx, flux_z, flux_y, us, gz_ends, last_z, qz,
             grad_ref, div_ref, total)
    if not final:
        send_faces(even, total, 1, 2 + ey, send_a, send_b)
        return
    for c in range(3):
        for j in range(4):
            at = slice((4 * c + j) * ey, (4 * c + j + 1) * ey)
            ahead = total[c, 1, j, 2 : 2 + ey, :]
            send_a[at, :] = ahead
            send_b[at, :] = ahead


def final_rows(ey, field, c, i=0):
    across = 4 * ey
    if field < 2:
        return (9 * field + 3 * c + i) * across
    return (18 + 3 * (field - 2) + c) * across


def pick_kernel(nx, a_ref, b_ref, out):
    even, first, _ = place("px", nx)
    out[...] = jnp.where(first, 0.0, jnp.where(even, b_ref[...], a_ref[...]))


def end_kernel(sizes, mine, core, force_ref, u_out, v_out, layer):
    nx, ey, lanes = sizes
    even, _, _ = place("px", nx)

    def at(start, j=None):
        rows = (slice(start, start + 4 * ey) if j is None else pl.ds(start + j, ey, stride=4), slice(None))
        return jnp.where(even, mine[rows], core[rows])

    for c in range(3):
        for j in range(4):
            rows = (slice((4 * c + j) * ey, (4 * c + j + 1) * ey), slice(None))
            mass = at(final_rows(ey, 4, 0), j)
            speed = at(final_rows(ey, 3, c), j) - time_step * mass * force_ref[rows]
            layer[3 + c, pl.ds(j, ey, stride=4), :] = speed
            layer[c, pl.ds(j, ey, stride=4), :] = at(final_rows(ey, 2, c), j) + time_step * speed
        u_out[c, 0] = layer[c, : 4 * ey, :]
        v_out[c, 0] = layer[3 + c, : 4 * ey, :]
        for i in range(3):
            u_out[c, 1 + i] = at(final_rows(ey, 0, c, i))
            v_out[c, 1 + i] = at(final_rows(ey, 1, c, i))


def call(kernel, name, outs, scratch, *args, cost=None):
    shapes = [jax.ShapeDtypeStruct(s, F32) if name == "end" else pltpu.VMEM(s, F32) for s in outs]
    return pl.pallas_call(
        kernel,
        out_shape=shapes,
        scratch_shapes=[pltpu.VMEM(s, F32) for s in scratch],
        compiler_params=pltpu.CompilerParams(vmem_limit_bytes=32 * 1024 * 1024),
        cost_estimate=cost,
        name=name,
    )(*args)


def shards(sizes, displacement, velocity, inverse_mass, lame_first, lame_second, level_map):
    nx, ny = sizes
    _, ex4, ey4, lanes = displacement.shape
    ey = ey4 // 4
    tall, wide, short = 4 * ey, 3 * ey, 2 * ey

    def move(kind, x):
        return lax.ppermute(x, ("px", "py"), pairs_of(kind, nx, ny))

    def along_x(a, b):
        return move("near", a), move("far", b)

    def along_y(x):
        return move("core", x), move("across", x)

    flat = [x.reshape(-1, lanes) for x in (displacement, velocity, inverse_mass)]
    u_e, u_o = along_y(flat[0])
    gradient, divergence = depth_tables(lanes // 4)
    tables = [jnp.asarray(t) for t in (gradient, divergence, weight_table(lanes // 4))]
    sources = flat + [lame_first, lame_second, level_map] + tables
    own_u, own_v, own_m, first, second, level, gradient, divergence, weights = pl.pallas_call(
        functools.partial(load_kernel, len(sources)),
        out_shape=[pltpu.VMEM(x.shape, x.dtype) for x in sources],
        in_specs=[pl.BlockSpec(memory_space=pl.ANY)] * len(sources),
        scratch_shapes=[pltpu.SemaphoreType.DMA((len(sources),))],
        name="load",
    )(*sources)
    long = pl.CostEstimate(flops=20_000_000_000, bytes_accessed=0, transcendentals=0)
    starts = [int(n) for n in np.cumsum([own_v.shape[0], own_m.shape[0], 128, 128])]
    (own,) = call(functools.partial(pack_kernel, starts), "pack", [(starts[3] + 8, lanes)], [], own_v, own_m, first, second, level)
    from_e, from_o = along_y(own)
    (rim,) = call(functools.partial(rim_kernel, ny, ey4), "rim", [(-(-3 * (3 * ey4 - 3) // 8) * 8, lanes)], [], own_u, u_e, u_o, cost=long)
    (rim_1,) = call(copy_kernel, "face", [rim.shape], [], rim, cost=long)
    rim_a, rim_b = along_x(rim_1, rim)
    sizes_y, sizes_x = (ny, ey, lanes), (nx, ey, lanes)

    def shape(*lead, rows=tall):
        return (*lead, rows, lanes)

    def near_shapes(rows):
        points = functools.partial(shape, rows=rows)
        return [(45, rows, 2 * lanes), points(3, 15), points(3, 25), points(3, 15), points(2, 15)]

    def ends_scratch(rows):
        points = functools.partial(shape, rows=rows)
        return [points(3, 2, 10), points(3, 10), points(24), (24, rows, 2 * lanes), (6, rows, 2 * lanes), points(3, 8)]

    def between_scratch(rows, rows_next):
        points = functools.partial(shape, rows=rows)
        return [points(3, 15), points(3, 2, 15), points(3, 15)] + ([shape(45, rows=rows_next)] if rows_next else [])

    u_ends, u_inner = call(
        functools.partial(spread_u_kernel, sizes_y), "spread_u", [shape(3, 4), shape(3, 3, 4)], [], own_u, u_e, u_o
    )
    lame, level = call(
        functools.partial(tables_kernel, sizes_y, starts), "tables", [shape(2, 2, 25), shape(2)], [(3, 264, lanes)],
        own, from_e, from_o, weights,
    )
    gz, gy, *near = call(first_kernel, "before0", near_shapes(tall), [shape(45)], u_inner, lame, gradient)
    v_ends, v_inner, m_ends, m_inner = call(
        functools.partial(spread_v_kernel, sizes_y, starts[0]), "spread_v",
        [shape(3, 4), shape(3, 3, 4), shape(4), shape(3, 4)], [], own, from_e, from_o,
    )

    tables = (lame, level, gradient, divergence)
    message = (message_rows(1, 3 * ey - 2, 4), lanes)
    rim_u, old_ends, flux_x, gx, total, send_a, send_b = call(
        functools.partial(start_kernel, sizes_x), "stress0",
        [shape(3, 4), shape(6, 2, 10), shape(3, 25), shape(3, 25), shape(3, 2, 4), message, message],
        [(3, 4 * tall, lanes)] + ends_scratch(tall),
        u_ends, v_ends, m_ends, rim_a, rim_b, *near, *tables,
    )
    got_a, got_b = along_x(send_a, send_b)
    every, window, mine = slice(0, tall), slice(ey - 2, 3 * ey - 2), slice(2, 2 + ey)
    *state, old_inner = call(
        functools.partial(between_kernel, every, False, None, (0, 0), True, newest, (0, 0)), "between0",
        [shape(3, 3, 4), shape(3, 3, 4), shape(3, 4)] + near_shapes(tall) + [shape(6, 2, 15)], between_scratch(tall, tall),
        flux_x, gx, gz, gy, u_inner, v_inner, m_inner, level, *tables,
    )
    u_inner, v_inner, m_inner, gz, gy, *near = state

    ends = shape(3, 2, 4, rows=short)
    message = (message_rows(0, 2 * ey - 1, 3), lanes)
    u_ends, v_ends, m_ends, flux_x, gx, total, send_a, send_b = call(
        functools.partial(second_kernel, sizes_x), "stress1",
        [ends, ends, ends[1:], shape(3, 25), shape(3, 25), ends, message, message],
        [shape(2, 4, 4), shape(3, 2, 4)] + ends_scratch(tall),
        u_ends, rim_u, v_ends, m_ends, total, got_a, got_b, *near, old_ends, *tables,
    )
    got_a, got_b = along_x(send_a, send_b)
    inner = shape(3, 3, 4, rows=short)
    u_inner, v_inner, m_inner, gz, gy, *near = call(
        functools.partial(between_kernel, window, False, newest, (0, 0), False, newer, (ey - 2, ey - 2)), "between1",
        [inner, inner, inner[1:]] + near_shapes(short), between_scratch(tall, short),
        flux_x, gx, gz, gy, u_inner, v_inner, m_inner, old_inner, *tables,
    )

    points, got = shape(3, 25, rows=short), shape(2, 3, 4, rows=short)
    message = (message_rows(1, 2 + ey, 3), lanes)
    u_ends, v_ends, old_ends, flux_x, gx, total, send_a, send_b = call(
        functools.partial(later_kernel, sizes_x, False), "stress2",
        [ends, ends, shape(6, 2, 10, rows=short), points, points, ends, message, message], [got] + ends_scratch(short),
        u_ends, v_ends, m_ends, total, got_a, got_b, *near, old_ends, *tables,
    )
    got_a, got_b = along_x(send_a, send_b)
    every = slice(0, short)
    *state, old_inner = call(
        functools.partial(between_kernel, every, False, newer, (ey - 2, ey - 2), True, newest, (ey - 2, 0)), "between2",
        [inner, inner, inner[1:]] + near_shapes(short) + [shape(6, 2, 15, rows=short)], between_scratch(short, short),
        flux_x, gx, gz, gy, u_inner, v_inner, m_inner, old_inner, *tables,
    )
    u_inner, v_inner, m_inner, gz, gy, *near = state

    message = (12 * ey, lanes)
    u_ends, v_ends, flux_x, gx, total, send_a, send_b = call(
        functools.partial(later_kernel, sizes_x, True), "stress3",
        [ends, ends, points, points, ends, message, message], [got] + ends_scratch(short),
        u_ends, v_ends, m_ends, total, got_a, got_b, *near, old_ends, *tables,
    )
    got_a, got_b = move("home", send_a), move("far", send_b)
    (results,) = call(
        functools.partial(between_kernel, mine, True, newest, (ey - 2, 0), False, None, None), "between3",
        [(26 * ey4, lanes)], between_scratch(short, 0),
        flux_x, gx, gz, gy, u_inner, v_inner, m_inner, old_inner, *tables, u_ends, v_ends, m_ends, total,
    )
    (force,) = call(functools.partial(pick_kernel, nx), "pick", [message], [], got_a, got_b, cost=long)
    return tuple(call(
        functools.partial(end_kernel, sizes_x), "end", [displacement.shape, velocity.shape], [(6, 2 * ey4, lanes)],
        results, move("core", results), force,
    ))


def solution(mesh):
    sizes = (mesh.shape["px"], mesh.shape["py"])
    in_specs = (
        P(None, "px", "py", None),
        P(None, "px", "py", None),
        P("px", "py", None),
        P(None, None, None, "px", "py"),
        P(None, None, None, "px", "py"),
        P("px", "py"),
    )
    out_specs = (P(None, "px", "py", None), P(None, "px", "py", None))
    return jax.shard_map(
        functools.partial(shards, sizes), mesh=mesh, in_specs=in_specs, out_specs=out_specs, check_vma=False
    )
```

```python
import functools

import jax
import jax.numpy as jnp
import numpy as np
from jax import lax
from jax.experimental import pallas as pl
from jax.experimental.pallas import tpu as pltpu
from jax.sharding import PartitionSpec as P

time_step = 0.1
LEVELS = 3
F32 = jnp.float32
BF16 = jnp.bfloat16


def gll_tables():
    points = np.array([-1.0, -np.sqrt(3.0 / 7.0), 0.0, np.sqrt(3.0 / 7.0), 1.0])
    weights = np.array([0.1, 49.0 / 90.0, 32.0 / 45.0, 49.0 / 90.0, 0.1])
    legendre = (35.0 * points**4 - 30.0 * points**2 + 3.0) / 8.0
    derivative = np.zeros((5, 5))
    for row_index in range(5):
        for col_index in range(5):
            if row_index != col_index:
                derivative[row_index, col_index] = legendre[row_index] / (
                    legendre[col_index] * (points[row_index] - points[col_index])
                )
    derivative[0, 0] = -5.0
    derivative[4, 4] = 5.0
    return (derivative, weights)


D, W = gll_tables()


def split(table):
    high = np.asarray(table, np.float32).astype(BF16)
    low = (np.asarray(table, np.float64) - high.astype(np.float64)).astype(BF16)
    return high, low


def depth_tables(depth):
    lanes = 4 * depth
    table = np.zeros((lanes, 2 * lanes))
    for c in range(depth):
        for i in range(5):
            if 4 * c + i < lanes:
                for k in range(4):
                    table[4 * c + i, 4 * c + k] = D[k, i]
                table[4 * c + i, lanes + (4 * (c + 1)) % lanes] = D[4, i]
    high, low = split(table)
    gradient = np.concatenate([high, high, low], axis=0)
    divergence = np.concatenate([high.T, low.T], axis=1)
    return gradient, divergence


def weight_table(depth):
    lanes = 4 * depth
    pair = (W[:, None] * W[None, :]).reshape(25, 1)
    main = pair * np.tile(W[:4], depth)[None, :]
    last = pair * np.where(np.arange(lanes) % 4 == 0, W[4], 0.0)[None, :]
    return np.concatenate([main, last], axis=0).astype(np.float32)


def apply5(matrix, x):
    s0, s1 = x[0] + x[4], x[1] + x[3]
    d0, d1 = x[0] - x[4], x[1] - x[3]

    def even(a):
        p, q = (matrix[a, 0] - matrix[a, 4]) / 2, (matrix[a, 1] - matrix[a, 3]) / 2
        return d0 * float(p) + d1 * float(q)

    def odd(a):
        p, q = (matrix[a, 0] + matrix[a, 4]) / 2, (matrix[a, 1] + matrix[a, 3]) / 2
        return s0 * float(p) + s1 * float(q) + x[2] * float(matrix[a, 2])

    e0, e1, e2 = even(0), even(1), even(2)
    o0, o1 = odd(0), odd(1)
    return [e0 + o0, e1 + o1, e2, e1 - o1, e0 - o0]


def apply5_middle(matrix, x):
    s1, d1 = x[0] + x[2], x[0] - x[2]
    e = [d1 * float((matrix[a, 1] - matrix[a, 3]) / 2) for a in range(3)]
    o = [s1 * float((matrix[a, 1] + matrix[a, 3]) / 2) + x[1] * float(matrix[a, 2]) for a in range(2)]
    return [e[0] + o[0], e[1] + o[1], e[2], e[1] - o[1], e[0] - o[0]]


def apply5_ends(matrix, first, last, middle):
    s0, d0 = first + last, first - last
    e = [d0 * float((matrix[a, 0] - matrix[a, 4]) / 2) for a in range(3)]
    o = [s0 * float((matrix[a, 0] + matrix[a, 4]) / 2) for a in range(2)]
    ends = [e[0] + o[0], e[1] + o[1], e[2], e[1] - o[1], e[0] - o[0]]
    return [middle[a] + ends[a] for a in range(5)]


def halves(x):
    high = x.astype(BF16)
    return high, (x - high.astype(F32)).astype(BF16)


def rolled(x, by):
    return pltpu.roll(x, by % x.shape[0], 0)


def pairs_of(kind, nx, ny):
    pairs = []
    for i in range(nx):
        for j in range(ny):
            if kind == "core":
                target = (i, j ^ 1)
            elif kind == "near":
                target = (i ^ 1, j ^ 1)
            elif kind == "home":
                target = (i ^ 1, j)
            elif kind == "far":
                there = i + 1 if i % 2 else i - 1
                target = (there if 0 <= there < nx else i, j ^ 1)
            elif i % 2:
                there = j + 2 if j % 2 else j - 2
                target = (i, there if 0 <= there < ny else j ^ 1)
            else:
                there = j + 1 if j % 2 else j - 1
                target = (i, there) if 0 <= there < ny else (i ^ 2, j) if nx % 4 == 0 else (i, ny - 1 - j)
            pairs.append((i * ny + j, target[0] * ny + target[1]))
    return pairs


def place(axis, size):
    here = lax.axis_index(axis)
    return lax.rem(here, 2) == 0, here == 0, here == size - 1


def load_kernel(count, *refs):
    sources, targets, sems = refs[:count], refs[count : 2 * count], refs[2 * count]
    copies = [pltpu.make_async_copy(a, b, sems.at[n]) for n, (a, b) in enumerate(zip(sources, targets))]
    for copy in copies:
        copy.start()
    for copy in copies:
        copy.wait()


def copy_kernel(x_ref, out):
    out[...] = x_ref[...]


def pack_kernel(starts, v_ref, m_ref, first_ref, second_ref, level_ref, out):
    out[0 : v_ref.shape[0], :] = v_ref[...]
    out[starts[0] : starts[0] + m_ref.shape[0], :] = m_ref[...]
    for p, table in enumerate((first_ref, second_ref)):
        for row in range(125):
            i, j, k = row // 25, row // 5 % 5, row % 5
            out[starts[1 + p] + row : starts[1 + p] + row + 1, :] = table[i, j, k]
    out[starts[3] : starts[3] + 1, :] = level_ref[...].astype(F32)


def sides(ny):
    here = lax.axis_index("py")
    changed = lax.rem(lax.axis_index("px"), 2) == 1
    even = (lax.rem(here, 2) == 0) != changed
    first = jnp.logical_and(here < 2, even)
    last = jnp.logical_and(here >= ny - 2, jnp.logical_not(even))

    def centre(own, core, chip, at):
        return jnp.where(changed, core[at], own[at])

    def other(own, core, at):
        return jnp.where(changed, own[at], core[at])

    def left(own, core, chip, at):
        return jnp.where(first, 0.0, jnp.where(even, chip[at], other(own, core, at)))

    def right(own, core, chip, at):
        return jnp.where(last, 0.0, jnp.where(even, other(own, core, at), chip[at]))

    return left, centre, right


def rim_kernel(ny, across, own, core, chip, out):
    ahead = across - 3
    for c in range(3):
        base = c * (2 * across + ahead)
        for n, (side, count) in enumerate(zip(sides(ny), (across, across, ahead))):
            at = (slice(4 * c * across, 4 * c * across + count), slice(None))
            out[base + n * across : base + n * across + count, :] = side(own, core, chip, at)


def spread(sizes, own, core, chip, base, out):
    ny, ey, lanes = sizes
    for j in range(4):
        at = (pl.ds(base + j, ey, stride=4), slice(None))
        for n, side in enumerate(sides(ny)):
            out[j, n * ey : (n + 1) * ey, :] = side(own, core, chip, at)
        out[j, 3 * ey :, :] = jnp.zeros((ey, lanes), F32)


def segments(low, high):
    found, offset = [], 0
    for j in range(4):
        stop = high + (j == 0)
        found.append((offset, slice(low, stop)))
        offset += stop - low
    return found, offset


def message_rows(low, high, fields):
    return -(-segments(low, high)[1] * fields // 8) * 8


def write_message(ref, low, high, field, rows_of):
    found, total = segments(low, high)
    for j, (offset, rows) in enumerate(found):
        start = field * total + offset
        ref[start : start + rows.stop - rows.start, :] = rows_of(j, rows)


def read_message(out, low, high, field, one_ref, other_ref, even, none):
    found, total = segments(low, high)
    for j, (offset, rows) in enumerate(found):
        at = (slice(field * total + offset, field * total + offset + rows.stop - rows.start), slice(None))
        out[j, rows, :] = jnp.where(none, 0.0, jnp.where(even, one_ref[at], other_ref[at]))


def spread_u_kernel(sizes, own, e, o, ends, inner):
    tall = 4 * sizes[1]
    for c in range(3):
        spread(sizes, own, e, o, 4 * c * tall, ends.at[c])
        for i in range(3):
            spread(sizes, own, e, o, (4 * c + 1 + i) * tall, inner.at[c, i])


def spread_v_kernel(sizes, start, own, e, o, v_ends, v_inner, m_ends, m_inner):
    tall = 4 * sizes[1]
    for c in range(3):
        spread(sizes, own, e, o, 4 * c * tall, v_ends.at[c])
        for i in range(3):
            spread(sizes, own, e, o, (4 * c + 1 + i) * tall, v_inner.at[c, i])
    spread(sizes, own, e, o, start, m_ends)
    for i in range(3):
        spread(sizes, own, e, o, start + (1 + i) * tall, m_inner.at[i])


def tables_kernel(sizes, starts, own_ref, e_ref, o_ref, weight_ref, lame_ref, level_ref, sel):
    ny, ey, lanes = sizes
    for n, side in enumerate(sides(ny)):
        sel[n] = side(own_ref, e_ref, o_ref, (slice(starts[1], own_ref.shape[0]), slice(None)))

    shape = (2 * ey, lanes)
    sub = lax.broadcasted_iota(jnp.int32, shape, 0)
    lane = lax.broadcasted_iota(jnp.int32, shape, 1)
    ez = lanes // 4
    column = lax.rem(sub, ey) * ez
    main_at = column + lane // 4
    last_at = column + lax.rem(lane // 4 + ez - 1, ez)
    point = lax.rem(lane, 4)
    upper = sub < ey

    def both(row):
        zero = jnp.zeros(shape, F32)
        a = jnp.broadcast_to(sel[0, pl.ds(row, 1), :], shape)
        b = jnp.broadcast_to(sel[1, pl.ds(row, 1), :], shape)
        c = jnp.broadcast_to(sel[2, pl.ds(row, 1), :], shape)
        return jnp.where(upper, a, b), jnp.where(upper, c, zero)

    def gather(x, at):
        return jnp.take_along_axis(x, at, axis=1, mode="promise_in_bounds")

    for ij in range(25):
        weight = jnp.broadcast_to(weight_ref[ij : ij + 1, :], shape)
        weight_last = jnp.broadcast_to(weight_ref[25 + ij : 26 + ij, :], shape)
        for p in range(2):
            points = [both(starts[1 + p] - starts[1] + ij * 5 + k) for k in range(5)]
            for h in range(2):
                got = [gather(points[k][h], main_at) for k in range(4)]
                main = jnp.where(
                    point < 2, jnp.where(point == 0, got[0], got[1]), jnp.where(point == 2, got[2], got[3])
                )
                lame_ref[p, 0, ij, 2 * ey * h : 2 * ey * (h + 1), :] = main * weight
                lame_ref[p, 1, ij, 2 * ey * h : 2 * ey * (h + 1), :] = gather(points[4][h], last_at) * weight_last
    levels = both(starts[3] - starts[1])
    for h in range(2):
        level_ref[0, 2 * ey * h : 2 * ey * (h + 1), :] = gather(levels[h], main_at)
        level_ref[1, 2 * ey * h : 2 * ey * (h + 1), :] = gather(levels[h], last_at)


def five(values):
    return list(values) + [rolled(values[0], -1)]


def grad_z(points, grad_ref, out):
    count, tall, lanes = points.shape
    high, low = halves(points[...].reshape(count * tall, lanes))
    lhs = jnp.concatenate([high, low, high], axis=1)
    out[...] = jnp.dot(lhs, grad_ref[...], preferred_element_type=F32).reshape(count, tall, 2 * lanes)


def div_z(main, point, div_ref):
    lanes = main.shape[-1]
    (main_high, main_low), (point_high, point_low) = halves(main), halves(point)
    high = jnp.dot(jnp.concatenate([main_high, point_high], axis=1), div_ref[...], preferred_element_type=F32)
    low = jnp.concatenate([main_low, point_low], axis=1)
    return high[:, :lanes] + (high[:, lanes:] + jnp.dot(low, div_ref[:, :lanes], preferred_element_type=F32))


def inside(lanes):
    return (lax.broadcasted_iota(jnp.int32, (8, lanes), 1) > 0).astype(F32)


def stress_of(first, second, x, y, z):
    trace = first * (x[0] + y[1] + z[2])
    twice = second + second
    return [
        trace + twice * x[0],
        trace + twice * y[1],
        second * (y[0] + x[1]),
        second * (z[0] + x[2]),
        second * (z[1] + y[2]),
        trace + twice * z[2],
    ]


def before(inner, tall, window, keep, lame, level, old, old_window, grad_ref, gz, gy, px, part, scale, us):
    lanes = gy.shape[-1]
    for c in range(3):
        points = [five(inner[c][i]) for i in range(3)]
        for i in range(3):
            for j in range(5):
                us[15 * c + 5 * i + j] = points[i][j]
        for i in range(3):
            y = apply5(D, points[i])
            for j in range(5):
                gy[c, 5 * i + j] = y[j]
        for j in range(5):
            y = apply5_middle(D, [points[i][j] for i in range(3)])
            for i in range(5):
                px[c, 5 * i + j] = y[i]
    grad_z(us, grad_ref, gz)
    mask = inside(lanes)
    for h in range(tall // 8):
        at = slice(8 * h, 8 * h + 8)
        table = slice(window + 8 * h, window + 8 * h + 8)
        stored = slice(old_window + 8 * h, old_window + 8 * h + 8)
        if keep is not None:
            fresh = [keep(level[e, table, :]) for e in range(2)]
        for p in range(15):
            y = [gy[c, p, at, :] for c in range(3)]
            sums = []
            for e in range(2):
                span = slice(e * lanes, (e + 1) * lanes)
                z0, z2 = gz[p, at, span], gz[30 + p, at, span]
                first, second = lame[0, e, 5 + p, table, :], lame[1, e, 5 + p, table, :]
                parts = [first * (y[1] + z2), second * y[0], second * z0]
                scales = [first + (second + second), second]
                if keep is not None:
                    parts = [jnp.where(fresh[e], parts[n], old[(0, 2, 3)[n], e, p, stored, :]) for n in range(3)]
                    scales = [jnp.where(fresh[e], x, 0.0) for x in scales]
                both = parts + scales
                sums.append([x * mask for x in both] if e == 1 else both)
            for n in range(3):
                part[n, p, at, :] = sums[0][n] + sums[1][n]
            for n in range(2):
                scale[n, p, at, :] = sums[0][3 + n] + sums[1][3 + n]


def stresses(tall, windows, keep, ends, px, part, scale, lame, level, old, new, flux_x, gx, flux_z, flux_y, us, gz_ends, last_z, qz, grad_ref, div_ref, total, known=None):
    lanes = px.shape[-1]
    points = [[five(ends[c][side]) for side in range(2)] for c in range(3)]
    for c in range(3):
        for side in range(2):
            for j in range(4):
                if known is None:
                    us[8 * c + 4 * side + j] = points[c][side][j]
                elif side == 1:
                    us[4 * c + j] = points[c][side][j]
    grad_z(us, grad_ref, gz_ends)

    def along_z(c, side, j):
        if known is None:
            return gz_ends.at[8 * c + 4 * side + j]
        return (gz_ends if side else known).at[4 * c + j]

    for n in range(6):
        last_z[n] = rolled(along_z(n // 2, n % 2, 0)[...], -1)
    for c in range(3):
        for j in range(5):
            y = apply5_ends(D, points[c][0][j], points[c][1][j], [px[c, 5 * i + j] for i in range(5)])
            for i in range(5):
                gx[c, 5 * i + j] = y[i]
                if 0 < i < 4:
                    flux_x[c, 5 * i + j] = scale[min(c, 1), 5 * i + j - 5] * y[i] + part[c, 5 * i + j - 5]
    mask = inside(lanes)
    for h in range(tall // 8):
        at = slice(8 * h, 8 * h + 8)
        table = slice(windows[0] + 8 * h, windows[0] + 8 * h + 8)
        stored = slice(windows[1] + 8 * h, windows[1] + 8 * h + 8)
        if keep is not None:
            fresh = [keep(level[e, table, :]) for e in range(2)]
        for side in range(2):
            ends_y = [apply5(D, [points[c][side][j][at] for j in range(5)]) for c in range(3)]
            for j in range(5):
                p, q = 20 * side + j, 5 * side + j
                x = [gx[c, p, at, :] for c in range(3)]
                y = [ends_y[c][j] for c in range(3)]
                sums = []
                for e in range(2):
                    span = slice(e * lanes, (e + 1) * lanes)
                    if j < 4:
                        z = [along_z(c, side, j)[at, span] for c in range(3)]
                    else:
                        z = [last_z[2 * c + side, at, span] for c in range(3)]
                    if e == 1:
                        x, y = [g * mask for g in x], [g * mask for g in y]
                    stress = stress_of(lame[0, e, p, table, :], lame[1, e, p, table, :], x, y, z)
                    if keep is not None:
                        stress = [jnp.where(fresh[e], stress[n], old[n, e, q, stored, :]) for n in range(6)]
                    if new is not None:
                        for n in range(6):
                            new[n, e, q, at, :] = stress[n]
                    for n in range(3):
                        flux_z[n, e, q, at, :] = stress[3 + n]
                    sums.append([v * mask for v in stress[:5]] if e == 1 else stress[:5])
                xx, yy, xy, xz, yz = [sums[0][n] + sums[1][n] for n in range(5)]
                for c in range(3):
                    flux_x[c, p, at, :] = (xx, xy, xz)[c]
                    flux_y[c, q, at, :] = (xy, yy, yz)[c]
    parts = []
    for e in range(2):
        rows = []
        for c in range(3):
            for side in range(2):
                first = 5 * side
                rows.append(flux_z[c, e, first] + rolled(flux_z[c, e, first + 4], 1))
                rows.append(flux_z[c, e, first + 1 : first + 4].reshape(3 * tall, lanes))
        parts.append(jnp.concatenate(rows, axis=0))
    qz[...] = div_z(*parts, div_ref).reshape(qz.shape)
    assemble((0, 4), flux_x, flux_y, qz, lambda c, side, j, value: total.__setitem__((c, side, j), value))


def assemble(layers, flux_x, flux_y, qz, put):
    count = qz.shape[1] // len(layers)
    for c in range(3):
        pieces = []
        for j in range(5):
            x = apply5(D.T, [flux_x[c, 5 * i + j] for i in range(5)])
            pieces.append([x[i] for i in layers])
        for n in range(len(layers)):
            y = apply5(D.T, [flux_y[c, 5 * n + j] for j in range(5)])
            z = [pieces[j][n] + (y[j] + qz[c, count * n + j] if j < count else y[j]) for j in range(5)]
            put(c, n, 0, z[0] + rolled(z[4], 1))
            for j in range(1, 4):
                put(c, n, j, z[j])


def first_kernel(u_ends, u_inner, lame, grad_ref, gz, gy, px, part, scale, gz_ends, us, us_ends):
    tall = u_inner.shape[3]
    for c in range(3):
        for j in range(4):
            us_ends[4 * c + j] = u_ends[c, j]
    grad_z(us_ends, grad_ref, gz_ends)
    inner = [[[u_inner[c, i, j] for j in range(4)] for i in range(3)] for c in range(3)]
    before(inner, tall, 0, None, lame, None, None, 0, grad_ref, gz, gy, px, part, scale, us)


def between_kernel(rows, last, keep, windows, stores, keep_next, windows_next, flux_x, gx, gz, gy, u_ref, v_ref, m_ref, old,
                   lame, level, grad_ref, div_ref, *refs):
    refs = list(refs)
    new = None
    if last:
        u_ends, v_ends, m_ends, total, send = refs[:5]
        count = rows.stop - rows.start
        for j in range(4):
            mass = m_ends[0, j, rows, :]
            send[pl.ds(final_rows(count, 4, 0) + j, count, stride=4), :] = mass
            for c in range(3):
                speed = v_ends[c, 0, j, rows, :] - time_step * mass * total[c, 0, j, rows, :]
                send[pl.ds(final_rows(count, 2, c) + j, count, stride=4), :] = u_ends[c, 0, j, rows, :]
                send[pl.ds(final_rows(count, 3, c) + j, count, stride=4), :] = speed
    else:
        u_out, v_out = refs[:2]
        m_out, gz_out, gy_out, px_out, part, scale = refs[2:8]
    if stores:
        new = refs[8]
    flux_y, flux_z, qz = refs[-4:-1] if not last else refs[-3:]
    us = None if last else refs[-1]
    _, _, tall, lanes = gx.shape
    mask = inside(lanes)
    for h in range(tall // 8):
        at = slice(8 * h, 8 * h + 8)
        table = slice(windows[0] + 8 * h, windows[0] + 8 * h + 8)
        stored = slice(windows[1] + 8 * h, windows[1] + 8 * h + 8)
        if keep is not None:
            fresh = [keep(level[e, table, :]) for e in range(2)]
        for p in range(15):
            x = [gx[c, 5 + p, at, :] for c in range(3)]
            y = [gy[c, p, at, :] for c in range(3)]
            sums = []
            for e in range(2):
                z = [gz[15 * c + p, at, e * lanes : (e + 1) * lanes] for c in range(3)]
                if e == 1:
                    x, y = [g * mask for g in x], [g * mask for g in y]
                stress = stress_of(lame[0, e, 5 + p, table, :], lame[1, e, 5 + p, table, :], x, y, z)
                if keep is not None:
                    stress = [jnp.where(fresh[e], stress[n], old[n, e, p, stored, :]) for n in range(6)]
                if stores:
                    for n in range(6):
                        new[n, e, p, at, :] = stress[n]
                else:
                    for n in range(3):
                        flux_z[n, e, p, at, :] = stress[3 + n]
                sums.append([v * mask for v in stress[:5]] if e == 1 else stress[:5])
            for c, n in enumerate((2, 1, 4)):
                flux_y[c, p, at, :] = sums[0][n] + sums[1][n]
    if stores:
        flux_z = new.at[3:6]
    qz[...] = div_z(*(flux_z[:, e].reshape(45 * tall, lanes) for e in range(2)), div_ref).reshape(qz.shape)
    inner = [[[None] * 4 for _ in range(3)] for _ in range(3)]

    def put(c, n, j, force):
        mass = m_ref[n, j, rows, :]
        speed = v_ref[c, n, j, rows, :] - time_step * mass * force[rows]
        position = u_ref[c, n, j, rows, :] + time_step * speed
        if last:
            send[pl.ds(final_rows(count, 0, c, n) + j, count, stride=4), :] = position
            send[pl.ds(final_rows(count, 1, c, n) + j, count, stride=4), :] = speed
            return
        u_out[c, n, j], v_out[c, n, j] = position, speed
        if c == 0:
            m_out[n, j] = mass
        inner[c][n][j] = position

    assemble((1, 2, 3), flux_x, flux_y, qz, put)
    if not last:
        before(inner, rows.stop - rows.start, windows_next[0], keep_next, lame, level, new if stores else old, windows_next[1],
               grad_ref, gz_out, gy_out, px_out, part, scale, us)


def newest(level_of):
    return level_of > LEVELS - 1.5


def newer(level_of):
    return level_of > LEVELS - 2.5


def start_kernel(sizes, known, u_ref, v_ref, m_ref, a_ref, b_ref, px, part, scale, lame, level, grad_ref, div_ref,
                 rim_ref, new, flux_x, gx, total, send_a, send_b, flux_z, flux_y, us, gz_ends, last_z, qz):
    nx, ey, lanes = sizes
    even, _, last = place("px", nx)
    tall = 4 * ey
    rim_ref[...] = jnp.zeros(rim_ref.shape, F32)
    for c in range(3):
        for j in range(4):
            count = 3 * ey - (j > 0)
            at = (pl.ds(c * (12 * ey - 3) + j, count, stride=4), slice(None))
            rim_ref[c, j, 0:count, :] = jnp.where(last, 0.0, jnp.where(even, a_ref[at], b_ref[at]))
    ends = [[[u_ref[c, j] for j in range(4)], [rim_ref[c, j] for j in range(4)]] for c in range(3)]
    stresses(tall, (0, 0), None, ends, px, part, scale, lame, level, None, new, flux_x, gx, flux_z, flux_y, us, gz_ends, last_z, qz,
             grad_ref, div_ref, total, known)
    low, high = 1, 3 * ey - 2
    for c in range(3):

        def back(j, rows):
            return v_ref[c, j, rows, :] - time_step * m_ref[j, rows, :] * total[c, 0, j, rows, :]

        def ahead(j, rows):
            return total[c, 1, j, rows, :]

        write_message(send_a, low, high, c, lambda j, rows: jnp.where(even, ahead(j, rows), back(j, rows)))
        write_message(send_b, low, high, c, lambda j, rows: jnp.where(even, back(j, rows), ahead(j, rows)))
    for send in (send_a, send_b):
        write_message(send, low, high, 3, lambda j, rows: m_ref[j, rows, :])


def second_kernel(sizes, u_ref, rim_ref, v_ref, m_ref, total_ref, a_ref, b_ref, px, part, scale, old, lame, level, grad_ref, div_ref,
                  u_out, v_out, m_out, flux_x, gx, total_out, send_a, send_b, got, total, flux_z, flux_y, us, gz_ends, last_z, qz):
    nx, ey, lanes = sizes
    even, first, last = place("px", nx)
    tall = 4 * ey
    window = slice(ey - 2, 3 * ey - 2)
    got[...] = jnp.zeros(got.shape, F32)
    for c in range(4):
        read_message(got.at[0, c], 1, 3 * ey - 2, c, a_ref, b_ref, even, last)
    for c in range(3):
        read_message(got.at[1, c], 1, 3 * ey - 2, c, b_ref, a_ref, even, first)
    ends = [[[], []] for _ in range(3)]
    for c in range(3):
        for side in range(2):
            for j in range(4):
                if side == 0:
                    mass, speed, position = m_ref[j], v_ref[c, j], u_ref[c, j]
                    force = total_ref[c, 0, j] + got[1, c, j]
                else:
                    mass, speed, position = got[0, 3, j], got[0, c, j], rim_ref[c, j]
                    force = total_ref[c, 1, j]
                speed = speed - time_step * mass * force
                position = position + time_step * speed
                u_out[c, side, j], v_out[c, side, j] = position[window], speed[window]
                if c == 0:
                    m_out[side, j] = mass[window]
                ends[c][side].append(position)
    stresses(tall, (0, 0), newest, ends, px, part, scale, lame, level, old, None, flux_x, gx, flux_z, flux_y, us, gz_ends, last_z, qz,
             grad_ref, div_ref, total)
    for c in range(3):
        for side in range(2):
            for j in range(4):
                total_out[c, side, j] = total[c, side, j, window, :]
    send_faces(even, total_out, 0, 2 * ey - 1, send_a, send_b)


def send_faces(even, total, low, high, send_a, send_b):
    for c in range(3):

        def back(j, rows):
            return total[c, 0, j, rows, :]

        def ahead(j, rows):
            return total[c, 1, j, rows, :]

        write_message(send_a, low, high, c, lambda j, rows: jnp.where(even, ahead(j, rows), back(j, rows)))
        write_message(send_b, low, high, c, lambda j, rows: jnp.where(even, back(j, rows), ahead(j, rows)))


def later_kernel(sizes, final, u_ref, v_ref, m_ref, total_ref, a_ref, b_ref, px, part, scale, old, lame, level, grad_ref, div_ref, *refs):
    nx, ey, lanes = sizes
    if final:
        u_out, v_out, flux_x, gx, total, send_a, send_b, got, flux_z, flux_y, us, gz_ends, last_z, qz = refs
        new, keep, windows, low, high = None, newest, (ey - 2, 0), 1, 2 + ey
    else:
        u_out, v_out, new, flux_x, gx, total, send_a, send_b, got, flux_z, flux_y, us, gz_ends, last_z, qz = refs
        keep, windows, low, high = newer, (ey - 2, ey - 2), 0, 2 * ey - 1
    even, first, last = place("px", nx)
    got[...] = jnp.zeros(got.shape, F32)
    for c in range(3):
        read_message(got.at[1, c], low, high, c, a_ref, b_ref, even, last)
        read_message(got.at[0, c], low, high, c, b_ref, a_ref, even, first)
    ends = [[[], []] for _ in range(3)]
    for c in range(3):
        for side in range(2):
            for j in range(4):
                speed = v_ref[c, side, j] - time_step * m_ref[side, j] * (total_ref[c, side, j] + got[side, c, j])
                position = u_ref[c, side, j] + time_step * speed
                u_out[c, side, j], v_out[c, side, j] = position, speed
                ends[c][side].append(position)
    stresses(2 * ey, windows, keep, ends, px, part, scale, lame, level, old, new, flux_x, gx, flux_z, flux_y, us, gz_ends, last_z, qz,
             grad_ref, div_ref, total)
    if not final:
        send_faces(even, total, 1, 2 + ey, send_a, send_b)
        return
    for c in range(3):
        for j in range(4):
            at = slice((4 * c + j) * ey, (4 * c + j + 1) * ey)
            ahead = total[c, 1, j, 2 : 2 + ey, :]
            send_a[at, :] = ahead
            send_b[at, :] = ahead


def final_rows(ey, field, c, i=0):
    across = 4 * ey
    if field < 2:
        return (9 * field + 3 * c + i) * across
    return (18 + 3 * (field - 2) + c) * across


def pick_kernel(nx, a_ref, b_ref, out):
    even, first, _ = place("px", nx)
    out[...] = jnp.where(first, 0.0, jnp.where(even, b_ref[...], a_ref[...]))


def end_kernel(sizes, mine, core, force_ref, u_out, v_out):
    nx, ey, lanes = sizes
    even, _, _ = place("px", nx)

    def at(start, j=None):
        rows = (slice(start, start + 4 * ey) if j is None else pl.ds(start + j, ey, stride=4), slice(None))
        return jnp.where(even, mine[rows], core[rows])

    for c in range(3):
        for j in range(4):
            rows = (slice((4 * c + j) * ey, (4 * c + j + 1) * ey), slice(None))
            mass = at(final_rows(ey, 4, 0), j)
            speed = at(final_rows(ey, 3, c), j) - time_step * mass * force_ref[rows]
            v_out[c, 0, pl.ds(j, ey, stride=4), :] = speed
            u_out[c, 0, pl.ds(j, ey, stride=4), :] = at(final_rows(ey, 2, c), j) + time_step * speed
        for i in range(3):
            u_out[c, 1 + i] = at(final_rows(ey, 0, c, i))
            v_out[c, 1 + i] = at(final_rows(ey, 1, c, i))


def call(kernel, name, outs, scratch, *args, cost=None):
    shapes = [jax.ShapeDtypeStruct(s, F32) if name == "end" else pltpu.VMEM(s, F32) for s in outs]
    return pl.pallas_call(
        kernel,
        out_shape=shapes,
        scratch_shapes=[pltpu.VMEM(s, F32) for s in scratch],
        compiler_params=pltpu.CompilerParams(vmem_limit_bytes=32 * 1024 * 1024),
        cost_estimate=cost,
        name=name,
    )(*args)


def shards(sizes, displacement, velocity, inverse_mass, lame_first, lame_second, level_map):
    nx, ny = sizes
    _, ex4, ey4, lanes = displacement.shape
    ey = ey4 // 4
    tall, wide, short = 4 * ey, 3 * ey, 2 * ey

    def move(kind, x):
        return lax.ppermute(x, ("px", "py"), pairs_of(kind, nx, ny))

    def along_x(a, b):
        return move("near", a), move("far", b)

    def along_y(x):
        return move("core", x), move("across", x)

    flat = [x.reshape(-1, lanes) for x in (displacement, velocity, inverse_mass)]
    u_e, u_o = along_y(flat[0])
    gradient, divergence = depth_tables(lanes // 4)
    tables = [jnp.asarray(t) for t in (gradient, divergence, weight_table(lanes // 4))]
    sources = flat + [lame_first, lame_second, level_map] + tables
    own_u, own_v, own_m, first, second, level, gradient, divergence, weights = pl.pallas_call(
        functools.partial(load_kernel, len(sources)),
        out_shape=[pltpu.VMEM(x.shape, x.dtype) for x in sources],
        in_specs=[pl.BlockSpec(memory_space=pl.ANY)] * len(sources),
        scratch_shapes=[pltpu.SemaphoreType.DMA((len(sources),))],
        name="load",
    )(*sources)
    long = pl.CostEstimate(flops=20_000_000_000, bytes_accessed=0, transcendentals=0)
    starts = [int(n) for n in np.cumsum([own_v.shape[0], own_m.shape[0], 128, 128])]
    (own,) = call(functools.partial(pack_kernel, starts), "pack", [(starts[3] + 8, lanes)], [], own_v, own_m, first, second, level)
    from_e, from_o = along_y(own)
    (rim,) = call(functools.partial(rim_kernel, ny, ey4), "rim", [(-(-3 * (3 * ey4 - 3) // 8) * 8, lanes)], [], own_u, u_e, u_o, cost=long)
    (rim_1,) = call(copy_kernel, "face", [rim.shape], [], rim, cost=long)
    rim_a, rim_b = along_x(rim_1, rim)
    sizes_y, sizes_x = (ny, ey, lanes), (nx, ey, lanes)

    def shape(*lead, rows=tall):
        return (*lead, rows, lanes)

    def near_shapes(rows):
        points = functools.partial(shape, rows=rows)
        return [(45, rows, 2 * lanes), points(3, 15), points(3, 25), points(3, 15), points(2, 15)]

    def ends_scratch(rows, count=2):
        points = functools.partial(shape, rows=rows)
        return [points(3, 2, 10), points(3, 10), points(12 * count), (12 * count, rows, 2 * lanes), (6, rows, 2 * lanes), points(3, 8)]

    def between_scratch(rows, rows_next):
        points = functools.partial(shape, rows=rows)
        return [points(3, 15), points(3, 2, 15), points(3, 15)] + ([shape(45, rows=rows_next)] if rows_next else [])

    u_ends, u_inner = call(
        functools.partial(spread_u_kernel, sizes_y), "spread_u", [shape(3, 4), shape(3, 3, 4)], [], own_u, u_e, u_o
    )
    lame, level = call(
        functools.partial(tables_kernel, sizes_y, starts), "tables", [shape(2, 2, 25), shape(2)], [(3, 264, lanes)],
        own, from_e, from_o, weights,
    )
    gz, gy, *near, known = call(
        first_kernel, "before0", near_shapes(tall) + [(12, tall, 2 * lanes)], [shape(45), shape(12)],
        u_ends, u_inner, lame, gradient,
    )
    v_ends, v_inner, m_ends, m_inner = call(
        functools.partial(spread_v_kernel, sizes_y, starts[0]), "spread_v",
        [shape(3, 4), shape(3, 3, 4), shape(4), shape(3, 4)], [], own, from_e, from_o,
    )

    tables = (lame, level, gradient, divergence)
    message = (message_rows(1, 3 * ey - 2, 4), lanes)
    rim_u, old_ends, flux_x, gx, total, send_a, send_b = call(
        functools.partial(start_kernel, sizes_x), "stress0",
        [shape(3, 4), shape(6, 2, 10), shape(3, 25), shape(3, 25), shape(3, 2, 4), message, message],
        ends_scratch(tall, 1),
        known, u_ends, v_ends, m_ends, rim_a, rim_b, *near, *tables,
    )
    got_a, got_b = along_x(send_a, send_b)
    every, window, mine = slice(0, tall), slice(ey - 2, 3 * ey - 2), slice(2, 2 + ey)
    *state, old_inner = call(
        functools.partial(between_kernel, every, False, None, (0, 0), True, newest, (0, 0)), "between0",
        [shape(3, 3, 4), shape(3, 3, 4), shape(3, 4)] + near_shapes(tall) + [shape(6, 2, 15)], between_scratch(tall, tall),
        flux_x, gx, gz, gy, u_inner, v_inner, m_inner, level, *tables,
    )
    u_inner, v_inner, m_inner, gz, gy, *near = state

    ends = shape(3, 2, 4, rows=short)
    message = (message_rows(0, 2 * ey - 1, 3), lanes)
    u_ends, v_ends, m_ends, flux_x, gx, total, send_a, send_b = call(
        functools.partial(second_kernel, sizes_x), "stress1",
        [ends, ends, ends[1:], shape(3, 25), shape(3, 25), ends, message, message],
        [shape(2, 4, 4), shape(3, 2, 4)] + ends_scratch(tall),
        u_ends, rim_u, v_ends, m_ends, total, got_a, got_b, *near, old_ends, *tables,
    )
    got_a, got_b = along_x(send_a, send_b)
    inner = shape(3, 3, 4, rows=short)
    u_inner, v_inner, m_inner, gz, gy, *near = call(
        functools.partial(between_kernel, window, False, newest, (0, 0), False, newer, (ey - 2, ey - 2)), "between1",
        [inner, inner, inner[1:]] + near_shapes(short), between_scratch(tall, short),
        flux_x, gx, gz, gy, u_inner, v_inner, m_inner, old_inner, *tables,
    )

    points, got = shape(3, 25, rows=short), shape(2, 3, 4, rows=short)
    message = (message_rows(1, 2 + ey, 3), lanes)
    u_ends, v_ends, old_ends, flux_x, gx, total, send_a, send_b = call(
        functools.partial(later_kernel, sizes_x, False), "stress2",
        [ends, ends, shape(6, 2, 10, rows=short), points, points, ends, message, message], [got] + ends_scratch(short),
        u_ends, v_ends, m_ends, total, got_a, got_b, *near, old_ends, *tables,
    )
    got_a, got_b = along_x(send_a, send_b)
    every = slice(0, short)
    *state, old_inner = call(
        functools.partial(between_kernel, every, False, newer, (ey - 2, ey - 2), True, newest, (ey - 2, 0)), "between2",
        [inner, inner, inner[1:]] + near_shapes(short) + [shape(6, 2, 15, rows=short)], between_scratch(short, short),
        flux_x, gx, gz, gy, u_inner, v_inner, m_inner, old_inner, *tables,
    )
    u_inner, v_inner, m_inner, gz, gy, *near = state

    message = (12 * ey, lanes)
    u_ends, v_ends, flux_x, gx, total, send_a, send_b = call(
        functools.partial(later_kernel, sizes_x, True), "stress3",
        [ends, ends, points, points, ends, message, message], [got] + ends_scratch(short),
        u_ends, v_ends, m_ends, total, got_a, got_b, *near, old_ends, *tables,
    )
    got_a, got_b = move("home", send_a), move("far", send_b)
    (results,) = call(
        functools.partial(between_kernel, mine, True, newest, (ey - 2, 0), False, None, None), "between3",
        [(25 * ey4, lanes)], between_scratch(short, 0),
        flux_x, gx, gz, gy, u_inner, v_inner, m_inner, old_inner, *tables, u_ends, v_ends, m_ends, total,
    )
    (force,) = call(functools.partial(pick_kernel, nx), "pick", [message], [], got_a, got_b, cost=long)
    return tuple(call(
        functools.partial(end_kernel, sizes_x), "end", [displacement.shape, velocity.shape], [],
        results, move("core", results), force,
    ))


def solution(mesh):
    sizes = (mesh.shape["px"], mesh.shape["py"])
    in_specs = (
        P(None, "px", "py", None),
        P(None, "px", "py", None),
        P("px", "py", None),
        P(None, None, None, "px", "py"),
        P(None, None, None, "px", "py"),
        P("px", "py"),
    )
    out_specs = (P(None, "px", "py", None), P(None, "px", "py", None))
    return jax.shard_map(
        functools.partial(shards, sizes), mesh=mesh, in_specs=in_specs, out_specs=out_specs, check_vma=False
    )
```

```python
import functools

import jax
import jax.numpy as jnp
import numpy as np
from jax import lax
from jax.experimental import pallas as pl
from jax.experimental.pallas import tpu as pltpu
from jax.sharding import PartitionSpec as P

time_step = 0.1
LEVELS = 3
F32 = jnp.float32
BF16 = jnp.bfloat16


def gll_tables():
    points = np.array([-1.0, -np.sqrt(3.0 / 7.0), 0.0, np.sqrt(3.0 / 7.0), 1.0])
    weights = np.array([0.1, 49.0 / 90.0, 32.0 / 45.0, 49.0 / 90.0, 0.1])
    legendre = (35.0 * points**4 - 30.0 * points**2 + 3.0) / 8.0
    derivative = np.zeros((5, 5))
    for row_index in range(5):
        for col_index in range(5):
            if row_index != col_index:
                derivative[row_index, col_index] = legendre[row_index] / (
                    legendre[col_index] * (points[row_index] - points[col_index])
                )
    derivative[0, 0] = -5.0
    derivative[4, 4] = 5.0
    return (derivative, weights)


D, W = gll_tables()


def split(table):
    high = np.asarray(table, np.float32).astype(BF16)
    low = (np.asarray(table, np.float64) - high.astype(np.float64)).astype(BF16)
    return high, low


def depth_tables(depth):
    lanes = 4 * depth
    table = np.zeros((lanes, 2 * lanes))
    for c in range(depth):
        for i in range(5):
            if 4 * c + i < lanes:
                for k in range(4):
                    table[4 * c + i, 4 * c + k] = D[k, i]
                table[4 * c + i, lanes + (4 * (c + 1)) % lanes] = D[4, i]
    high, low = split(table)
    gradient = np.concatenate([high, high, low], axis=0)
    divergence = np.concatenate([high.T, low.T], axis=1)
    return gradient, divergence


def weight_table(depth):
    lanes = 4 * depth
    pair = (W[:, None] * W[None, :]).reshape(25, 1)
    main = pair * np.tile(W[:4], depth)[None, :]
    last = pair * np.where(np.arange(lanes) % 4 == 0, W[4], 0.0)[None, :]
    return np.concatenate([main, last], axis=0).astype(np.float32)


def apply5(matrix, x):
    s0, s1 = x[0] + x[4], x[1] + x[3]
    d0, d1 = x[0] - x[4], x[1] - x[3]

    def even(a):
        p, q = (matrix[a, 0] - matrix[a, 4]) / 2, (matrix[a, 1] - matrix[a, 3]) / 2
        return d0 * float(p) + d1 * float(q)

    def odd(a):
        p, q = (matrix[a, 0] + matrix[a, 4]) / 2, (matrix[a, 1] + matrix[a, 3]) / 2
        return s0 * float(p) + s1 * float(q) + x[2] * float(matrix[a, 2])

    e0, e1, e2 = even(0), even(1), even(2)
    o0, o1 = odd(0), odd(1)
    return [e0 + o0, e1 + o1, e2, e1 - o1, e0 - o0]


def apply5_middle(matrix, x):
    s1, d1 = x[0] + x[2], x[0] - x[2]
    e = [d1 * float((matrix[a, 1] - matrix[a, 3]) / 2) for a in range(3)]
    o = [s1 * float((matrix[a, 1] + matrix[a, 3]) / 2) + x[1] * float(matrix[a, 2]) for a in range(2)]
    return [e[0] + o[0], e[1] + o[1], e[2], e[1] - o[1], e[0] - o[0]]


def apply5_ends(matrix, first, last, middle):
    s0, d0 = first + last, first - last
    e = [d0 * float((matrix[a, 0] - matrix[a, 4]) / 2) for a in range(3)]
    o = [s0 * float((matrix[a, 0] + matrix[a, 4]) / 2) for a in range(2)]
    ends = [e[0] + o[0], e[1] + o[1], e[2], e[1] - o[1], e[0] - o[0]]
    return [middle[a] + ends[a] for a in range(5)]


def halves(x):
    high = x.astype(BF16)
    return high, (x - high.astype(F32)).astype(BF16)


def rolled(x, by):
    return pltpu.roll(x, by % x.shape[0], 0)


def pairs_of(kind, nx, ny):
    pairs = []
    for i in range(nx):
        for j in range(ny):
            if kind == "core":
                target = (i, j ^ 1)
            elif kind == "near":
                target = (i ^ 1, j ^ 1)
            elif kind == "home":
                target = (i ^ 1, j)
            elif kind == "far":
                there = i + 1 if i % 2 else i - 1
                target = (there if 0 <= there < nx else i, j ^ 1)
            elif i % 2:
                there = j + 2 if j % 2 else j - 2
                target = (i, there if 0 <= there < ny else j ^ 1)
            else:
                there = j + 1 if j % 2 else j - 1
                target = (i, there) if 0 <= there < ny else (i ^ 2, j) if nx % 4 == 0 else (i, ny - 1 - j)
            pairs.append((i * ny + j, target[0] * ny + target[1]))
    return pairs


def place(axis, size):
    here = lax.axis_index(axis)
    return lax.rem(here, 2) == 0, here == 0, here == size - 1


def load_kernel(count, *refs):
    sources, targets, sems = refs[:count], refs[count : 2 * count], refs[2 * count]
    copies = [pltpu.make_async_copy(a, b, sems.at[n]) for n, (a, b) in enumerate(zip(sources, targets))]
    for copy in copies:
        copy.start()
    for copy in copies:
        copy.wait()


def copy_kernel(x_ref, out):
    out[...] = x_ref[...]


def pack_kernel(starts, v_ref, m_ref, first_ref, second_ref, level_ref, out):
    out[0 : v_ref.shape[0], :] = v_ref[...]
    out[starts[0] : starts[0] + m_ref.shape[0], :] = m_ref[...]
    for p, table in enumerate((first_ref, second_ref)):
        for row in range(125):
            i, j, k = row // 25, row // 5 % 5, row % 5
            out[starts[1 + p] + row : starts[1 + p] + row + 1, :] = table[i, j, k]
    out[starts[3] : starts[3] + 1, :] = level_ref[...].astype(F32)


def sides(ny):
    here = lax.axis_index("py")
    changed = lax.rem(lax.axis_index("px"), 2) == 1
    even = (lax.rem(here, 2) == 0) != changed
    first = jnp.logical_and(here < 2, even)
    last = jnp.logical_and(here >= ny - 2, jnp.logical_not(even))

    def centre(own, core, chip, at):
        return jnp.where(changed, core[at], own[at])

    def other(own, core, at):
        return jnp.where(changed, own[at], core[at])

    def left(own, core, chip, at):
        return jnp.where(first, 0.0, jnp.where(even, chip[at], other(own, core, at)))

    def right(own, core, chip, at):
        return jnp.where(last, 0.0, jnp.where(even, other(own, core, at), chip[at]))

    return left, centre, right


def rim_kernel(ny, across, own, core, chip, out):
    ahead = across - 3
    for c in range(3):
        base = c * (2 * across + ahead)
        for n, (side, count) in enumerate(zip(sides(ny), (across, across, ahead))):
            at = (slice(4 * c * across, 4 * c * across + count), slice(None))
            out[base + n * across : base + n * across + count, :] = side(own, core, chip, at)


def spread(sizes, own, core, chip, base, out):
    ny, ey, lanes = sizes
    for j in range(4):
        at = (pl.ds(base + j, ey, stride=4), slice(None))
        for n, side in enumerate(sides(ny)):
            out[j, n * ey : (n + 1) * ey, :] = side(own, core, chip, at)
        out[j, 3 * ey :, :] = jnp.zeros((ey, lanes), F32)


def segments(low, high):
    found, offset = [], 0
    for j in range(4):
        stop = high + (j == 0)
        found.append((offset, slice(low, stop)))
        offset += stop - low
    return found, offset


def message_rows(low, high, fields):
    return -(-segments(low, high)[1] * fields // 8) * 8


def write_message(ref, low, high, field, rows_of):
    found, total = segments(low, high)
    for j, (offset, rows) in enumerate(found):
        start = field * total + offset
        ref[start : start + rows.stop - rows.start, :] = rows_of(j, rows)


def read_message(out, low, high, field, one_ref, other_ref, even, none):
    found, total = segments(low, high)
    for j, (offset, rows) in enumerate(found):
        at = (slice(field * total + offset, field * total + offset + rows.stop - rows.start), slice(None))
        out[j, rows, :] = jnp.where(none, 0.0, jnp.where(even, one_ref[at], other_ref[at]))


def spread_u_kernel(sizes, own, e, o, ends, inner):
    tall = 4 * sizes[1]
    for c in range(3):
        spread(sizes, own, e, o, 4 * c * tall, ends.at[c])
        for i in range(3):
            spread(sizes, own, e, o, (4 * c + 1 + i) * tall, inner.at[c, i])


def spread_v_kernel(sizes, start, own, e, o, v_ends, v_inner, m_ends, m_inner):
    tall = 4 * sizes[1]
    for c in range(3):
        spread(sizes, own, e, o, 4 * c * tall, v_ends.at[c])
        for i in range(3):
            spread(sizes, own, e, o, (4 * c + 1 + i) * tall, v_inner.at[c, i])
    spread(sizes, own, e, o, start, m_ends)
    for i in range(3):
        spread(sizes, own, e, o, start + (1 + i) * tall, m_inner.at[i])


def tables_kernel(sizes, starts, own_ref, e_ref, o_ref, weight_ref, lame_ref, level_ref, sel):
    ny, ey, lanes = sizes
    for n, side in enumerate(sides(ny)):
        sel[n] = side(own_ref, e_ref, o_ref, (slice(starts[1], own_ref.shape[0]), slice(None)))

    shape = (2 * ey, lanes)
    sub = lax.broadcasted_iota(jnp.int32, shape, 0)
    lane = lax.broadcasted_iota(jnp.int32, shape, 1)
    ez = lanes // 4
    column = lax.rem(sub, ey) * ez
    main_at = column + lane // 4
    last_at = column + lax.rem(lane // 4 + ez - 1, ez)
    point = lax.rem(lane, 4)
    upper = sub < ey

    def both(row):
        zero = jnp.zeros(shape, F32)
        a = jnp.broadcast_to(sel[0, pl.ds(row, 1), :], shape)
        b = jnp.broadcast_to(sel[1, pl.ds(row, 1), :], shape)
        c = jnp.broadcast_to(sel[2, pl.ds(row, 1), :], shape)
        return jnp.where(upper, a, b), jnp.where(upper, c, zero)

    def gather(x, at):
        return jnp.take_along_axis(x, at, axis=1, mode="promise_in_bounds")

    for ij in range(25):
        weight = jnp.broadcast_to(weight_ref[ij : ij + 1, :], shape)
        weight_last = jnp.broadcast_to(weight_ref[25 + ij : 26 + ij, :], shape)
        for p in range(2):
            points = [both(starts[1 + p] - starts[1] + ij * 5 + k) for k in range(5)]
            for h in range(2):
                got = [gather(points[k][h], main_at) for k in range(4)]
                main = jnp.where(
                    point < 2, jnp.where(point == 0, got[0], got[1]), jnp.where(point == 2, got[2], got[3])
                )
                lame_ref[p, 0, ij, 2 * ey * h : 2 * ey * (h + 1), :] = main * weight
                lame_ref[p, 1, ij, 2 * ey * h : 2 * ey * (h + 1), :] = gather(points[4][h], last_at) * weight_last
    levels = both(starts[3] - starts[1])
    for h in range(2):
        level_ref[0, 2 * ey * h : 2 * ey * (h + 1), :] = gather(levels[h], main_at)
        level_ref[1, 2 * ey * h : 2 * ey * (h + 1), :] = gather(levels[h], last_at)


def five(values):
    return list(values) + [rolled(values[0], -1)]


def grad_z(points, grad_ref, out):
    count, tall, lanes = points.shape
    high, low = halves(points[...].reshape(count * tall, lanes))
    lhs = jnp.concatenate([high, low, high], axis=1)
    out[...] = jnp.dot(lhs, grad_ref[...], preferred_element_type=F32).reshape(count, tall, 2 * lanes)


def div_z(main, point, div_ref):
    lanes = main.shape[-1]
    (main_high, main_low), (point_high, point_low) = halves(main), halves(point)
    high = jnp.dot(jnp.concatenate([main_high, point_high], axis=1), div_ref[...], preferred_element_type=F32)
    low = jnp.concatenate([main_low, point_low], axis=1)
    return high[:, :lanes] + (high[:, lanes:] + jnp.dot(low, div_ref[:, :lanes], preferred_element_type=F32))


def inside(lanes):
    return (lax.broadcasted_iota(jnp.int32, (8, lanes), 1) > 0).astype(F32)


def stress_of(first, second, x, y, z):
    trace = first * (x[0] + y[1] + z[2])
    twice = second + second
    return [
        trace + twice * x[0],
        trace + twice * y[1],
        second * (y[0] + x[1]),
        second * (z[0] + x[2]),
        second * (z[1] + y[2]),
        trace + twice * z[2],
    ]


def before(inner, tall, window, keep, lame, level, old, old_window, grad_ref, gz, gy, px, part, scale, us):
    lanes = gy.shape[-1]
    for c in range(3):
        points = [five(inner[c][i]) for i in range(3)]
        for i in range(3):
            for j in range(5):
                us[15 * c + 5 * i + j] = points[i][j]
        for i in range(3):
            y = apply5(D, points[i])
            for j in range(5):
                gy[c, 5 * i + j] = y[j]
        for j in range(5):
            y = apply5_middle(D, [points[i][j] for i in range(3)])
            for i in range(5):
                px[c, 5 * i + j] = y[i]
    grad_z(us, grad_ref, gz)
    mask = inside(lanes)
    for h in range(tall // 8):
        at = slice(8 * h, 8 * h + 8)
        table = slice(window + 8 * h, window + 8 * h + 8)
        stored = slice(old_window + 8 * h, old_window + 8 * h + 8)
        if keep is not None:
            fresh = [keep(level[e, table, :]) for e in range(2)]
        for p in range(15):
            y = [gy[c, p, at, :] for c in range(3)]
            sums = []
            for e in range(2):
                span = slice(e * lanes, (e + 1) * lanes)
                z0, z2 = gz[p, at, span], gz[30 + p, at, span]
                first, second = lame[0, e, 5 + p, table, :], lame[1, e, 5 + p, table, :]
                parts = [first * (y[1] + z2), second * y[0], second * z0]
                scales = [first + (second + second), second]
                if keep is not None:
                    parts = [jnp.where(fresh[e], parts[n], old[(0, 2, 3)[n], e, p, stored, :]) for n in range(3)]
                    scales = [jnp.where(fresh[e], x, 0.0) for x in scales]
                both = parts + scales
                sums.append([x * mask for x in both] if e == 1 else both)
            for n in range(3):
                part[n, p, at, :] = sums[0][n] + sums[1][n]
            for n in range(2):
                scale[n, p, at, :] = sums[0][3 + n] + sums[1][3 + n]


def stresses(tall, windows, keep, ends, px, part, scale, lame, level, old, new, flux_x, gx, flux_z, flux_y, us, gz_ends, last_z, qz, grad_ref, div_ref, total, known=None):
    lanes = px.shape[-1]
    points = [[five(ends[c][side]) for side in range(2)] for c in range(3)]
    for c in range(3):
        for side in range(2):
            for j in range(4):
                if known is None:
                    us[8 * c + 4 * side + j] = points[c][side][j]
                elif side == 1:
                    us[4 * c + j] = points[c][side][j]
    grad_z(us, grad_ref, gz_ends)

    def along_z(c, side, j):
        if known is None:
            return gz_ends.at[8 * c + 4 * side + j]
        return (gz_ends if side else known).at[4 * c + j]

    for n in range(6):
        last_z[n] = rolled(along_z(n // 2, n % 2, 0)[...], -1)
    for c in range(3):
        for j in range(5):
            y = apply5_ends(D, points[c][0][j], points[c][1][j], [px[c, 5 * i + j] for i in range(5)])
            for i in range(5):
                gx[c, 5 * i + j] = y[i]
    mask = inside(lanes)
    for h in range(tall // 8):
        at = slice(8 * h, 8 * h + 8)
        table = slice(windows[0] + 8 * h, windows[0] + 8 * h + 8)
        stored = slice(windows[1] + 8 * h, windows[1] + 8 * h + 8)
        if keep is not None:
            fresh = [keep(level[e, table, :]) for e in range(2)]
        for side in range(2):
            ends_y = [apply5(D, [points[c][side][j][at] for j in range(5)]) for c in range(3)]
            for j in range(5):
                p, q = 20 * side + j, 5 * side + j
                x = [gx[c, p, at, :] for c in range(3)]
                y = [ends_y[c][j] for c in range(3)]
                sums = []
                for e in range(2):
                    span = slice(e * lanes, (e + 1) * lanes)
                    if j < 4:
                        z = [along_z(c, side, j)[at, span] for c in range(3)]
                    else:
                        z = [last_z[2 * c + side, at, span] for c in range(3)]
                    if e == 1:
                        x, y = [g * mask for g in x], [g * mask for g in y]
                    stress = stress_of(lame[0, e, p, table, :], lame[1, e, p, table, :], x, y, z)
                    if keep is not None:
                        stress = [jnp.where(fresh[e], stress[n], old[n, e, q, stored, :]) for n in range(6)]
                    if new is not None:
                        for n in range(6):
                            new[n, e, q, at, :] = stress[n]
                    for n in range(3):
                        flux_z[n, e, q, at, :] = stress[3 + n]
                    sums.append([v * mask for v in stress[:5]] if e == 1 else stress[:5])
                xx, yy, xy, xz, yz = [sums[0][n] + sums[1][n] for n in range(5)]
                for c in range(3):
                    flux_x[c, p, at, :] = (xx, xy, xz)[c]
                    flux_y[c, q, at, :] = (xy, yy, yz)[c]
    parts = []
    for e in range(2):
        rows = []
        for c in range(3):
            for side in range(2):
                first = 5 * side
                rows.append(flux_z[c, e, first] + rolled(flux_z[c, e, first + 4], 1))
                rows.append(flux_z[c, e, first + 1 : first + 4].reshape(3 * tall, lanes))
        parts.append(jnp.concatenate(rows, axis=0))
    qz[...] = div_z(*parts, div_ref).reshape(qz.shape)
    for c in range(3):
        for p in range(5, 20):
            flux_x[c, p] = scale[min(c, 1), p - 5] * gx[c, p] + part[c, p - 5]
    assemble((0, 4), flux_x, flux_y, qz, lambda c, side, j, value: total.__setitem__((c, side, j), value))


def assemble(layers, flux_x, flux_y, qz, put):
    count = qz.shape[1] // len(layers)
    for c in range(3):
        pieces = []
        for j in range(5):
            x = apply5(D.T, [flux_x[c, 5 * i + j] for i in range(5)])
            pieces.append([x[i] for i in layers])
        for n in range(len(layers)):
            y = apply5(D.T, [flux_y[c, 5 * n + j] for j in range(5)])
            z = [pieces[j][n] + (y[j] + qz[c, count * n + j] if j < count else y[j]) for j in range(5)]
            put(c, n, 0, z[0] + rolled(z[4], 1))
            for j in range(1, 4):
                put(c, n, j, z[j])


def first_kernel(u_ends, u_inner, lame, grad_ref, gz, gy, px, part, scale, gz_ends, us, us_ends):
    tall = u_inner.shape[3]
    for c in range(3):
        for j in range(4):
            us_ends[4 * c + j] = u_ends[c, j]
    grad_z(us_ends, grad_ref, gz_ends)
    inner = [[[u_inner[c, i, j] for j in range(4)] for i in range(3)] for c in range(3)]
    before(inner, tall, 0, None, lame, None, None, 0, grad_ref, gz, gy, px, part, scale, us)


def between_kernel(rows, last, keep, windows, stores, keep_next, windows_next, flux_x, gx, gz, gy, u_ref, v_ref, m_ref, old,
                   lame, level, grad_ref, div_ref, *refs):
    refs = list(refs)
    new = None
    if last:
        u_ends, v_ends, m_ends, total, send = refs[:5]
        count = rows.stop - rows.start
        for j in range(4):
            mass = m_ends[0, j, rows, :]
            send[pl.ds(final_rows(count, 4, 0) + j, count, stride=4), :] = mass
            for c in range(3):
                speed = v_ends[c, 0, j, rows, :] - time_step * mass * total[c, 0, j, rows, :]
                send[pl.ds(final_rows(count, 2, c) + j, count, stride=4), :] = u_ends[c, 0, j, rows, :]
                send[pl.ds(final_rows(count, 3, c) + j, count, stride=4), :] = speed
    else:
        u_out, v_out = refs[:2]
        m_out, gz_out, gy_out, px_out, part, scale = refs[2:8]
    if stores:
        new = refs[8]
    flux_y, flux_z, qz = refs[-4:-1] if not last else refs[-3:]
    us = None if last else refs[-1]
    _, _, tall, lanes = gx.shape
    mask = inside(lanes)
    for h in range(tall // 8):
        at = slice(8 * h, 8 * h + 8)
        table = slice(windows[0] + 8 * h, windows[0] + 8 * h + 8)
        stored = slice(windows[1] + 8 * h, windows[1] + 8 * h + 8)
        if keep is not None:
            fresh = [keep(level[e, table, :]) for e in range(2)]
        for p in range(15):
            x = [gx[c, 5 + p, at, :] for c in range(3)]
            y = [gy[c, p, at, :] for c in range(3)]
            sums = []
            for e in range(2):
                z = [gz[15 * c + p, at, e * lanes : (e + 1) * lanes] for c in range(3)]
                if e == 1:
                    x, y = [g * mask for g in x], [g * mask for g in y]
                stress = stress_of(lame[0, e, 5 + p, table, :], lame[1, e, 5 + p, table, :], x, y, z)
                if keep is not None:
                    stress = [jnp.where(fresh[e], stress[n], old[n, e, p, stored, :]) for n in range(6)]
                if stores:
                    for n in range(6):
                        new[n, e, p, at, :] = stress[n]
                else:
                    for n in range(3):
                        flux_z[n, e, p, at, :] = stress[3 + n]
                sums.append([v * mask for v in stress[:5]] if e == 1 else stress[:5])
            for c, n in enumerate((2, 1, 4)):
                flux_y[c, p, at, :] = sums[0][n] + sums[1][n]
    if stores:
        flux_z = new.at[3:6]
    qz[...] = div_z(*(flux_z[:, e].reshape(45 * tall, lanes) for e in range(2)), div_ref).reshape(qz.shape)
    inner = [[[None] * 4 for _ in range(3)] for _ in range(3)]

    def put(c, n, j, force):
        mass = m_ref[n, j, rows, :]
        speed = v_ref[c, n, j, rows, :] - time_step * mass * force[rows]
        position = u_ref[c, n, j, rows, :] + time_step * speed
        if last:
            send[pl.ds(final_rows(count, 0, c, n) + j, count, stride=4), :] = position
            send[pl.ds(final_rows(count, 1, c, n) + j, count, stride=4), :] = speed
            return
        u_out[c, n, j], v_out[c, n, j] = position, speed
        if c == 0:
            m_out[n, j] = mass
        inner[c][n][j] = position

    assemble((1, 2, 3), flux_x, flux_y, qz, put)
    if not last:
        before(inner, rows.stop - rows.start, windows_next[0], keep_next, lame, level, new if stores else old, windows_next[1],
               grad_ref, gz_out, gy_out, px_out, part, scale, us)


def newest(level_of):
    return level_of > LEVELS - 1.5


def newer(level_of):
    return level_of > LEVELS - 2.5


def start_kernel(sizes, known, u_ref, v_ref, m_ref, a_ref, b_ref, px, part, scale, lame, level, grad_ref, div_ref,
                 rim_ref, new, flux_x, gx, total, send_a, send_b, flux_z, flux_y, us, gz_ends, last_z, qz):
    nx, ey, lanes = sizes
    even, _, last = place("px", nx)
    tall = 4 * ey
    rim_ref[...] = jnp.zeros(rim_ref.shape, F32)
    for c in range(3):
        for j in range(4):
            count = 3 * ey - (j > 0)
            at = (pl.ds(c * (12 * ey - 3) + j, count, stride=4), slice(None))
            rim_ref[c, j, 0:count, :] = jnp.where(last, 0.0, jnp.where(even, a_ref[at], b_ref[at]))
    ends = [[[u_ref[c, j] for j in range(4)], [rim_ref[c, j] for j in range(4)]] for c in range(3)]
    stresses(tall, (0, 0), None, ends, px, part, scale, lame, level, None, new, flux_x, gx, flux_z, flux_y, us, gz_ends, last_z, qz,
             grad_ref, div_ref, total, known)
    low, high = 1, 3 * ey - 2
    for c in range(3):

        def back(j, rows):
            return v_ref[c, j, rows, :] - time_step * m_ref[j, rows, :] * total[c, 0, j, rows, :]

        def ahead(j, rows):
            return total[c, 1, j, rows, :]

        write_message(send_a, low, high, c, lambda j, rows: jnp.where(even, ahead(j, rows), back(j, rows)))
        write_message(send_b, low, high, c, lambda j, rows: jnp.where(even, back(j, rows), ahead(j, rows)))
    for send in (send_a, send_b):
        write_message(send, low, high, 3, lambda j, rows: m_ref[j, rows, :])


def second_kernel(sizes, u_ref, rim_ref, v_ref, m_ref, total_ref, a_ref, b_ref, px, part, scale, old, lame, level, grad_ref, div_ref,
                  u_out, v_out, m_out, flux_x, gx, total_out, send_a, send_b, got, total, flux_z, flux_y, us, gz_ends, last_z, qz):
    nx, ey, lanes = sizes
    even, first, last = place("px", nx)
    tall = 4 * ey
    window = slice(ey - 2, 3 * ey - 2)
    got[...] = jnp.zeros(got.shape, F32)
    for c in range(4):
        read_message(got.at[0, c], 1, 3 * ey - 2, c, a_ref, b_ref, even, last)
    for c in range(3):
        read_message(got.at[1, c], 1, 3 * ey - 2, c, b_ref, a_ref, even, first)
    ends = [[[], []] for _ in range(3)]
    for c in range(3):
        for side in range(2):
            for j in range(4):
                if side == 0:
                    mass, speed, position = m_ref[j], v_ref[c, j], u_ref[c, j]
                    force = total_ref[c, 0, j] + got[1, c, j]
                else:
                    mass, speed, position = got[0, 3, j], got[0, c, j], rim_ref[c, j]
                    force = total_ref[c, 1, j]
                speed = speed - time_step * mass * force
                position = position + time_step * speed
                u_out[c, side, j], v_out[c, side, j] = position[window], speed[window]
                if c == 0:
                    m_out[side, j] = mass[window]
                ends[c][side].append(position)
    stresses(tall, (0, 0), newest, ends, px, part, scale, lame, level, old, None, flux_x, gx, flux_z, flux_y, us, gz_ends, last_z, qz,
             grad_ref, div_ref, total)
    for c in range(3):
        for side in range(2):
            for j in range(4):
                total_out[c, side, j] = total[c, side, j, window, :]
    send_faces(even, total_out, 0, 2 * ey - 1, send_a, send_b)


def send_faces(even, total, low, high, send_a, send_b):
    for c in range(3):

        def back(j, rows):
            return total[c, 0, j, rows, :]

        def ahead(j, rows):
            return total[c, 1, j, rows, :]

        write_message(send_a, low, high, c, lambda j, rows: jnp.where(even, ahead(j, rows), back(j, rows)))
        write_message(send_b, low, high, c, lambda j, rows: jnp.where(even, back(j, rows), ahead(j, rows)))


def later_kernel(sizes, final, u_ref, v_ref, m_ref, total_ref, a_ref, b_ref, px, part, scale, old, lame, level, grad_ref, div_ref, *refs):
    nx, ey, lanes = sizes
    if final:
        u_out, v_out, flux_x, gx, total, send_a, send_b, got, flux_z, flux_y, us, gz_ends, last_z, qz = refs
        new, keep, windows, low, high = None, newest, (ey - 2, 0), 1, 2 + ey
    else:
        u_out, v_out, new, flux_x, gx, total, send_a, send_b, got, flux_z, flux_y, us, gz_ends, last_z, qz = refs
        keep, windows, low, high = newer, (ey - 2, ey - 2), 0, 2 * ey - 1
    even, first, last = place("px", nx)
    got[...] = jnp.zeros(got.shape, F32)
    for c in range(3):
        read_message(got.at[1, c], low, high, c, a_ref, b_ref, even, last)
        read_message(got.at[0, c], low, high, c, b_ref, a_ref, even, first)
    ends = [[[], []] for _ in range(3)]
    for c in range(3):
        for side in range(2):
            for j in range(4):
                speed = v_ref[c, side, j] - time_step * m_ref[side, j] * (total_ref[c, side, j] + got[side, c, j])
                position = u_ref[c, side, j] + time_step * speed
                u_out[c, side, j], v_out[c, side, j] = position, speed
                ends[c][side].append(position)
    stresses(2 * ey, windows, keep, ends, px, part, scale, lame, level, old, new, flux_x, gx, flux_z, flux_y, us, gz_ends, last_z, qz,
             grad_ref, div_ref, total)
    if not final:
        send_faces(even, total, 1, 2 + ey, send_a, send_b)
        return
    for c in range(3):
        for j in range(4):
            at = slice((4 * c + j) * ey, (4 * c + j + 1) * ey)
            ahead = total[c, 1, j, 2 : 2 + ey, :]
            send_a[at, :] = ahead
            send_b[at, :] = ahead


def final_rows(ey, field, c, i=0):
    across = 4 * ey
    if field < 2:
        return (9 * field + 3 * c + i) * across
    return (18 + 3 * (field - 2) + c) * across


def pick_kernel(nx, a_ref, b_ref, out):
    even, first, _ = place("px", nx)
    out[...] = jnp.where(first, 0.0, jnp.where(even, b_ref[...], a_ref[...]))


def end_kernel(sizes, mine, core, force_ref, u_out, v_out):
    nx, ey, lanes = sizes
    even, _, _ = place("px", nx)

    def at(start, j=None):
        rows = (slice(start, start + 4 * ey) if j is None else pl.ds(start + j, ey, stride=4), slice(None))
        return jnp.where(even, mine[rows], core[rows])

    for c in range(3):
        for j in range(4):
            rows = (slice((4 * c + j) * ey, (4 * c + j + 1) * ey), slice(None))
            mass = at(final_rows(ey, 4, 0), j)
            speed = at(final_rows(ey, 3, c), j) - time_step * mass * force_ref[rows]
            v_out[c, 0, pl.ds(j, ey, stride=4), :] = speed
            u_out[c, 0, pl.ds(j, ey, stride=4), :] = at(final_rows(ey, 2, c), j) + time_step * speed
        for i in range(3):
            u_out[c, 1 + i] = at(final_rows(ey, 0, c, i))
            v_out[c, 1 + i] = at(final_rows(ey, 1, c, i))


def call(kernel, name, outs, scratch, *args, cost=None):
    shapes = [jax.ShapeDtypeStruct(s, F32) if name == "end" else pltpu.VMEM(s, F32) for s in outs]
    return pl.pallas_call(
        kernel,
        out_shape=shapes,
        scratch_shapes=[pltpu.VMEM(s, F32) for s in scratch],
        compiler_params=pltpu.CompilerParams(vmem_limit_bytes=32 * 1024 * 1024),
        cost_estimate=cost,
        name=name,
    )(*args)


def shards(sizes, displacement, velocity, inverse_mass, lame_first, lame_second, level_map):
    nx, ny = sizes
    _, ex4, ey4, lanes = displacement.shape
    ey = ey4 // 4
    tall, wide, short = 4 * ey, 3 * ey, 2 * ey

    def move(kind, x):
        return lax.ppermute(x, ("px", "py"), pairs_of(kind, nx, ny))

    def along_x(a, b):
        return move("near", a), move("far", b)

    def along_y(x):
        return move("core", x), move("across", x)

    flat = [x.reshape(-1, lanes) for x in (displacement, velocity, inverse_mass)]
    u_e, u_o = along_y(flat[0])
    gradient, divergence = depth_tables(lanes // 4)
    tables = [jnp.asarray(t) for t in (gradient, divergence, weight_table(lanes // 4))]
    sources = flat + [lame_first, lame_second, level_map] + tables
    own_u, own_v, own_m, first, second, level, gradient, divergence, weights = pl.pallas_call(
        functools.partial(load_kernel, len(sources)),
        out_shape=[pltpu.VMEM(x.shape, x.dtype) for x in sources],
        in_specs=[pl.BlockSpec(memory_space=pl.ANY)] * len(sources),
        scratch_shapes=[pltpu.SemaphoreType.DMA((len(sources),))],
        name="load",
    )(*sources)
    long = pl.CostEstimate(flops=20_000_000_000, bytes_accessed=0, transcendentals=0)
    starts = [int(n) for n in np.cumsum([own_v.shape[0], own_m.shape[0], 128, 128])]
    (own,) = call(functools.partial(pack_kernel, starts), "pack", [(starts[3] + 8, lanes)], [], own_v, own_m, first, second, level)
    from_e, from_o = along_y(own)
    (rim,) = call(functools.partial(rim_kernel, ny, ey4), "rim", [(-(-3 * (3 * ey4 - 3) // 8) * 8, lanes)], [], own_u, u_e, u_o, cost=long)
    (rim_1,) = call(copy_kernel, "face", [rim.shape], [], rim, cost=long)
    rim_a, rim_b = along_x(rim_1, rim)
    sizes_y, sizes_x = (ny, ey, lanes), (nx, ey, lanes)

    def shape(*lead, rows=tall):
        return (*lead, rows, lanes)

    def near_shapes(rows):
        points = functools.partial(shape, rows=rows)
        return [(45, rows, 2 * lanes), points(3, 15), points(3, 25), points(3, 15), points(2, 15)]

    def ends_scratch(rows, count=2):
        points = functools.partial(shape, rows=rows)
        return [points(3, 2, 10), points(3, 10), points(12 * count), (12 * count, rows, 2 * lanes), (6, rows, 2 * lanes), points(3, 8)]

    def between_scratch(rows, rows_next):
        points = functools.partial(shape, rows=rows)
        return [points(3, 15), points(3, 2, 15), points(3, 15)] + ([shape(45, rows=rows_next)] if rows_next else [])

    u_ends, u_inner = call(
        functools.partial(spread_u_kernel, sizes_y), "spread_u", [shape(3, 4), shape(3, 3, 4)], [], own_u, u_e, u_o
    )
    lame, level = call(
        functools.partial(tables_kernel, sizes_y, starts), "tables", [shape(2, 2, 25), shape(2)], [(3, 264, lanes)],
        own, from_e, from_o, weights,
    )
    gz, gy, *near, known = call(
        first_kernel, "before0", near_shapes(tall) + [(12, tall, 2 * lanes)], [shape(45), shape(12)],
        u_ends, u_inner, lame, gradient,
    )
    v_ends, v_inner, m_ends, m_inner = call(
        functools.partial(spread_v_kernel, sizes_y, starts[0]), "spread_v",
        [shape(3, 4), shape(3, 3, 4), shape(4), shape(3, 4)], [], own, from_e, from_o,
    )

    tables = (lame, level, gradient, divergence)
    message = (message_rows(1, 3 * ey - 2, 4), lanes)
    rim_u, old_ends, flux_x, gx, total, send_a, send_b = call(
        functools.partial(start_kernel, sizes_x), "stress0",
        [shape(3, 4), shape(6, 2, 10), shape(3, 25), shape(3, 25), shape(3, 2, 4), message, message],
        ends_scratch(tall, 1),
        known, u_ends, v_ends, m_ends, rim_a, rim_b, *near, *tables,
    )
    got_a, got_b = along_x(send_a, send_b)
    every, window, mine = slice(0, tall), slice(ey - 2, 3 * ey - 2), slice(2, 2 + ey)
    *state, old_inner = call(
        functools.partial(between_kernel, every, False, None, (0, 0), True, newest, (0, 0)), "between0",
        [shape(3, 3, 4), shape(3, 3, 4), shape(3, 4)] + near_shapes(tall) + [shape(6, 2, 15)], between_scratch(tall, tall),
        flux_x, gx, gz, gy, u_inner, v_inner, m_inner, level, *tables,
    )
    u_inner, v_inner, m_inner, gz, gy, *near = state

    ends = shape(3, 2, 4, rows=short)
    message = (message_rows(0, 2 * ey - 1, 3), lanes)
    u_ends, v_ends, m_ends, flux_x, gx, total, send_a, send_b = call(
        functools.partial(second_kernel, sizes_x), "stress1",
        [ends, ends, ends[1:], shape(3, 25), shape(3, 25), ends, message, message],
        [shape(2, 4, 4), shape(3, 2, 4)] + ends_scratch(tall),
        u_ends, rim_u, v_ends, m_ends, total, got_a, got_b, *near, old_ends, *tables,
    )
    got_a, got_b = along_x(send_a, send_b)
    inner = shape(3, 3, 4, rows=short)
    u_inner, v_inner, m_inner, gz, gy, *near = call(
        functools.partial(between_kernel, window, False, newest, (0, 0), False, newer, (ey - 2, ey - 2)), "between1",
        [inner, inner, inner[1:]] + near_shapes(short), between_scratch(tall, short),
        flux_x, gx, gz, gy, u_inner, v_inner, m_inner, old_inner, *tables,
    )

    points, got = shape(3, 25, rows=short), shape(2, 3, 4, rows=short)
    message = (message_rows(1, 2 + ey, 3), lanes)
    u_ends, v_ends, old_ends, flux_x, gx, total, send_a, send_b = call(
        functools.partial(later_kernel, sizes_x, False), "stress2",
        [ends, ends, shape(6, 2, 10, rows=short), points, points, ends, message, message], [got] + ends_scratch(short),
        u_ends, v_ends, m_ends, total, got_a, got_b, *near, old_ends, *tables,
    )
    got_a, got_b = along_x(send_a, send_b)
    every = slice(0, short)
    *state, old_inner = call(
        functools.partial(between_kernel, every, False, newer, (ey - 2, ey - 2), True, newest, (ey - 2, 0)), "between2",
        [inner, inner, inner[1:]] + near_shapes(short) + [shape(6, 2, 15, rows=short)], between_scratch(short, short),
        flux_x, gx, gz, gy, u_inner, v_inner, m_inner, old_inner, *tables,
    )
    u_inner, v_inner, m_inner, gz, gy, *near = state

    message = (12 * ey, lanes)
    u_ends, v_ends, flux_x, gx, total, send_a, send_b = call(
        functools.partial(later_kernel, sizes_x, True), "stress3",
        [ends, ends, points, points, ends, message, message], [got] + ends_scratch(short),
        u_ends, v_ends, m_ends, total, got_a, got_b, *near, old_ends, *tables,
    )
    got_a, got_b = move("home", send_a), move("far", send_b)
    (results,) = call(
        functools.partial(between_kernel, mine, True, newest, (ey - 2, 0), False, None, None), "between3",
        [(25 * ey4, lanes)], between_scratch(short, 0),
        flux_x, gx, gz, gy, u_inner, v_inner, m_inner, old_inner, *tables, u_ends, v_ends, m_ends, total,
    )
    (force,) = call(functools.partial(pick_kernel, nx), "pick", [message], [], got_a, got_b, cost=long)
    return tuple(call(
        functools.partial(end_kernel, sizes_x), "end", [displacement.shape, velocity.shape], [],
        results, move("core", results), force,
    ))


def solution(mesh):
    sizes = (mesh.shape["px"], mesh.shape["py"])
    in_specs = (
        P(None, "px", "py", None),
        P(None, "px", "py", None),
        P("px", "py", None),
        P(None, None, None, "px", "py"),
        P(None, None, None, "px", "py"),
        P("px", "py"),
    )
    out_specs = (P(None, "px", "py", None), P(None, "px", "py", None))
    return jax.shard_map(
        functools.partial(shards, sizes), mesh=mesh, in_specs=in_specs, out_specs=out_specs, check_vma=False
    )
```
